32 devices in a mesh: gy: 2 (over x), gz: 16 (over z, y, core).
Axes of the slice: x: 2, y: 2, z: 4, core: 2. Of those that a mesh axis runs over, the one named last changes fastest.
Arguments:
- residual: float32 [128, 2, 8, 1024], P('gz', None, None, 'gy'), may hold values from -130 to 130
- direction_prev: float32 [128, 2, 8, 1024], P('gz', None, None, 'gy'), may hold values from -12 to 12
- phase_labels: int32 [128, 1024], P('gz', 'gy'), may hold values from 0 to 2
- phase_diffusivity: float32 [3], replicated, may hold values from 0.1 to 1
- x_eigen: float32 [8], replicated, may hold values from 0.00390625 to 2
- rz_prev: float32 [1], replicated, may hold values from 4194304 to 62914560
Outputs:
- preconditioned: float32 [128, 2, 8, 1024], P('gz', None, None, 'gy')
- direction: float32 [128, 2, 8, 1024], P('gz', None, None, 'gy')
- rz_total: float32 [1], replicated
The draws below stay inside these ranges and needn't reach their ends.
All inputs are finite; a program needn't handle non-finite values.
Results may differ from the reference program's by a relative error of at most 0.0003.
Values sent between devices are 32-bit elements; how exact they have to be, the bound alone decides.
No kernel may reach another device: no remote copies, remote signals or barrier semaphores. Data moves between devices by JAX's collectives and lax.ppermute only.
A program may use at most 64 MiB of HBM per device.

```python
import math
import jax
import jax.numpy as jnp
from jax import lax

NY = 1024
KW = 8
PHASES = 3
NZ = 128


def draw_residual(key, part):
    noise_base = jnp.clip(jax.random.normal(jax.random.fold_in(key, 1), (NZ, 2, KW, NY), jnp.float32), -4.0, 4.0)
    depth_frac = jnp.arange(NZ, dtype=jnp.float32) / NZ
    growth = 0.3 * jnp.exp(depth_frac * 2.302585)
    drawn = noise_base * growth[:, None, None, None]
    return drawn.astype(jnp.float32)


def touch_ends(values, key, low, top_value):
    longest = values.shape.index(max(values.shape))
    spots = []
    for shift in (0, 1):
        where = [jax.random.randint(jax.random.fold_in(key, axis), (), 0, length) for axis, length in enumerate(values.shape)]
        where[longest] = (where[longest] + shift) % values.shape[longest]
        spots.append(tuple(where))
    return values.at[spots[0]].set(low).at[spots[1]].set(top_value)


def shard_levels(rng, extent, pieces, least, high):
    loudness = 1.0
    for axis_at, blocks in pieces:
        draws = jax.random.uniform(jax.random.fold_in(jax.random.fold_in(rng, 6), axis_at), (blocks,), jnp.float32, least / len(pieces), high / len(pieces))
        loudness = loudness * jnp.repeat(jnp.exp(draws), extent[axis_at] // blocks).reshape((-1,) + (1,) * (len(extent) - 1 - axis_at))
    return loudness


def bell_draw(key, extent, spread, bound, cuts=(), kind=jnp.bfloat16):
    values = spread * jax.random.normal(key, extent, jnp.float32)
    if cuts:
        values = values * shard_levels(key, extent, cuts, -0.22, 0.18)
    return jnp.clip(values, -bound, bound).astype(kind)


def setup_inputs(seed: int = 0) -> dict:
    seeds = jax.random.split(jax.random.key(seed), 7)
    residual = draw_residual(jax.random.fold_in(seeds[6], 71), 0)
    direction_prev = bell_draw(seeds[1], (NZ, 2, KW, NY), 2.0, 12.0, ((0, 16), (3, 2)), jnp.float32)
    phase_labels = touch_ends(jax.random.randint(seeds[2], (NZ, NY), 0, PHASES), jax.random.fold_in(seeds[2], 1), 0, PHASES - 1).astype(jnp.int32)
    phase_diffusivity = jnp.clip(jnp.exp(jax.random.uniform(seeds[3], (PHASES,), jnp.float32, math.log(0.1), math.log(1.0))), 0.1, 1.0)
    x_eigen = jnp.clip(jnp.exp(jax.random.uniform(seeds[4], (KW,), jnp.float32, math.log(0.00390625), math.log(2.0))), 0.00390625, 2.0)
    rz_prev = jnp.clip(jnp.exp(jax.random.uniform(seeds[5], (1,), jnp.float32, math.log(4194304), math.log(62914560))), 4194304, 62914560)
    return dict(residual=residual, direction_prev=direction_prev, phase_labels=phase_labels, phase_diffusivity=phase_diffusivity, x_eigen=x_eigen, rz_prev=rz_prev)


def reference(residual, direction_prev, phase_labels, phase_diffusivity, x_eigen, rz_prev):
    weight = phase_diffusivity[phase_labels] ** (-0.5)
    scaled = residual * weight[:, None, None, :]
    spectrum = jnp.fft.fft(scaled[:, 0] + 1j * scaled[:, 1], axis=-1)
    wave_ids = jnp.arange(NY).astype(jnp.float32)
    shift_mode = x_eigen[:, None] + 2.0 - 2.0 * jnp.cos(2.0 * jnp.pi * wave_ids / NY)
    stacked = jnp.stack([jnp.real(spectrum), jnp.imag(spectrum)], axis=-1).astype(jnp.float32)
    system_rhs = jnp.transpose(stacked, (1, 2, 0, 3))
    depth_ids = jnp.arange(NZ)
    below_diag = jnp.broadcast_to(jnp.where(depth_ids > 0, -1.0, 0.0).astype(jnp.float32), (KW, NY, NZ))
    above_diag = jnp.broadcast_to(jnp.where(depth_ids < NZ - 1, -1.0, 0.0).astype(jnp.float32), (KW, NY, NZ))
    main_diag = jnp.broadcast_to((2.0 + shift_mode)[:, :, None], (KW, NY, NZ)).astype(jnp.float32)
    solved = lax.linalg.tridiagonal_solve(below_diag, main_diag, above_diag, system_rhs)
    solved_back = jnp.transpose(solved, (2, 0, 1, 3))
    field_y = jnp.fft.ifft(solved_back[..., 0] + 1j * solved_back[..., 1], axis=-1)
    preconditioned = jnp.stack([jnp.real(field_y), jnp.imag(field_y)], axis=1).astype(jnp.float32) * weight[:, None, None, :]
    rz_total = jnp.sum(residual * preconditioned).reshape(1)
    direction = preconditioned + rz_total / rz_prev * direction_prev
    return (preconditioned, direction, rz_total)
```

```python
import functools

import jax
import jax.numpy as jnp
import numpy as np
from jax import lax
from jax.experimental import pallas as pl
from jax.experimental.pallas import tpu as pltpu
from jax.sharding import PartitionSpec as P

LANES = 128
SUBS = 8
HALF = 4
VMEM = pl.BlockSpec(memory_space=pltpu.VMEM)
SMEM = pl.BlockSpec(memory_space=pltpu.SMEM)


def split_bf16(table):
    high = table.astype(jnp.bfloat16)
    low = (table - np.asarray(high, np.float64)).astype(jnp.bfloat16)
    return np.stack([np.asarray(high), np.asarray(low)])


def lane_transform(sign):
    ids = np.arange(LANES)
    angle = 2.0 * np.pi * (ids[:, None] * ids[None, :] % LANES) / LANES
    cosine, sine = np.cos(angle), sign * np.sin(angle)
    return split_bf16(np.block([[cosine, sine], [-sine, cosine]]))


def twiddles(radix):
    angle = 2.0 * np.pi * np.arange(radix)[:, None] * np.arange(LANES)[None, :] / (radix * LANES)
    return np.stack([np.cos(angle), np.sin(angle)]).astype(np.float32)


def y_eigen(radix):
    wave = np.arange(radix)[:, None] + radix * np.arange(LANES)[None, :]
    return (4.0 * np.sin(np.pi * wave / (radix * LANES)) ** 2).astype(np.float32)


def power(base, exponent):
    result = None
    while exponent:
        if exponent & 1:
            result = base if result is None else result * base
        exponent >>= 1
        if exponent:
            base = base * base
    return result


def small_dft(re, im, sign):
    count = len(re)
    if count == 1:
        return re, im
    even_re, even_im = small_dft(re[0::2], im[0::2], sign)
    odd_re, odd_im = small_dft(re[1::2], im[1::2], sign)
    out_re, out_im = [None] * count, [None] * count
    for i in range(count // 2):
        angle = 2.0 * np.pi * i / count
        c, s = float(np.cos(angle)), float(sign * np.sin(angle))
        if i == 0:
            a, b = odd_re[i], odd_im[i]
        elif 4 * i == count:
            a, b = (odd_im[i], -odd_re[i]) if sign < 0 else (-odd_im[i], odd_re[i])
        else:
            a = odd_re[i] * c - odd_im[i] * s
            b = odd_re[i] * s + odd_im[i] * c
        out_re[i], out_im[i] = even_re[i] + a, even_im[i] + b
        out_re[i + count // 2], out_im[i + count // 2] = even_re[i] - a, even_im[i] - b
    return out_re, out_im


def lane_product(re, im, table_ref):
    count, shape = len(re), re[0].shape
    rows = int(np.prod(shape[:-1]))
    flat = jnp.concatenate(
        [jnp.concatenate([a.reshape(rows, LANES), b.reshape(rows, LANES)], axis=1) for a, b in zip(re, im)],
        axis=0,
    )
    high = flat.astype(jnp.bfloat16)
    low = (flat - high.astype(jnp.float32)).astype(jnp.bfloat16)
    dot = functools.partial(jnp.dot, preferred_element_type=jnp.float32)
    out = dot(high, table_ref[0]) + (dot(low, table_ref[0]) + dot(high, table_ref[1]))
    out_re = [out[i * rows : (i + 1) * rows, :LANES].reshape(shape) for i in range(count)]
    out_im = [out[i * rows : (i + 1) * rows, LANES:].reshape(shape) for i in range(count)]
    return out_re, out_im


def sub_ids(shape):
    return lax.broadcasted_iota(jnp.int32, shape, len(shape) - 2)


def turn(value, shift):
    shift = shift % SUBS
    return value if shift == 0 else pltpu.roll(value, shift, value.ndim - 2)


def for_targets(pieces, me):
    peers = len(pieces)
    out = []
    for s in range(peers):
        chosen = pieces[0]
        for t in range(1, peers):
            chosen = jnp.where(lax.rem(me + s, peers) == t, pieces[t], chosen)
        out.append(chosen)
    return out


def by_source(held, me):
    peers = len(held)
    out = []
    for t in range(peers):
        chosen = held[0]
        for s in range(1, peers):
            chosen = jnp.where(lax.rem(me + (peers - t), peers) == s, held[s], chosen)
        out.append(chosen)
    return out


def cell_weight(labels, diffusivity_ref):
    weight = jnp.zeros(labels.shape, jnp.float32)
    for i in range(diffusivity_ref.shape[0]):
        value = lax.rsqrt(jnp.full(labels.shape, diffusivity_ref[i], jnp.float32))
        weight = jnp.where(labels == i, value, weight)
    return weight


def mode_roots(eigen_ref, y_eigen_ref, me, kept, length):
    radix = y_eigen_ref.shape[0]
    subs = sub_ids((SUBS, LANES))
    x_part = jnp.zeros((SUBS, LANES), jnp.float32)
    for i in range(kept):
        x_part = jnp.where(lax.rem(subs, kept) == i, eigen_ref[me * kept + i], x_part)
    half_shift = 0.5 * jnp.stack([x_part + y_eigen_ref[a : a + 1, :] for a in range(radix)])
    root = jnp.sqrt(half_shift * (half_shift + 2.0))
    return 1.0 / (1.0 + half_shift + root), (0.5 / length) / root


def group_powers(decay, cells, groups, kept):
    group = sub_ids((SUBS, LANES)) // kept
    ahead = jnp.ones_like(decay)
    behind = jnp.ones_like(decay)
    bit = 1
    while bit < groups:
        factor = power(decay, cells * bit)
        ahead = ahead * jnp.where((group & bit) != 0, factor, 1.0)
        behind = behind * jnp.where((group & bit) != 0, 1.0, factor)
        bit *= 2
    return ahead, behind


def pack_kernel(groups, residual_ref, labels_ref, diffusivity_ref, *out_refs):
    cells, _, waves, planes = residual_ref.shape
    kept, inner = waves // groups, cells // groups
    me = lax.axis_index("gy")
    group = sub_ids((SUBS, LANES)) // kept
    weight = cell_weight(labels_ref[...], diffusivity_ref)
    for part in range(2):
        for a in range(planes // LANES):
            lanes = slice(a * LANES, (a + 1) * LANES)
            rows = [residual_ref[z, part, :, lanes] * weight[z : z + 1, lanes] for z in range(cells)]
            for zp in range(inner):
                pieces = []
                for t in range(groups):
                    piece = turn(rows[zp], -t * kept)
                    for zg in range(1, groups):
                        piece = jnp.where(group == zg, turn(rows[zg * inner + zp], (zg - t) * kept), piece)
                    pieces.append(piece)
                for ref, value in zip(out_refs, for_targets(pieces, me)):
                    ref[part, a, zp] = value


def forward_kernel(groups, *refs):
    held = refs[:groups]
    lane_ref, twiddle_ref, y_eigen_ref, eigen_ref = refs[groups : groups + 4]
    message_ref, local_ref, decay_ref, scale_ref = refs[groups + 4 :]
    _, block_rows, inner, _, _ = held[0].shape
    radix = block_rows * groups
    length = radix * LANES
    kept = SUBS // groups
    me = lax.axis_index("gy")
    re, im = [], []
    blocks = [by_source([ref[part] for ref in held], me) for part in range(2)]
    for t in range(groups):
        for a in range(block_rows):
            re.append(blocks[0][t][a])
            im.append(blocks[1][t][a])
    re, im = small_dft(re, im, -1.0)
    turned_re, turned_im = [], []
    for a in range(radix):
        c, s = twiddle_ref[0, a : a + 1, :], twiddle_ref[1, a : a + 1, :]
        turned_re.append(re[a] * c + im[a] * s)
        turned_im.append(im[a] * c - re[a] * s)
    re, im = lane_product(turned_re, turned_im, lane_ref)
    decay, scale = mode_roots(eigen_ref, y_eigen_ref, me, kept, length)
    decay_ref[...] = decay
    scale_ref[...] = scale
    group = sub_ids((SUBS, LANES)) // kept
    subs = sub_ids((SUBS, LANES))
    energy = jnp.zeros((SUBS, LANES), jnp.float32)
    for part, field in enumerate((re, im)):
        for a in range(radix):
            d, g = decay[a], scale[a]
            cell = [field[a][i] for i in range(inner)]
            ahead, behind = [cell[0]], [cell[-1]]
            for i in range(1, inner):
                ahead.append(cell[i] + d * ahead[-1])
                behind.append(cell[inner - 1 - i] + d * behind[-1])
            behind = behind[::-1]
            value = [ahead[i] + behind[i] - cell[i] for i in range(inner)]
            total = sum(cell[i] * value[i] for i in range(inner))
            last, first = ahead[-1], behind[0]
            from_low = jnp.zeros_like(last)
            from_high = jnp.zeros_like(first)
            low_weight, high_weight = jnp.ones_like(last), jnp.ones_like(first)
            bit = 1
            while bit < groups:
                upper = (group & bit) != 0
                step = bit * kept
                if 2 * step == SUBS:
                    other_last, other_first = turn(last, step), turn(first, step)
                else:
                    other_last = jnp.where(upper, turn(last, step), turn(last, -step))
                    other_first = jnp.where(upper, turn(first, step), turn(first, -step))
                span = power(d, inner * bit)
                joined = 2.0 * d * other_last * first
                total = total + jnp.where(upper & ((group & (bit - 1)) == 0), joined, 0.0)
                from_low = from_low + jnp.where(upper, low_weight * other_last, 0.0)
                from_high = from_high + jnp.where(upper, 0.0, high_weight * other_first)
                low_weight = low_weight * jnp.where(upper, span, 1.0)
                high_weight = high_weight * jnp.where(upper, 1.0, span)
                last = jnp.where(upper, last + span * other_last, other_last + span * last)
                first = jnp.where(upper, other_first + span * first, first + span * other_first)
                bit *= 2
            energy = energy + g * total
            message_ref[part * radix + a] = jnp.where(subs < HALF, last, first)
            for i in range(inner):
                spread = power(d, i + 1) * from_low + power(d, inner - i) * from_high
                local_ref[part, a, i] = value[i] + spread
    message_ref[2 * radix] = energy


def join(level, cells, groups, own, other, decay, scale, slab):
    radix = decay.shape[0]
    kept = SUBS // groups
    subs = sub_ids((SUBS, LANES))
    right = lax.rem(lax.shift_right_logical(slab, level), 2)
    mine = jnp.where(subs < HALF, 1, 0) != right
    energy = own[2 * radix] + other[2 * radix]
    joined, couple = [], jnp.zeros((SUBS, LANES), jnp.float32)
    for i in range(2 * radix):
        d, g = decay[i % radix], scale[i % radix]
        span = power(d, cells << level)
        mate = other[i]
        joined.append(jnp.where(mine, mate + span * own[i], own[i] + span * mate))
        couple = couple + (2.0 * g * d) * jnp.where(mine, own[i] * turn(mate, HALF), 0.0)
    couple = couple + turn(couple, HALF)
    energy = energy + jnp.where(subs < kept, couple, 0.0)
    return joined, energy


def join_kernel(level, cells, groups, own_ref, other_ref, decay_ref, scale_ref, out_ref):
    joined, energy = join(
        level, cells, groups, own_ref, other_ref, decay_ref[...], scale_ref[...], lax.axis_index("gz")
    )
    for i, value in enumerate(joined):
        out_ref[i] = value
    out_ref[len(joined)] = energy


def backward_kernel(groups, slabs, *refs):
    levels = slabs.bit_length() - 1
    own_ref, received = refs[0], refs[1 : 1 + levels]
    local_ref, decay_ref, scale_ref, lane_ref, twiddle_ref = refs[1 + levels : 6 + levels]
    out_refs, energy_refs = refs[6 + levels : 6 + levels + groups], refs[6 + levels + groups :]
    _, radix, inner, _, _ = local_ref.shape
    kept, cells = SUBS // groups, inner * groups
    me, slab = lax.axis_index("gy"), lax.axis_index("gz")
    decay, scale = decay_ref[...], scale_ref[...]
    subs = sub_ids((SUBS, LANES))
    totals, energy = join(levels - 1, cells, groups, own_ref, received[-1], decay, scale, slab)
    low = subs < HALF
    fields, walls = ([], []), jnp.zeros((SUBS, LANES), jnp.float32)
    ahead, behind = group_powers(decay, inner, groups, kept)
    for part in range(2):
        for a in range(radix):
            i, d = part * radix + a, decay[a]
            span, weight = power(d, cells), jnp.ones_like(d)
            incoming = jnp.zeros_like(d)
            for level in range(levels):
                right = lax.rem(lax.shift_right_logical(slab, level), 2)
                mine = jnp.where(low, 1, 0) != right
                incoming = incoming + jnp.where(mine, 0.0, weight * received[level][i])
                weight = weight * jnp.where(mine, 1.0, span)
                span = span * span
            far = span * d
            turned = turn(totals[i], HALF)
            image = d * (turned - far * totals[i]) / (1.0 - far * far)
            walls = walls + (scale[a] * d) * (turned * image)
            incoming = incoming - weight * image
            turned = turn(incoming, HALF)
            from_low = ahead[a] * jnp.where(low, incoming, turned)
            from_high = behind[a] * jnp.where(low, turned, incoming)
            fields[part].append(
                jnp.stack(
                    [
                        scale[a] * (local_ref[part, a, z] + power(d, z + 1) * from_low + power(d, inner - z) * from_high)
                        for z in range(inner)
                    ]
                )
            )
    energy = energy - jnp.where(lax.rem(subs, HALF) < kept, walls, 0.0)
    re, im = lane_product(fields[0], fields[1], lane_ref)
    turned_re, turned_im = [], []
    for a in range(radix):
        c, s = twiddle_ref[0, a : a + 1, :], twiddle_ref[1, a : a + 1, :]
        turned_re.append(re[a] * c - im[a] * s)
        turned_im.append(im[a] * c + re[a] * s)
    re, im = small_dft(turned_re, turned_im, 1.0)
    rows = radix // groups
    for part, field in enumerate((re, im)):
        for a in range(rows):
            pieces = [field[t * rows + a] for t in range(groups)]
            for ref, value in zip(out_refs, for_targets(pieces, me)):
                ref[part * rows + a] = value
    for ref in out_refs:
        ref[2 * rows] = jnp.stack([energy] * inner)


def unpack_kernel(groups, *refs):
    held = refs[:groups]
    labels_ref, diffusivity_ref, previous_ref, rz_prev_ref = refs[groups : groups + 4]
    out_ref, direction_ref, total_ref = refs[groups + 4 :]
    cells, _, waves, planes = out_ref.shape
    kept, inner, rows = waves // groups, cells // groups, planes // LANES
    me = lax.axis_index("gy")
    block = sub_ids((SUBS, LANES)) // kept
    weight = cell_weight(labels_ref[...], diffusivity_ref)
    energies = by_source([ref[2 * rows, 0] for ref in held], me)
    total = jnp.sum(sum(energies[1:], energies[0]), axis=(0, 1), keepdims=True)
    total_ref[...] = total
    ratio = total / rz_prev_ref[0]
    for part in range(2):
        for a in range(rows):
            lanes = slice(a * LANES, (a + 1) * LANES)
            for zp in range(inner):
                sources = by_source([ref[part * rows + a, zp] for ref in held], me)
                for zg in range(groups):
                    z = zg * inner + zp
                    value = turn(sources[0], -zg * kept)
                    for t in range(1, groups):
                        value = jnp.where(block == t, turn(sources[t], (t - zg) * kept), value)
                    value = value * weight[z : z + 1, lanes]
                    out_ref[z, part, :, lanes] = value
                    direction_ref[z, part, :, lanes] = value + ratio * previous_ref[z, part, :, lanes]


def float_array(*shape):
    return jax.ShapeDtypeStruct(shape, jnp.float32)


def on_device(residual, direction_prev, phase_labels, phase_diffusivity, x_eigen, rz_prev):
    cells, parts, waves, planes = residual.shape
    groups, slabs = lax.axis_size("gy"), lax.axis_size("gz")
    levels = slabs.bit_length() - 1
    inner, rows = cells // groups, planes // LANES
    radix = rows * groups
    distances = [[(i, (i + s) % groups) for i in range(groups)] for s in range(1, groups)]

    pieces = pl.pallas_call(
        functools.partial(pack_kernel, groups),
        out_shape=[float_array(parts, rows, inner, SUBS, LANES)] * groups,
        in_specs=[VMEM, VMEM, SMEM],
        out_specs=[VMEM] * groups,
        name="pack",
    )(residual, phase_labels, phase_diffusivity)
    held = [pieces[0]] + [lax.ppermute(x, "gy", d) for x, d in zip(pieces[1:], distances)]

    message, local, decay, scale = pl.pallas_call(
        functools.partial(forward_kernel, groups),
        out_shape=[
            float_array(parts * radix + 1, SUBS, LANES),
            float_array(parts, radix, inner, SUBS, LANES),
            float_array(radix, SUBS, LANES),
            float_array(radix, SUBS, LANES),
        ],
        in_specs=[VMEM] * (groups + 3) + [SMEM],
        out_specs=[VMEM] * 4,
        name="forward",
    )(*held, lane_transform(-1.0), twiddles(radix), y_eigen(radix), x_eigen)

    received = []
    for level in range(levels):
        swap = [(i, i ^ (1 << level)) for i in range(slabs)]
        received.append(lax.ppermute(message, "gz", swap))
        if level < levels - 1:
            message = pl.pallas_call(
                functools.partial(join_kernel, level, cells, groups),
                out_shape=float_array(*message.shape),
                in_specs=[VMEM] * 4,
                out_specs=VMEM,
                name=f"join{level}",
            )(message, received[-1], decay, scale)

    pieces = pl.pallas_call(
        functools.partial(backward_kernel, groups, slabs),
        out_shape=[float_array(parts * rows + 1, inner, SUBS, LANES)] * groups,
        in_specs=[VMEM] * (6 + levels),
        out_specs=[VMEM] * groups,
        name="backward",
    )(message, *received, local, decay, scale, lane_transform(1.0), twiddles(radix))
    held = [pieces[0]] + [lax.ppermute(x, "gy", d) for x, d in zip(pieces[1:], distances)]

    preconditioned, direction, total = pl.pallas_call(
        functools.partial(unpack_kernel, groups),
        out_shape=[float_array(*residual.shape), float_array(*residual.shape), float_array(1, 1)],
        in_specs=[VMEM] * (groups + 1) + [SMEM, VMEM, SMEM],
        out_specs=[VMEM] * 3,
        name="unpack",
    )(*held, phase_labels, phase_diffusivity, direction_prev, rz_prev)
    return preconditioned, direction, jnp.reshape(total, (1,))


def solution(mesh):
    placed = (P("gz", None, None, "gy"), P("gz", None, None, "gy"), P("gz", "gy"), P(), P(), P())
    return jax.shard_map(
        on_device,
        mesh=mesh,
        in_specs=placed,
        out_specs=(P("gz", None, None, "gy"), P("gz", None, None, "gy"), P()),
        check_vma=False,
    )
```

```python
import functools

import jax
import jax.numpy as jnp
import numpy as np
from jax import lax
from jax.experimental import pallas as pl
from jax.experimental.pallas import tpu as pltpu
from jax.sharding import PartitionSpec as P

LANES = 128
SUBS = 8
HALF = 4
VMEM = pl.BlockSpec(memory_space=pltpu.VMEM)
SMEM = pl.BlockSpec(memory_space=pltpu.SMEM)


def split_bf16(table):
    high = table.astype(jnp.bfloat16)
    low = (table - np.asarray(high, np.float64)).astype(jnp.bfloat16)
    return np.stack([np.asarray(high), np.asarray(low)])


def lane_transform(sign):
    ids = np.arange(LANES)
    angle = 2.0 * np.pi * (ids[:, None] * ids[None, :] % LANES) / LANES
    cosine, sine = np.cos(angle), sign * np.sin(angle)
    return split_bf16(np.block([[cosine, sine], [-sine, cosine]]))


def twiddles(radix):
    angle = 2.0 * np.pi * np.arange(radix)[:, None] * np.arange(LANES)[None, :] / (radix * LANES)
    return np.stack([np.cos(angle), np.sin(angle)]).astype(np.float32)


def y_eigen(radix):
    wave = np.arange(radix)[:, None] + radix * np.arange(LANES)[None, :]
    return (4.0 * np.sin(np.pi * wave / (radix * LANES)) ** 2).astype(np.float32)


def power(base, exponent):
    result = None
    while exponent:
        if exponent & 1:
            result = base if result is None else result * base
        exponent >>= 1
        if exponent:
            base = base * base
    return result


def small_dft(re, im, sign):
    count = len(re)
    if count == 1:
        return re, im
    even_re, even_im = small_dft(re[0::2], im[0::2], sign)
    odd_re, odd_im = small_dft(re[1::2], im[1::2], sign)
    out_re, out_im = [None] * count, [None] * count
    for i in range(count // 2):
        angle = 2.0 * np.pi * i / count
        c, s = float(np.cos(angle)), float(sign * np.sin(angle))
        if i == 0:
            a, b = odd_re[i], odd_im[i]
        elif 4 * i == count:
            a, b = (odd_im[i], -odd_re[i]) if sign < 0 else (-odd_im[i], odd_re[i])
        else:
            a = odd_re[i] * c - odd_im[i] * s
            b = odd_re[i] * s + odd_im[i] * c
        out_re[i], out_im[i] = even_re[i] + a, even_im[i] + b
        out_re[i + count // 2], out_im[i + count // 2] = even_re[i] - a, even_im[i] - b
    return out_re, out_im


def lane_product(re, im, table_ref):
    count, shape = len(re), re[0].shape
    rows = int(np.prod(shape[:-1]))
    flat = jnp.concatenate(
        [jnp.concatenate([a.reshape(rows, LANES), b.reshape(rows, LANES)], axis=1) for a, b in zip(re, im)],
        axis=0,
    )
    high = flat.astype(jnp.bfloat16)
    low = (flat - high.astype(jnp.float32)).astype(jnp.bfloat16)
    dot = functools.partial(jnp.dot, preferred_element_type=jnp.float32)
    out = dot(high, table_ref[0]) + (dot(low, table_ref[0]) + dot(high, table_ref[1]))
    out_re = [out[i * rows : (i + 1) * rows, :LANES].reshape(shape) for i in range(count)]
    out_im = [out[i * rows : (i + 1) * rows, LANES:].reshape(shape) for i in range(count)]
    return out_re, out_im


def sub_ids(shape):
    return lax.broadcasted_iota(jnp.int32, shape, len(shape) - 2)


def turn(value, shift):
    shift = shift % SUBS
    return value if shift == 0 else pltpu.roll(value, shift, value.ndim - 2)


def for_targets(pieces, me):
    peers = len(pieces)
    out = []
    for s in range(peers):
        chosen = pieces[0]
        for t in range(1, peers):
            chosen = jnp.where(lax.rem(me + s, peers) == t, pieces[t], chosen)
        out.append(chosen)
    return out


def by_source(held, me):
    peers = len(held)
    out = []
    for t in range(peers):
        chosen = held[0]
        for s in range(1, peers):
            chosen = jnp.where(lax.rem(me + (peers - t), peers) == s, held[s], chosen)
        out.append(chosen)
    return out


def cell_weight(labels, diffusivity_ref):
    weight = jnp.zeros(labels.shape, jnp.float32)
    for i in range(diffusivity_ref.shape[0]):
        value = lax.rsqrt(jnp.full(labels.shape, diffusivity_ref[i], jnp.float32))
        weight = jnp.where(labels == i, value, weight)
    return weight


def mode_roots(eigen_ref, y_eigen_ref, me, kept, length):
    radix = y_eigen_ref.shape[0]
    subs = sub_ids((SUBS, LANES))
    x_part = jnp.zeros((SUBS, LANES), jnp.float32)
    for i in range(kept):
        x_part = jnp.where(lax.rem(subs, kept) == i, eigen_ref[me * kept + i], x_part)
    half_shift = 0.5 * jnp.stack([x_part + y_eigen_ref[a : a + 1, :] for a in range(radix)])
    root = jnp.sqrt(half_shift * (half_shift + 2.0))
    return 1.0 / (1.0 + half_shift + root), (0.5 / length) / root


def group_powers(decay, cells, groups, kept):
    group = sub_ids((SUBS, LANES)) // kept
    ahead = jnp.ones_like(decay)
    behind = jnp.ones_like(decay)
    bit = 1
    while bit < groups:
        factor = power(decay, cells * bit)
        ahead = ahead * jnp.where((group & bit) != 0, factor, 1.0)
        behind = behind * jnp.where((group & bit) != 0, 1.0, factor)
        bit *= 2
    return ahead, behind


def pack_kernel(groups, residual_ref, labels_ref, diffusivity_ref, *out_refs):
    cells, _, waves, planes = residual_ref.shape
    kept, inner = waves // groups, cells // groups
    me = lax.axis_index("gy")
    group = sub_ids((SUBS, LANES)) // kept
    weight = cell_weight(labels_ref[...], diffusivity_ref)
    for part in range(2):
        for a in range(planes // LANES):
            lanes = slice(a * LANES, (a + 1) * LANES)
            rows = [residual_ref[z, part, :, lanes] * weight[z : z + 1, lanes] for z in range(cells)]
            for zp in range(inner):
                pieces = []
                for t in range(groups):
                    piece = turn(rows[zp], -t * kept)
                    for zg in range(1, groups):
                        piece = jnp.where(group == zg, turn(rows[zg * inner + zp], (zg - t) * kept), piece)
                    pieces.append(piece)
                for ref, value in zip(out_refs, for_targets(pieces, me)):
                    ref[part, a, zp] = value


def forward_kernel(groups, *refs):
    held = refs[:groups]
    lane_ref, twiddle_ref, y_eigen_ref, eigen_ref = refs[groups : groups + 4]
    message_ref, local_ref, decay_ref, scale_ref = refs[groups + 4 :]
    _, block_rows, inner, _, _ = held[0].shape
    radix = block_rows * groups
    length = radix * LANES
    kept = SUBS // groups
    me = lax.axis_index("gy")
    re, im = [], []
    blocks = [by_source([ref[part] for ref in held], me) for part in range(2)]
    for t in range(groups):
        for a in range(block_rows):
            re.append(blocks[0][t][a])
            im.append(blocks[1][t][a])
    re, im = small_dft(re, im, -1.0)
    turned_re, turned_im = [], []
    for a in range(radix):
        c, s = twiddle_ref[0, a : a + 1, :], twiddle_ref[1, a : a + 1, :]
        turned_re.append(re[a] * c + im[a] * s)
        turned_im.append(im[a] * c - re[a] * s)
    re, im = lane_product(turned_re, turned_im, lane_ref)
    decay, scale = mode_roots(eigen_ref, y_eigen_ref, me, kept, length)
    decay_ref[...] = decay
    scale_ref[...] = scale
    group = sub_ids((SUBS, LANES)) // kept
    subs = sub_ids((SUBS, LANES))
    energy = jnp.zeros((SUBS, LANES), jnp.float32)
    for part, field in enumerate((re, im)):
        for a in range(radix):
            d, g = decay[a], scale[a]
            cell = [field[a][i] for i in range(inner)]
            ahead, behind = [cell[0]], [cell[-1]]
            for i in range(1, inner):
                ahead.append(cell[i] + d * ahead[-1])
                behind.append(cell[inner - 1 - i] + d * behind[-1])
            behind = behind[::-1]
            value = [ahead[i] + behind[i] - cell[i] for i in range(inner)]
            total = sum(cell[i] * value[i] for i in range(inner))
            last, first = ahead[-1], behind[0]
            from_low = jnp.zeros_like(last)
            from_high = jnp.zeros_like(first)
            low_weight, high_weight = jnp.ones_like(last), jnp.ones_like(first)
            bit = 1
            while bit < groups:
                upper = (group & bit) != 0
                step = bit * kept
                if 2 * step == SUBS:
                    other_last, other_first = turn(last, step), turn(first, step)
                else:
                    other_last = jnp.where(upper, turn(last, step), turn(last, -step))
                    other_first = jnp.where(upper, turn(first, step), turn(first, -step))
                span = power(d, inner * bit)
                joined = 2.0 * d * other_last * first
                total = total + jnp.where(upper & ((group & (bit - 1)) == 0), joined, 0.0)
                from_low = from_low + jnp.where(upper, low_weight * other_last, 0.0)
                from_high = from_high + jnp.where(upper, 0.0, high_weight * other_first)
                low_weight = low_weight * jnp.where(upper, span, 1.0)
                high_weight = high_weight * jnp.where(upper, 1.0, span)
                last = jnp.where(upper, last + span * other_last, other_last + span * last)
                first = jnp.where(upper, other_first + span * first, first + span * other_first)
                bit *= 2
            energy = energy + g * total
            message_ref[part * radix + a] = jnp.where(subs < HALF, last, first)
            for i in range(inner):
                spread = power(d, i + 1) * from_low + power(d, inner - i) * from_high
                local_ref[part, a, i] = value[i] + spread
    message_ref[2 * radix] = energy


def join(level, cells, groups, own, other, decay, scale, slab):
    radix = decay.shape[0]
    kept = SUBS // groups
    subs = sub_ids((SUBS, LANES))
    right = lax.rem(lax.shift_right_logical(slab, level), 2)
    mine = jnp.where(subs < HALF, 1, 0) != right
    energy = own[2 * radix] + other[2 * radix]
    joined, couple = [], jnp.zeros((SUBS, LANES), jnp.float32)
    for i in range(2 * radix):
        d, g = decay[i % radix], scale[i % radix]
        span = power(d, cells << level)
        mate = other[i]
        joined.append(jnp.where(mine, mate + span * own[i], own[i] + span * mate))
        couple = couple + (2.0 * g * d) * jnp.where(mine, own[i] * turn(mate, HALF), 0.0)
    couple = couple + turn(couple, HALF)
    energy = energy + jnp.where(subs < kept, couple, 0.0)
    return joined, energy


def join_kernel(level, cells, groups, own_ref, other_ref, decay_ref, scale_ref, out_ref):
    joined, energy = join(
        level, cells, groups, own_ref, other_ref, decay_ref[...], scale_ref[...], lax.axis_index("gz")
    )
    for i, value in enumerate(joined):
        out_ref[i] = value
    out_ref[len(joined)] = energy


def backward_kernel(groups, slabs, *refs):
    levels = slabs.bit_length() - 1
    own_ref, received = refs[0], refs[1 : 1 + levels]
    local_ref, decay_ref, scale_ref, lane_ref, twiddle_ref = refs[1 + levels : 6 + levels]
    out_refs, energy_refs = refs[6 + levels : 6 + levels + groups], refs[6 + levels + groups :]
    _, radix, inner, _, _ = local_ref.shape
    kept, cells = SUBS // groups, inner * groups
    me, slab = lax.axis_index("gy"), lax.axis_index("gz")
    decay, scale = decay_ref[...], scale_ref[...]
    subs = sub_ids((SUBS, LANES))
    totals, energy = join(levels - 1, cells, groups, own_ref, received[-1], decay, scale, slab)
    low = subs < HALF
    fields, walls = ([], []), jnp.zeros((SUBS, LANES), jnp.float32)
    ahead, behind = group_powers(decay, inner, groups, kept)
    for part in range(2):
        for a in range(radix):
            i, d = part * radix + a, decay[a]
            span, weight = power(d, cells), jnp.ones_like(d)
            incoming = jnp.zeros_like(d)
            for level in range(levels):
                right = lax.rem(lax.shift_right_logical(slab, level), 2)
                mine = jnp.where(low, 1, 0) != right
                incoming = incoming + jnp.where(mine, 0.0, weight * received[level][i])
                weight = weight * jnp.where(mine, 1.0, span)
                span = span * span
            far = span * d
            turned = turn(totals[i], HALF)
            image = d * (turned - far * totals[i]) / (1.0 - far * far)
            walls = walls + (scale[a] * d) * (turned * image)
            incoming = incoming - weight * image
            turned = turn(incoming, HALF)
            from_low = ahead[a] * jnp.where(low, incoming, turned)
            from_high = behind[a] * jnp.where(low, turned, incoming)
            fields[part].append(
                jnp.stack(
                    [
                        scale[a] * (local_ref[part, a, z] + power(d, z + 1) * from_low + power(d, inner - z) * from_high)
                        for z in range(inner)
                    ]
                )
            )
    energy = energy - jnp.where(lax.rem(subs, HALF) < kept, walls, 0.0)
    re, im = lane_product(fields[0], fields[1], lane_ref)
    turned_re, turned_im = [], []
    for a in range(radix):
        c, s = twiddle_ref[0, a : a + 1, :], twiddle_ref[1, a : a + 1, :]
        turned_re.append(re[a] * c - im[a] * s)
        turned_im.append(im[a] * c + re[a] * s)
    re, im = small_dft(turned_re, turned_im, 1.0)
    rows = radix // groups
    for part, field in enumerate((re, im)):
        for a in range(rows):
            pieces = [field[t * rows + a] for t in range(groups)]
            for ref, value in zip(out_refs, for_targets(pieces, me)):
                ref[part * rows + a] = value
    for ref in out_refs:
        ref[2 * rows] = jnp.stack([energy] * inner)


def unpack_kernel(groups, *refs):
    held = refs[:groups]
    labels_ref, diffusivity_ref, previous_ref, rz_prev_ref = refs[groups : groups + 4]
    out_ref, direction_ref, total_ref = refs[groups + 4 :]
    cells, _, waves, planes = out_ref.shape
    kept, inner, rows = waves // groups, cells // groups, planes // LANES
    me = lax.axis_index("gy")
    block = sub_ids((SUBS, LANES)) // kept
    weight = cell_weight(labels_ref[...], diffusivity_ref)
    energies = by_source([ref[2 * rows, 0] for ref in held], me)
    total = jnp.sum(sum(energies[1:], energies[0]), axis=(0, 1), keepdims=True)
    total_ref[...] = total
    ratio = total / rz_prev_ref[0]
    for part in range(2):
        for a in range(rows):
            lanes = slice(a * LANES, (a + 1) * LANES)
            for zp in range(inner):
                sources = by_source([ref[part * rows + a, zp] for ref in held], me)
                for zg in range(groups):
                    z = zg * inner + zp
                    value = turn(sources[0], -zg * kept)
                    for t in range(1, groups):
                        value = jnp.where(block == t, turn(sources[t], (t - zg) * kept), value)
                    value = value * weight[z : z + 1, lanes]
                    out_ref[z, part, :, lanes] = value
                    direction_ref[z, part, :, lanes] = value + ratio * previous_ref[z, part, :, lanes]


def float_array(*shape):
    return jax.ShapeDtypeStruct(shape, jnp.float32)


def held_array(*shape):
    return pltpu.VMEM(shape, jnp.float32)


def inside(value):
    return pltpu.with_memory_space_constraint(value, pltpu.VMEM)


def on_device(residual, direction_prev, phase_labels, phase_diffusivity, x_eigen, rz_prev):
    cells, parts, waves, planes = residual.shape
    groups, slabs = lax.axis_size("gy"), lax.axis_size("gz")
    levels = slabs.bit_length() - 1
    inner, rows = cells // groups, planes // LANES
    radix = rows * groups
    distances = [[(i, (i + s) % groups) for i in range(groups)] for s in range(1, groups)]

    pieces = pl.pallas_call(
        functools.partial(pack_kernel, groups),
        out_shape=[held_array(parts, rows, inner, SUBS, LANES)] * groups,
        in_specs=[VMEM, VMEM, SMEM],
        out_specs=[VMEM] * groups,
        name="pack",
    )(residual, phase_labels, phase_diffusivity)
    held = [pieces[0]] + [lax.ppermute(x, "gy", d) for x, d in zip(pieces[1:], distances)]

    message, local, decay, scale = pl.pallas_call(
        functools.partial(forward_kernel, groups),
        out_shape=[
            held_array(parts * radix + 1, SUBS, LANES),
            held_array(parts, radix, inner, SUBS, LANES),
            held_array(radix, SUBS, LANES),
            held_array(radix, SUBS, LANES),
        ],
        in_specs=[VMEM] * (groups + 3) + [SMEM],
        out_specs=[VMEM] * 4,
        name="forward",
    )(*map(inside, held), lane_transform(-1.0), twiddles(radix), y_eigen(radix), x_eigen)

    received = []
    for level in range(levels):
        swap = [(i, i ^ (1 << level)) for i in range(slabs)]
        received.append(lax.ppermute(message, "gz", swap))
        if level < levels - 1:
            message = pl.pallas_call(
                functools.partial(join_kernel, level, cells, groups),
                out_shape=held_array(*message.shape),
                in_specs=[VMEM] * 4,
                out_specs=VMEM,
                name=f"join{level}",
            )(*map(inside, (message, received[-1], decay, scale)))

    pieces = pl.pallas_call(
        functools.partial(backward_kernel, groups, slabs),
        out_shape=[held_array(parts * rows + 1, inner, SUBS, LANES)] * groups,
        in_specs=[VMEM] * (6 + levels),
        out_specs=[VMEM] * groups,
        name="backward",
    )(*map(inside, (message, *received, local, decay, scale)), lane_transform(1.0), twiddles(radix))
    held = [pieces[0]] + [lax.ppermute(x, "gy", d) for x, d in zip(pieces[1:], distances)]

    preconditioned, direction, total = pl.pallas_call(
        functools.partial(unpack_kernel, groups),
        out_shape=[float_array(*residual.shape), float_array(*residual.shape), float_array(1, 1)],
        in_specs=[VMEM] * (groups + 1) + [SMEM, VMEM, SMEM],
        out_specs=[VMEM] * 3,
        name="unpack",
    )(*map(inside, held), phase_labels, phase_diffusivity, direction_prev, rz_prev)
    return preconditioned, direction, jnp.reshape(total, (1,))


def solution(mesh):
    placed = (P("gz", None, None, "gy"), P("gz", None, None, "gy"), P("gz", "gy"), P(), P(), P())
    return jax.shard_map(
        on_device,
        mesh=mesh,
        in_specs=placed,
        out_specs=(P("gz", None, None, "gy"), P("gz", None, None, "gy"), P()),
        check_vma=False,
    )
```

```python
import functools

import jax
import jax.numpy as jnp
import numpy as np
from jax import lax
from jax.experimental import pallas as pl
from jax.experimental.pallas import tpu as pltpu
from jax.sharding import PartitionSpec as P

LANES = 128
SUBS = 8
HALF = 4
VMEM = pl.BlockSpec(memory_space=pltpu.VMEM)
SMEM = pl.BlockSpec(memory_space=pltpu.SMEM)
ANY = pl.BlockSpec(memory_space=pl.ANY)


def split_bf16(table):
    high = table.astype(jnp.bfloat16)
    low = (table - np.asarray(high, np.float64)).astype(jnp.bfloat16)
    return np.stack([np.asarray(high), np.asarray(low)])


def lane_transform(sign):
    ids = np.arange(LANES)
    angle = 2.0 * np.pi * (ids[:, None] * ids[None, :] % LANES) / LANES
    cosine, sine = np.cos(angle), sign * np.sin(angle)
    return split_bf16(np.block([[cosine, sine], [-sine, cosine]]))


def twiddles(radix):
    angle = 2.0 * np.pi * np.arange(radix)[:, None] * np.arange(LANES)[None, :] / (radix * LANES)
    return np.stack([np.cos(angle), np.sin(angle)]).astype(np.float32)


def y_eigen(radix):
    wave = np.arange(radix)[:, None] + radix * np.arange(LANES)[None, :]
    return (4.0 * np.sin(np.pi * wave / (radix * LANES)) ** 2).astype(np.float32)


def power(base, exponent):
    result = None
    while exponent:
        if exponent & 1:
            result = base if result is None else result * base
        exponent >>= 1
        if exponent:
            base = base * base
    return result


def small_dft(re, im, sign):
    count = len(re)
    if count == 1:
        return re, im
    even_re, even_im = small_dft(re[0::2], im[0::2], sign)
    odd_re, odd_im = small_dft(re[1::2], im[1::2], sign)
    out_re, out_im = [None] * count, [None] * count
    for i in range(count // 2):
        angle = 2.0 * np.pi * i / count
        c, s = float(np.cos(angle)), float(sign * np.sin(angle))
        if i == 0:
            a, b = odd_re[i], odd_im[i]
        elif 4 * i == count:
            a, b = (odd_im[i], -odd_re[i]) if sign < 0 else (-odd_im[i], odd_re[i])
        else:
            a = odd_re[i] * c - odd_im[i] * s
            b = odd_re[i] * s + odd_im[i] * c
        out_re[i], out_im[i] = even_re[i] + a, even_im[i] + b
        out_re[i + count // 2], out_im[i + count // 2] = even_re[i] - a, even_im[i] - b
    return out_re, out_im


def lane_product(re, im, table_ref):
    count, shape = len(re), re[0].shape
    rows = int(np.prod(shape[:-1]))
    flat = jnp.concatenate(
        [jnp.concatenate([a.reshape(rows, LANES), b.reshape(rows, LANES)], axis=1) for a, b in zip(re, im)],
        axis=0,
    )
    high = flat.astype(jnp.bfloat16)
    low = (flat - high.astype(jnp.float32)).astype(jnp.bfloat16)
    dot = functools.partial(jnp.dot, preferred_element_type=jnp.float32)
    out = dot(high, table_ref[0]) + (dot(low, table_ref[0]) + dot(high, table_ref[1]))
    out_re = [out[i * rows : (i + 1) * rows, :LANES].reshape(shape) for i in range(count)]
    out_im = [out[i * rows : (i + 1) * rows, LANES:].reshape(shape) for i in range(count)]
    return out_re, out_im


def sub_ids(shape):
    return lax.broadcasted_iota(jnp.int32, shape, len(shape) - 2)


def turn(value, shift):
    shift = shift % SUBS
    return value if shift == 0 else pltpu.roll(value, shift, value.ndim - 2)


def for_targets(pieces, me):
    peers = len(pieces)
    out = []
    for s in range(peers):
        chosen = pieces[0]
        for t in range(1, peers):
            chosen = jnp.where(lax.rem(me + s, peers) == t, pieces[t], chosen)
        out.append(chosen)
    return out


def by_source(held, me):
    peers = len(held)
    out = []
    for t in range(peers):
        chosen = held[0]
        for s in range(1, peers):
            chosen = jnp.where(lax.rem(me + (peers - t), peers) == s, held[s], chosen)
        out.append(chosen)
    return out


def cell_weight(labels, diffusivity_ref):
    weight = jnp.zeros(labels.shape, jnp.float32)
    for i in range(diffusivity_ref.shape[0]):
        value = lax.rsqrt(jnp.full(labels.shape, diffusivity_ref[i], jnp.float32))
        weight = jnp.where(labels == i, value, weight)
    return weight


def mode_roots(eigen_ref, y_eigen_ref, me, kept, length):
    radix = y_eigen_ref.shape[0]
    subs = sub_ids((SUBS, LANES))
    x_part = jnp.zeros((SUBS, LANES), jnp.float32)
    for i in range(kept):
        x_part = jnp.where(lax.rem(subs, kept) == i, eigen_ref[me * kept + i], x_part)
    half_shift = 0.5 * jnp.stack([x_part + y_eigen_ref[a : a + 1, :] for a in range(radix)])
    root = jnp.sqrt(half_shift * (half_shift + 2.0))
    return 1.0 / (1.0 + half_shift + root), (0.5 / length) / root


def group_powers(decay, cells, groups, kept):
    group = sub_ids((SUBS, LANES)) // kept
    ahead = jnp.ones_like(decay)
    behind = jnp.ones_like(decay)
    bit = 1
    while bit < groups:
        factor = power(decay, cells * bit)
        ahead = ahead * jnp.where((group & bit) != 0, factor, 1.0)
        behind = behind * jnp.where((group & bit) != 0, 1.0, factor)
        bit *= 2
    return ahead, behind


def pack_kernel(groups, residual_any, labels_any, diffusivity_any, weight_ref, *refs):
    out_refs, (residual_ref, labels_ref, diffusivity_ref, cell_sems, label_sem, value_sem) = refs[:groups], refs[groups:]
    values = pltpu.make_async_copy(diffusivity_any, diffusivity_ref, value_sem)
    labels = pltpu.make_async_copy(labels_any, labels_ref, label_sem)
    values.start()
    labels.start()
    arriving = [
        pltpu.make_async_copy(residual_any.at[z], residual_ref.at[z], cell_sems.at[z]) for z in range(residual_ref.shape[0])
    ]
    order = [zg * (len(arriving) // groups) + zp for zp in range(len(arriving) // groups) for zg in range(groups)]
    for z in order:
        arriving[z].start()
    values.wait()
    labels.wait()
    cells, _, waves, planes = residual_ref.shape
    kept, inner = waves // groups, cells // groups
    me = lax.axis_index("gy")
    group = sub_ids((SUBS, LANES)) // kept
    weight = cell_weight(labels_ref[...], diffusivity_ref)
    weight_ref[...] = weight
    for zp in range(inner):
        for zg in range(groups):
            arriving[zg * inner + zp].wait()
        for part in range(2):
            for a in range(planes // LANES):
                lanes = slice(a * LANES, (a + 1) * LANES)
                rows = [residual_ref[z, part, :, lanes] * weight[z : z + 1, lanes] for z in range(zp, cells, inner)]
                pieces = []
                for t in range(groups):
                    piece = turn(rows[0], -t * kept)
                    for zg in range(1, groups):
                        piece = jnp.where(group == zg, turn(rows[zg], (zg - t) * kept), piece)
                    pieces.append(piece)
                for ref, value in zip(out_refs, for_targets(pieces, me)):
                    ref[part, a, zp] = value


def roots_kernel(groups, y_eigen_ref, eigen_ref, decay_ref, scale_ref):
    length = y_eigen_ref.shape[0] * LANES
    decay, scale = mode_roots(eigen_ref, y_eigen_ref, lax.axis_index("gy"), SUBS // groups, length)
    decay_ref[...] = decay
    scale_ref[...] = scale


def forward_kernel(groups, *refs):
    held = refs[:groups]
    lane_ref, twiddle_ref, decay_ref, scale_ref = refs[groups : groups + 4]
    message_ref, local_ref = refs[groups + 4 :]
    _, block_rows, inner, _, _ = held[0].shape
    radix = block_rows * groups
    kept = SUBS // groups
    me = lax.axis_index("gy")
    re, im = [], []
    blocks = [by_source([ref[part] for ref in held], me) for part in range(2)]
    for t in range(groups):
        for a in range(block_rows):
            re.append(blocks[0][t][a])
            im.append(blocks[1][t][a])
    re, im = small_dft(re, im, -1.0)
    turned_re, turned_im = [], []
    for a in range(radix):
        c, s = twiddle_ref[0, a : a + 1, :], twiddle_ref[1, a : a + 1, :]
        turned_re.append(re[a] * c + im[a] * s)
        turned_im.append(im[a] * c - re[a] * s)
    re, im = lane_product(turned_re, turned_im, lane_ref)
    decay, scale = decay_ref[...], scale_ref[...]
    group = sub_ids((SUBS, LANES)) // kept
    subs = sub_ids((SUBS, LANES))
    energy = jnp.zeros((SUBS, LANES), jnp.float32)
    for part, field in enumerate((re, im)):
        for a in range(radix):
            d, g = decay[a], scale[a]
            cell = [field[a][i] for i in range(inner)]
            ahead, behind = [cell[0]], [cell[-1]]
            for i in range(1, inner):
                ahead.append(cell[i] + d * ahead[-1])
                behind.append(cell[inner - 1 - i] + d * behind[-1])
            behind = behind[::-1]
            value = [ahead[i] + behind[i] - cell[i] for i in range(inner)]
            total = sum(cell[i] * value[i] for i in range(inner))
            last, first = ahead[-1], behind[0]
            from_low = jnp.zeros_like(last)
            from_high = jnp.zeros_like(first)
            low_weight, high_weight = jnp.ones_like(last), jnp.ones_like(first)
            bit = 1
            while bit < groups:
                upper = (group & bit) != 0
                step = bit * kept
                if 2 * step == SUBS:
                    other_last, other_first = turn(last, step), turn(first, step)
                else:
                    other_last = jnp.where(upper, turn(last, step), turn(last, -step))
                    other_first = jnp.where(upper, turn(first, step), turn(first, -step))
                span = power(d, inner * bit)
                joined = 2.0 * d * other_last * first
                total = total + jnp.where(upper & ((group & (bit - 1)) == 0), joined, 0.0)
                from_low = from_low + jnp.where(upper, low_weight * other_last, 0.0)
                from_high = from_high + jnp.where(upper, 0.0, high_weight * other_first)
                low_weight = low_weight * jnp.where(upper, span, 1.0)
                high_weight = high_weight * jnp.where(upper, 1.0, span)
                last = jnp.where(upper, last + span * other_last, other_last + span * last)
                first = jnp.where(upper, other_first + span * first, first + span * other_first)
                bit *= 2
            energy = energy + g * total
            message_ref[part * radix + a] = jnp.where(subs < HALF, last, first)
            for i in range(inner):
                spread = power(d, i + 1) * from_low + power(d, inner - i) * from_high
                local_ref[part, a, i] = value[i] + spread
    message_ref[2 * radix] = energy


def facing(level):
    low = sub_ids((SUBS, LANES)) < HALF
    right = lax.rem(lax.shift_right_logical(lax.axis_index("gz"), level), 2)
    return jnp.where(low, 1, 0) != right, right


def join(level, cells, groups, own, other, decay, scale):
    radix = decay.shape[0]
    kept = SUBS // groups
    outer, _ = facing(level)
    joined, couple = [], jnp.zeros((SUBS, LANES), jnp.float32)
    for i in range(2 * radix):
        d, g = decay[i % radix], scale[i % radix]
        span = power(d, cells << level)
        joined.append(jnp.where(outer, other[i] + span * own[i], own[i] + span * other[i]))
        couple = couple + (2.0 * g * d) * jnp.where(outer, own[i] * turn(other[i], HALF), 0.0)
    couple = couple + turn(couple, HALF)
    joined.append(own[-1] + other[-1] + jnp.where(sub_ids((SUBS, LANES)) < kept, couple, 0.0))
    return joined


def rows_of(ref):
    return [ref[i] for i in range(ref.shape[0])]


def join_kernel(level, cells, groups, own_ref, other_ref, decay_ref, scale_ref, out_ref):
    joined = join(level, cells, groups, rows_of(own_ref), rows_of(other_ref), decay_ref[...], scale_ref[...])
    for i, value in enumerate(joined):
        out_ref[i] = value


def join_two_kernel(
    level, cells, groups, own_ref, one_ref, two_ref, cross_ref, decay_ref, scale_ref, out_ref, near_ref, pair_ref
):
    decay, scale = decay_ref[...], scale_ref[...]
    odd = lax.rem(lax.axis_index("gz"), 2) == 1
    near = [jnp.where(odd, b, a) for a, b in zip(rows_of(one_ref), rows_of(two_ref))]
    far = [jnp.where(odd, a, b) for a, b in zip(rows_of(one_ref), rows_of(two_ref))]
    own = join(level, cells, groups, rows_of(own_ref), near, decay, scale)
    other = join(level, cells, groups, far, rows_of(cross_ref), decay, scale)
    joined = join(level + 1, cells, groups, own, other, decay, scale)
    for i in range(len(joined)):
        out_ref[i] = joined[i]
        near_ref[i] = near[i]
        pair_ref[i] = other[i]


def edge_kernel(level, cells, groups, own_ref, decay_ref, scale_ref, out_ref):
    radix = decay_ref.shape[0]
    kept = SUBS // groups
    subs = sub_ids((SUBS, LANES))
    outer, _ = facing(level)
    walls = jnp.zeros((SUBS, LANES), jnp.float32)
    for a in range(radix):
        d = decay_ref[a]
        image = power(d, (cells << level) + 1)
        both = []
        for part in range(2):
            own = own_ref[part * radix + a]
            near = jnp.where(outer, 0.0, own)
            walls = walls + (scale_ref[a] * d * d) * (near * near)
            sent = own - image * turn(own, HALF)
            both.append(jnp.where(outer, sent, turn(sent, HALF)))
        out_ref[a] = jnp.where(subs < HALF, both[0], both[1])
    out_ref[radix] = own_ref[2 * radix] - jnp.where(lax.rem(subs, HALF) < kept, walls, 0.0)


def backward_kernel(groups, slabs, *refs):
    levels = slabs.bit_length() - 1
    own_ref, received = refs[0], refs[1:levels]
    edge_ref, other_ref, local_ref, decay_ref, scale_ref, lane_ref, twiddle_ref = refs[levels : levels + 7]
    out_refs = refs[levels + 7 :]
    _, radix, inner, _, _ = local_ref.shape
    kept, cells = SUBS // groups, inner * groups
    me = lax.axis_index("gy")
    decay, scale = decay_ref[...], scale_ref[...]
    subs = sub_ids((SUBS, LANES))
    low = subs < HALF
    outers = [facing(level)[0] for level in range(levels)]
    right = facing(levels - 1)[1] == 1
    couple = jnp.zeros((SUBS, LANES), jnp.float32)
    fields = ([], [])
    ahead, behind = group_powers(decay, inner, groups, kept)
    for a in range(radix):
        d = decay[a]
        spans = [power(d, cells)]
        for level in range(1, levels + 1):
            spans.append(spans[-1] * spans[-1])
        far = spans[levels] * d
        image = spans[levels - 1] * d
        rest = 1.0 / (1.0 - far * far)
        edge, other = edge_ref[a], other_ref[a]
        edge_turned, other_turned = turn(edge, HALF), turn(other, HALF)
        for part in range(2):
            i = part * radix + a
            weight, incoming = jnp.ones_like(d), jnp.zeros_like(d)
            for level in range(levels - 1):
                incoming = incoming + jnp.where(outers[level], 0.0, weight * received[level][i])
                weight = weight * jnp.where(outers[level], 1.0, spans[level])
            mine = jnp.where(low, edge, edge_turned) if part == 0 else jnp.where(low, edge_turned, edge)
            theirs = jnp.where(low, other, other_turned) if part == 0 else jnp.where(low, other_turned, other)
            entering = rest * (theirs - far * mine)
            leaving = rest * (mine - far * theirs)
            here, there = mine * entering, theirs * leaving
            couple = couple + (scale[a] * d) * (jnp.where(right, there, here) + jnp.where(right, here, there))
            wall = d * turn(own_ref[i], HALF) + image * entering
            incoming = incoming + weight * jnp.where(outers[levels - 1], -wall, entering)
            turned = turn(incoming, HALF)
            from_low = ahead[a] * jnp.where(low, incoming, turned)
            from_high = behind[a] * jnp.where(low, turned, incoming)
            fields[part].append(
                jnp.stack(
                    [
                        scale[a] * (local_ref[part, a, z] + power(d, z + 1) * from_low + power(d, inner - z) * from_high)
                        for z in range(inner)
                    ]
                )
            )
    energy = edge_ref[radix] + other_ref[radix] + jnp.where(subs < kept, couple, 0.0)
    re, im = lane_product(fields[0], fields[1], lane_ref)
    turned_re, turned_im = [], []
    for a in range(radix):
        c, s = twiddle_ref[0, a : a + 1, :], twiddle_ref[1, a : a + 1, :]
        turned_re.append(re[a] * c - im[a] * s)
        turned_im.append(im[a] * c + re[a] * s)
    re, im = small_dft(turned_re, turned_im, 1.0)
    rows = radix // groups
    for part, field in enumerate((re, im)):
        for a in range(rows):
            pieces = [field[t * rows + a] for t in range(groups)]
            for ref, value in zip(out_refs, for_targets(pieces, me)):
                ref[part * rows + a] = value
    for ref in out_refs:
        ref[2 * rows] = jnp.stack([energy] * inner)


def unpack_kernel(groups, *refs):
    held = refs[:groups]
    weight_ref, previous_ref, rz_prev_ref = refs[groups : groups + 3]
    out_ref, direction_ref, total_ref, out_buffer, direction_buffer, total_buffer, sems, total_sem = refs[groups + 3 :]
    cells, _, waves, planes = out_buffer.shape
    kept, inner, rows = waves // groups, cells // groups, planes // LANES
    me = lax.axis_index("gy")
    block = sub_ids((SUBS, LANES)) // kept
    energies = by_source([ref[2 * rows, 0] for ref in held], me)
    total = jnp.sum(sum(energies[1:], energies[0]), axis=(0, 1), keepdims=True)
    total_buffer[...] = total
    copies = [pltpu.make_async_copy(total_buffer, total_ref, total_sem)]
    copies[0].start()
    ratio = total / rz_prev_ref[0]
    for zp in range(inner):
        for part in range(2):
            for a in range(rows):
                lanes = slice(a * LANES, (a + 1) * LANES)
                sources = by_source([ref[part * rows + a, zp] for ref in held], me)
                for zg in range(groups):
                    z = zg * inner + zp
                    value = turn(sources[0], -zg * kept)
                    for t in range(1, groups):
                        value = jnp.where(block == t, turn(sources[t], (t - zg) * kept), value)
                    value = value * weight_ref[z : z + 1, lanes]
                    out_buffer[z, part, :, lanes] = value
                    direction_buffer[z, part, :, lanes] = value + ratio * previous_ref[z, part, :, lanes]
        for zg in range(groups):
            z = zg * inner + zp
            for i, (source, target) in enumerate(((out_buffer, out_ref), (direction_buffer, direction_ref))):
                copies.append(pltpu.make_async_copy(source.at[z], target.at[z], sems.at[i, z]))
                copies[-1].start()
    for copy in copies:
        copy.wait()


def float_array(*shape):
    return jax.ShapeDtypeStruct(shape, jnp.float32)


def held_array(*shape):
    return pltpu.VMEM(shape, jnp.float32)


def inside(value):
    return pltpu.with_memory_space_constraint(jnp.asarray(value), pltpu.VMEM)


def on_device(residual, direction_prev, phase_labels, phase_diffusivity, x_eigen, rz_prev):
    cells, parts, waves, planes = residual.shape
    groups, slabs = lax.axis_size("gy"), lax.axis_size("gz")
    levels = slabs.bit_length() - 1
    inner, rows = cells // groups, planes // LANES
    radix = rows * groups
    distances = [[(i, (i + s) % groups) for i in range(groups)] for s in range(1, groups)]

    weight, *pieces = pl.pallas_call(
        functools.partial(pack_kernel, groups),
        out_shape=[held_array(cells, planes)] + [held_array(parts, rows, inner, SUBS, LANES)] * groups,
        in_specs=[ANY] * 3,
        out_specs=[VMEM] * (groups + 1),
        scratch_shapes=[
            pltpu.VMEM(residual.shape, jnp.float32),
            pltpu.VMEM(phase_labels.shape, jnp.int32),
            pltpu.SMEM(phase_diffusivity.shape, jnp.float32),
            pltpu.SemaphoreType.DMA((cells,)),
            pltpu.SemaphoreType.DMA,
            pltpu.SemaphoreType.DMA,
        ],
        name="pack",
    )(residual, phase_labels, phase_diffusivity)
    held = [pieces[0]] + [lax.ppermute(x, "gy", d) for x, d in zip(pieces[1:], distances)]
    decay, scale = pl.pallas_call(
        functools.partial(roots_kernel, groups),
        out_shape=[held_array(radix, SUBS, LANES)] * 2,
        in_specs=[VMEM, SMEM],
        out_specs=[VMEM] * 2,
        name="roots",
    )(inside(y_eigen(radix)), x_eigen)

    message, local = pl.pallas_call(
        functools.partial(forward_kernel, groups),
        out_shape=[
            held_array(parts * radix + 1, SUBS, LANES),
            held_array(parts, radix, inner, SUBS, LANES),
        ],
        in_specs=[VMEM] * (groups + 4),
        out_specs=[VMEM] * 2,
        name="forward",
    )(*map(inside, (*held, lane_transform(-1.0), twiddles(radix), decay, scale)))

    def swapped(value, even, odd):
        return lax.ppermute(value, "gz", [(i, i ^ (odd if i & 1 else even)) for i in range(slabs)])

    received, level = [], 0
    while level < levels - 1:
        one_bit, next_bit = 1 << level, 2 << level
        if level == 0 or level == levels - 2:
            received.append(swapped(message, one_bit, one_bit))
            message = pl.pallas_call(
                functools.partial(join_kernel, level, cells, groups),
                out_shape=held_array(*message.shape),
                in_specs=[VMEM] * 4,
                out_specs=VMEM,
                name=f"join{level}",
            )(*map(inside, (message, received[-1], decay, scale)))
            level += 1
        else:
            one = swapped(message, one_bit, next_bit)
            two = swapped(message, next_bit, one_bit)
            cross = swapped(message, one_bit | next_bit, one_bit | next_bit)
            message, near, pair = pl.pallas_call(
                functools.partial(join_two_kernel, level, cells, groups),
                out_shape=[held_array(*message.shape)] * 3,
                in_specs=[VMEM] * 6,
                out_specs=[VMEM] * 3,
                name=f"join{level}",
            )(*map(inside, (message, one, two, cross, decay, scale)))
            received += [near, pair]
            level += 2
    edge = pl.pallas_call(
        functools.partial(edge_kernel, level, cells, groups),
        out_shape=held_array(radix + 1, SUBS, LANES),
        in_specs=[VMEM] * 3,
        out_specs=VMEM,
        name="edge",
    )(*map(inside, (message, decay, scale)))
    other = swapped(edge, 1 << level, 1 << level)

    pieces = pl.pallas_call(
        functools.partial(backward_kernel, groups, slabs),
        out_shape=[held_array(parts * rows + 1, inner, SUBS, LANES)] * groups,
        in_specs=[VMEM] * (levels + 7),
        out_specs=[VMEM] * groups,
        name="backward",
    )(*map(inside, (message, *received, edge, other, local, decay, scale, lane_transform(1.0), twiddles(radix))))
    held = [pieces[0]] + [lax.ppermute(x, "gy", d) for x, d in zip(pieces[1:], distances)]

    preconditioned, direction, total = pl.pallas_call(
        functools.partial(unpack_kernel, groups),
        out_shape=[float_array(*residual.shape), float_array(*residual.shape), float_array(1, 1)],
        in_specs=[VMEM] * (groups + 2) + [SMEM],
        out_specs=[ANY] * 3,
        scratch_shapes=[
            pltpu.VMEM(residual.shape, jnp.float32),
            pltpu.VMEM(residual.shape, jnp.float32),
            pltpu.VMEM((1, 1), jnp.float32),
            pltpu.SemaphoreType.DMA((2, cells)),
            pltpu.SemaphoreType.DMA,
        ],
        name="unpack",
    )(*map(inside, (*held, weight, direction_prev)), rz_prev)
    return preconditioned, direction, jnp.reshape(total, (1,))


def solution(mesh):
    placed = (P("gz", None, None, "gy"), P("gz", None, None, "gy"), P("gz", "gy"), P(), P(), P())
    return jax.shard_map(
        on_device,
        mesh=mesh,
        in_specs=placed,
        out_specs=(P("gz", None, None, "gy"), P("gz", None, None, "gy"), P()),
        check_vma=False,
    )
```

```python
import functools

import jax
import jax.numpy as jnp
import numpy as np
from jax import lax
from jax.experimental import pallas as pl
from jax.experimental.pallas import tpu as pltpu
from jax.sharding import PartitionSpec as P

LANES = 128
SUBS = 8
HALF = 4
VMEM = pl.BlockSpec(memory_space=pltpu.VMEM)
SMEM = pl.BlockSpec(memory_space=pltpu.SMEM)
ANY = pl.BlockSpec(memory_space=pl.ANY)


def split_bf16(table):
    high = table.astype(jnp.bfloat16)
    low = (table - np.asarray(high, np.float64)).astype(jnp.bfloat16)
    return np.stack([np.asarray(high), np.asarray(low)])


def lane_transform(sign):
    ids = np.arange(LANES)
    angle = 2.0 * np.pi * (ids[:, None] * ids[None, :] % LANES) / LANES
    cosine, sine = np.cos(angle), sign * np.sin(angle)
    return split_bf16(np.block([[cosine, sine], [-sine, cosine]]))


def twiddles(radix):
    angle = 2.0 * np.pi * np.arange(radix)[:, None] * np.arange(LANES)[None, :] / (radix * LANES)
    return np.stack([np.cos(angle), np.sin(angle)]).astype(np.float32)


def y_eigen(radix):
    wave = np.arange(radix)[:, None] + radix * np.arange(LANES)[None, :]
    return (4.0 * np.sin(np.pi * wave / (radix * LANES)) ** 2).astype(np.float32)


def power(base, exponent):
    result = None
    while exponent:
        if exponent & 1:
            result = base if result is None else result * base
        exponent >>= 1
        if exponent:
            base = base * base
    return result


def small_dft(re, im, sign):
    count = len(re)
    if count == 1:
        return re, im
    even_re, even_im = small_dft(re[0::2], im[0::2], sign)
    odd_re, odd_im = small_dft(re[1::2], im[1::2], sign)
    out_re, out_im = [None] * count, [None] * count
    for i in range(count // 2):
        angle = 2.0 * np.pi * i / count
        c, s = float(np.cos(angle)), float(sign * np.sin(angle))
        if i == 0:
            a, b = odd_re[i], odd_im[i]
        elif 4 * i == count:
            a, b = (odd_im[i], -odd_re[i]) if sign < 0 else (-odd_im[i], odd_re[i])
        else:
            a = odd_re[i] * c - odd_im[i] * s
            b = odd_re[i] * s + odd_im[i] * c
        out_re[i], out_im[i] = even_re[i] + a, even_im[i] + b
        out_re[i + count // 2], out_im[i + count // 2] = even_re[i] - a, even_im[i] - b
    return out_re, out_im


def lane_product(re, im, table_ref):
    count, shape = len(re), re[0].shape
    rows = int(np.prod(shape[:-1]))
    flat = jnp.concatenate(
        [jnp.concatenate([a.reshape(rows, LANES), b.reshape(rows, LANES)], axis=1) for a, b in zip(re, im)],
        axis=0,
    )
    high = flat.astype(jnp.bfloat16)
    low = (flat - high.astype(jnp.float32)).astype(jnp.bfloat16)
    dot = functools.partial(jnp.dot, preferred_element_type=jnp.float32)
    out = dot(high, table_ref[0]) + (dot(low, table_ref[0]) + dot(high, table_ref[1]))
    out_re = [out[i * rows : (i + 1) * rows, :LANES].reshape(shape) for i in range(count)]
    out_im = [out[i * rows : (i + 1) * rows, LANES:].reshape(shape) for i in range(count)]
    return out_re, out_im


def sub_ids(shape):
    return lax.broadcasted_iota(jnp.int32, shape, len(shape) - 2)


def turn(value, shift):
    shift = shift % SUBS
    return value if shift == 0 else pltpu.roll(value, shift, value.ndim - 2)


def for_targets(pieces, me):
    peers = len(pieces)
    out = []
    for s in range(peers):
        chosen = pieces[0]
        for t in range(1, peers):
            chosen = jnp.where(lax.rem(me + s, peers) == t, pieces[t], chosen)
        out.append(chosen)
    return out


def by_source(held, me):
    peers = len(held)
    out = []
    for t in range(peers):
        chosen = held[0]
        for s in range(1, peers):
            chosen = jnp.where(lax.rem(me + (peers - t), peers) == s, held[s], chosen)
        out.append(chosen)
    return out


def cell_weight(labels, diffusivity_ref):
    weight = jnp.zeros(labels.shape, jnp.float32)
    for i in range(diffusivity_ref.shape[0]):
        value = lax.rsqrt(jnp.full(labels.shape, diffusivity_ref[i], jnp.float32))
        weight = jnp.where(labels == i, value, weight)
    return weight


def mode_roots(eigen_ref, y_eigen_ref, me, kept, length):
    radix = y_eigen_ref.shape[0]
    subs = sub_ids((SUBS, LANES))
    x_part = jnp.zeros((SUBS, LANES), jnp.float32)
    for i in range(kept):
        x_part = jnp.where(lax.rem(subs, kept) == i, eigen_ref[me * kept + i], x_part)
    half_shift = 0.5 * jnp.stack([x_part + y_eigen_ref[a : a + 1, :] for a in range(radix)])
    root = jnp.sqrt(half_shift * (half_shift + 2.0))
    return 1.0 / (1.0 + half_shift + root), (0.5 / length) / root


def group_powers(decay, cells, groups, kept):
    group = sub_ids((SUBS, LANES)) // kept
    ahead = jnp.ones_like(decay)
    behind = jnp.ones_like(decay)
    bit = 1
    while bit < groups:
        factor = power(decay, cells * bit)
        ahead = ahead * jnp.where((group & bit) != 0, factor, 1.0)
        behind = behind * jnp.where((group & bit) != 0, 1.0, factor)
        bit *= 2
    return ahead, behind


def pack_kernel(groups, residual_any, labels_any, diffusivity_any, weight_ref, *refs):
    out_refs, (residual_ref, labels_ref, diffusivity_ref, cell_sems, label_sem, value_sem) = refs[:groups], refs[groups:]
    values = pltpu.make_async_copy(diffusivity_any, diffusivity_ref, value_sem)
    labels = pltpu.make_async_copy(labels_any, labels_ref, label_sem)
    values.start()
    labels.start()
    arriving = [
        pltpu.make_async_copy(residual_any.at[z], residual_ref.at[z], cell_sems.at[z]) for z in range(residual_ref.shape[0])
    ]
    order = [zg * (len(arriving) // groups) + zp for zp in range(len(arriving) // groups) for zg in range(groups)]
    for z in order:
        arriving[z].start()
    values.wait()
    labels.wait()
    cells, _, waves, planes = residual_ref.shape
    kept, inner = waves // groups, cells // groups
    me = lax.axis_index("gy")
    group = sub_ids((SUBS, LANES)) // kept
    weight = cell_weight(labels_ref[...], diffusivity_ref)
    weight_ref[...] = weight
    for zp in range(inner):
        for zg in range(groups):
            arriving[zg * inner + zp].wait()
        for part in range(2):
            for a in range(planes // LANES):
                lanes = slice(a * LANES, (a + 1) * LANES)
                rows = [residual_ref[z, part, :, lanes] * weight[z : z + 1, lanes] for z in range(zp, cells, inner)]
                pieces = []
                for t in range(groups):
                    piece = turn(rows[0], -t * kept)
                    for zg in range(1, groups):
                        piece = jnp.where(group == zg, turn(rows[zg], (zg - t) * kept), piece)
                    pieces.append(piece)
                for ref, value in zip(out_refs, for_targets(pieces, me)):
                    ref[part, a, zp] = value


def roots_kernel(groups, y_eigen_ref, eigen_ref, *out_refs):
    length = y_eigen_ref.shape[0] * LANES
    for s in range(groups):
        device = lax.rem(lax.axis_index("gy") + groups - s, groups)
        decay, scale = mode_roots(eigen_ref, y_eigen_ref, device, SUBS // groups, length)
        out_refs[2 * s][...] = decay
        out_refs[2 * s + 1][...] = scale


def forward_kernel(groups, *refs):
    held = refs[:groups]
    lane_ref, twiddle_ref, decay_ref, scale_ref = refs[groups : groups + 4]
    message_ref, local_ref = refs[groups + 4 :]
    _, block_rows, inner, _, _ = held[0].shape
    radix = block_rows * groups
    kept = SUBS // groups
    me = lax.axis_index("gy")
    re, im = [], []
    blocks = [by_source([ref[part] for ref in held], me) for part in range(2)]
    for t in range(groups):
        for a in range(block_rows):
            re.append(blocks[0][t][a])
            im.append(blocks[1][t][a])
    re, im = small_dft(re, im, -1.0)
    turned_re, turned_im = [], []
    for a in range(radix):
        c, s = twiddle_ref[0, a : a + 1, :], twiddle_ref[1, a : a + 1, :]
        turned_re.append(re[a] * c + im[a] * s)
        turned_im.append(im[a] * c - re[a] * s)
    re, im = lane_product(turned_re, turned_im, lane_ref)
    decay, scale = decay_ref[...], scale_ref[...]
    group = sub_ids((SUBS, LANES)) // kept
    subs = sub_ids((SUBS, LANES))
    energy = jnp.zeros((SUBS, LANES), jnp.float32)
    for part, field in enumerate((re, im)):
        for a in range(radix):
            d, g = decay[a], scale[a]
            cell = [field[a][i] for i in range(inner)]
            ahead, behind = [cell[0]], [cell[-1]]
            for i in range(1, inner):
                ahead.append(cell[i] + d * ahead[-1])
                behind.append(cell[inner - 1 - i] + d * behind[-1])
            behind = behind[::-1]
            value = [ahead[i] + behind[i] - cell[i] for i in range(inner)]
            total = sum(cell[i] * value[i] for i in range(inner))
            last, first = ahead[-1], behind[0]
            from_low = jnp.zeros_like(last)
            from_high = jnp.zeros_like(first)
            low_weight, high_weight = jnp.ones_like(last), jnp.ones_like(first)
            bit = 1
            while bit < groups:
                upper = (group & bit) != 0
                step = bit * kept
                if 2 * step == SUBS:
                    other_last, other_first = turn(last, step), turn(first, step)
                else:
                    other_last = jnp.where(upper, turn(last, step), turn(last, -step))
                    other_first = jnp.where(upper, turn(first, step), turn(first, -step))
                span = power(d, inner * bit)
                joined = 2.0 * d * other_last * first
                total = total + jnp.where(upper & ((group & (bit - 1)) == 0), joined, 0.0)
                from_low = from_low + jnp.where(upper, low_weight * other_last, 0.0)
                from_high = from_high + jnp.where(upper, 0.0, high_weight * other_first)
                low_weight = low_weight * jnp.where(upper, span, 1.0)
                high_weight = high_weight * jnp.where(upper, 1.0, span)
                last = jnp.where(upper, last + span * other_last, other_last + span * last)
                first = jnp.where(upper, other_first + span * first, first + span * other_first)
                bit *= 2
            energy = energy + g * total
            message_ref[part * radix + a] = jnp.where(subs < HALF, last, first)
            for i in range(inner):
                spread = power(d, i + 1) * from_low + power(d, inner - i) * from_high
                local_ref[part, a, i] = value[i] + spread
    message_ref[2 * radix] = energy


def facing(level):
    low = sub_ids((SUBS, LANES)) < HALF
    right = lax.rem(lax.shift_right_logical(lax.axis_index("gz"), level), 2)
    return jnp.where(low, 1, 0) != right, right


def join(level, cells, groups, own, other, decay, scale):
    radix = decay.shape[0]
    kept = SUBS // groups
    outer, _ = facing(level)
    joined, couple = [], jnp.zeros((SUBS, LANES), jnp.float32)
    for i in range(2 * radix):
        d, g = decay[i % radix], scale[i % radix]
        span = power(d, cells << level)
        joined.append(jnp.where(outer, other[i] + span * own[i], own[i] + span * other[i]))
        couple = couple + (2.0 * g * d) * jnp.where(outer, own[i] * turn(other[i], HALF), 0.0)
    couple = couple + turn(couple, HALF)
    joined.append(own[-1] + other[-1] + jnp.where(sub_ids((SUBS, LANES)) < kept, couple, 0.0))
    return joined


def rows_of(ref):
    return [ref[i] for i in range(ref.shape[0])]


def join_kernel(level, cells, groups, own_ref, other_ref, decay_ref, scale_ref, out_ref):
    joined = join(level, cells, groups, rows_of(own_ref), rows_of(other_ref), decay_ref[...], scale_ref[...])
    for i, value in enumerate(joined):
        out_ref[i] = value


def join_two_kernel(
    level, cells, groups, own_ref, one_ref, two_ref, cross_ref, decay_ref, scale_ref, out_ref, near_ref, pair_ref
):
    decay, scale = decay_ref[...], scale_ref[...]
    odd = lax.rem(lax.axis_index("gz"), 2) == 1
    near = [jnp.where(odd, b, a) for a, b in zip(rows_of(one_ref), rows_of(two_ref))]
    far = [jnp.where(odd, a, b) for a, b in zip(rows_of(one_ref), rows_of(two_ref))]
    own = join(level, cells, groups, rows_of(own_ref), near, decay, scale)
    other = join(level, cells, groups, far, rows_of(cross_ref), decay, scale)
    joined = join(level + 1, cells, groups, own, other, decay, scale)
    for i in range(len(joined)):
        out_ref[i] = joined[i]
        near_ref[i] = near[i]
        pair_ref[i] = other[i]


def edge_kernel(level, cells, groups, own_ref, decay_ref, scale_ref, out_ref):
    radix = decay_ref.shape[0]
    kept = SUBS // groups
    subs = sub_ids((SUBS, LANES))
    outer, _ = facing(level)
    walls = jnp.zeros((SUBS, LANES), jnp.float32)
    for a in range(radix):
        d = decay_ref[a]
        image = power(d, (cells << level) + 1)
        both = []
        for part in range(2):
            own = own_ref[part * radix + a]
            near = jnp.where(outer, 0.0, own)
            walls = walls + (scale_ref[a] * d * d) * (near * near)
            sent = own - image * turn(own, HALF)
            both.append(jnp.where(outer, sent, turn(sent, HALF)))
        out_ref[a] = jnp.where(subs < HALF, both[0], both[1])
    out_ref[radix] = own_ref[2 * radix] - jnp.where(lax.rem(subs, HALF) < kept, walls, 0.0)


def to_planes(re, im, lane_ref, twiddle_ref):
    re, im = lane_product(re, im, lane_ref)
    turned_re, turned_im = [], []
    for a in range(len(re)):
        c, s = twiddle_ref[0, a : a + 1, :], twiddle_ref[1, a : a + 1, :]
        turned_re.append(re[a] * c - im[a] * s)
        turned_im.append(im[a] * c + re[a] * s)
    return small_dft(turned_re, turned_im, 1.0)


def local_kernel(groups, local_ref, scale_ref, lane_ref, twiddle_ref, after_ref, *out_refs):
    radix = scale_ref.shape[0]
    rows = radix // groups
    fields = [[scale_ref[a] * local_ref[part, a] for a in range(radix)] for part in range(2)]
    for part, field in enumerate(to_planes(*fields, lane_ref, twiddle_ref)):
        for a in range(rows):
            pieces = [field[t * rows + a] for t in range(groups)]
            for ref, value in zip(out_refs, for_targets(pieces, lax.axis_index("gy"))):
                ref[part * rows + a] = value


def entering_kernel(groups, slabs, cells, *refs):
    levels = slabs.bit_length() - 1
    own_ref, received = refs[0], refs[1:levels]
    edge_ref, other_ref, decay_ref, scale_ref, out_ref = refs[levels:]
    radix = decay_ref.shape[0]
    kept = SUBS // groups
    subs = sub_ids((SUBS, LANES))
    low = subs < HALF
    outers = [facing(level)[0] for level in range(levels)]
    right = facing(levels - 1)[1] == 1
    couple = jnp.zeros((SUBS, LANES), jnp.float32)
    for a in range(radix):
        d = decay_ref[a]
        spans = [power(d, cells)]
        for level in range(1, levels + 1):
            spans.append(spans[-1] * spans[-1])
        far = spans[levels] * d
        image = spans[levels - 1] * d
        rest = 1.0 / (1.0 - far * far)
        edge, other = edge_ref[a], other_ref[a]
        edge_turned, other_turned = turn(edge, HALF), turn(other, HALF)
        for part in range(2):
            i = part * radix + a
            weight, incoming = jnp.ones_like(d), jnp.zeros_like(d)
            for level in range(levels - 1):
                incoming = incoming + jnp.where(outers[level], 0.0, weight * received[level][i])
                weight = weight * jnp.where(outers[level], 1.0, spans[level])
            mine = jnp.where(low, edge, edge_turned) if part == 0 else jnp.where(low, edge_turned, edge)
            theirs = jnp.where(low, other, other_turned) if part == 0 else jnp.where(low, other_turned, other)
            entering = rest * (theirs - far * mine)
            leaving = rest * (mine - far * theirs)
            here, there = mine * entering, theirs * leaving
            couple = couple + (scale_ref[a] * d) * (jnp.where(right, there, here) + jnp.where(right, here, there))
            wall = d * turn(own_ref[i], HALF) + image * entering
            out_ref[i] = incoming + weight * jnp.where(outers[levels - 1], -wall, entering)
    out_ref[2 * radix] = edge_ref[radix] + other_ref[radix] + jnp.where(subs < kept, couple, 0.0)


def response(groups, inner, entering_ref, decay_ref, scale_ref, lane_ref, twiddle_ref):
    radix = decay_ref.shape[0]
    rows = radix // groups
    low = sub_ids((SUBS, LANES)) < HALF
    decay = decay_ref[...]
    ahead, behind = group_powers(decay, inner, groups, SUBS // groups)
    fields = ([], [])
    for part in range(2):
        for a in range(radix):
            d, incoming = decay[a], entering_ref[part * radix + a]
            turned = turn(incoming, HALF)
            from_low = scale_ref[a] * ahead[a] * jnp.where(low, incoming, turned)
            from_high = scale_ref[a] * behind[a] * jnp.where(low, turned, incoming)
            fields[part].append(
                jnp.stack([power(d, z + 1) * from_low + power(d, inner - z) * from_high for z in range(inner)])
            )
    planes = to_planes(*fields, lane_ref, twiddle_ref)
    me = lax.axis_index("gy")
    return [[for_targets([field[t * rows + a] for t in range(groups)], me)[0] for a in range(rows)] for field in planes]


def own_kernel(groups, entering_ref, decay_ref, scale_ref, lane_ref, twiddle_ref, local_ref, out_ref):
    rows, inner = local_ref.shape[0] // 2, local_ref.shape[1]
    field = response(groups, inner, entering_ref, decay_ref, scale_ref, lane_ref, twiddle_ref)
    for part in range(2):
        for a in range(rows):
            out_ref[part * rows + a] = field[part][a] + local_ref[part * rows + a]


def finish_kernel(groups, *refs):
    entering, parts = refs[:groups], refs[groups : 2 * groups]
    roots = refs[2 * groups : 4 * groups]
    lane_ref, twiddle_ref, weight_ref, previous_ref, rz_prev_ref = refs[4 * groups : 4 * groups + 5]
    out_ref, direction_ref, total_ref, out_buffer, direction_buffer, total_buffer, sems, total_sem = refs[4 * groups + 5 :]
    cells, _, waves, planes = out_buffer.shape
    kept, inner, rows = waves // groups, cells // groups, planes // LANES
    me = lax.axis_index("gy")
    block = sub_ids((SUBS, LANES)) // kept
    energies = by_source([ref[ref.shape[0] - 1] for ref in entering], me)
    total = jnp.sum(sum(energies[1:], energies[0]), axis=(0, 1), keepdims=True)
    total_buffer[...] = total
    copies = [pltpu.make_async_copy(total_buffer, total_ref, total_sem)]
    copies[0].start()
    ratio = total / rz_prev_ref[0]
    held = [[[parts[0][part * rows + a] for a in range(rows)] for part in range(2)]]
    for s in range(1, groups):
        field = response(groups, inner, entering[s], roots[2 * s], roots[2 * s + 1], lane_ref, twiddle_ref)
        held.append([[field[part][a] + parts[s][part * rows + a] for a in range(rows)] for part in range(2)])
    for zp in range(inner):
        for part in range(2):
            for a in range(rows):
                lanes = slice(a * LANES, (a + 1) * LANES)
                sources = by_source([fields[part][a][zp] for fields in held], me)
                for zg in range(groups):
                    z = zg * inner + zp
                    value = turn(sources[0], -zg * kept)
                    for t in range(1, groups):
                        value = jnp.where(block == t, turn(sources[t], (t - zg) * kept), value)
                    value = value * weight_ref[z : z + 1, lanes]
                    out_buffer[z, part, :, lanes] = value
                    direction_buffer[z, part, :, lanes] = value + ratio * previous_ref[z, part, :, lanes]
        for zg in range(groups):
            z = zg * inner + zp
            for i, (source, target) in enumerate(((out_buffer, out_ref), (direction_buffer, direction_ref))):
                copies.append(pltpu.make_async_copy(source.at[z], target.at[z], sems.at[i, z]))
                copies[-1].start()
    for copy in copies:
        copy.wait()


def float_array(*shape):
    return jax.ShapeDtypeStruct(shape, jnp.float32)


def held_array(*shape):
    return pltpu.VMEM(shape, jnp.float32)


def inside(value):
    return pltpu.with_memory_space_constraint(jnp.asarray(value), pltpu.VMEM)


def on_device(residual, direction_prev, phase_labels, phase_diffusivity, x_eigen, rz_prev):
    cells, parts, waves, planes = residual.shape
    groups, slabs = lax.axis_size("gy"), lax.axis_size("gz")
    levels = slabs.bit_length() - 1
    inner, rows = cells // groups, planes // LANES
    radix = rows * groups
    distances = [[(i, (i + s) % groups) for i in range(groups)] for s in range(1, groups)]

    weight, *pieces = pl.pallas_call(
        functools.partial(pack_kernel, groups),
        out_shape=[held_array(cells, planes)] + [held_array(parts, rows, inner, SUBS, LANES)] * groups,
        in_specs=[ANY] * 3,
        out_specs=[VMEM] * (groups + 1),
        scratch_shapes=[
            pltpu.VMEM(residual.shape, jnp.float32),
            pltpu.VMEM(phase_labels.shape, jnp.int32),
            pltpu.SMEM(phase_diffusivity.shape, jnp.float32),
            pltpu.SemaphoreType.DMA((cells,)),
            pltpu.SemaphoreType.DMA,
            pltpu.SemaphoreType.DMA,
        ],
        name="pack",
    )(residual, phase_labels, phase_diffusivity)
    held = [pieces[0]] + [lax.ppermute(x, "gy", d) for x, d in zip(pieces[1:], distances)]
    roots = pl.pallas_call(
        functools.partial(roots_kernel, groups),
        out_shape=[held_array(radix, SUBS, LANES)] * (2 * groups),
        in_specs=[VMEM, SMEM],
        out_specs=[VMEM] * (2 * groups),
        name="roots",
    )(inside(y_eigen(radix)), x_eigen)
    decay, scale = roots[:2]

    message, local = pl.pallas_call(
        functools.partial(forward_kernel, groups),
        out_shape=[
            held_array(parts * radix + 1, SUBS, LANES),
            held_array(parts, radix, inner, SUBS, LANES),
        ],
        in_specs=[VMEM] * (groups + 4),
        out_specs=[VMEM] * 2,
        name="forward",
    )(*map(inside, (*held, lane_transform(-1.0), twiddles(radix), decay, scale)))

    def swapped(value, even, odd):
        return lax.ppermute(value, "gz", [(i, i ^ (odd if i & 1 else even)) for i in range(slabs)])

    received, level, after = [], 0, None
    while level < levels - 1:
        one_bit, next_bit = 1 << level, 2 << level
        if level == 0 or level == levels - 2:
            received.append(swapped(message, one_bit, one_bit))
            message = pl.pallas_call(
                functools.partial(join_kernel, level, cells, groups),
                out_shape=held_array(*message.shape),
                in_specs=[VMEM] * 4,
                out_specs=VMEM,
                name=f"join{level}",
            )(*map(inside, (message, received[-1], decay, scale)))
            level += 1
        else:
            one = swapped(message, one_bit, next_bit)
            after = one if after is None else after
            two = swapped(message, next_bit, one_bit)
            cross = swapped(message, one_bit | next_bit, one_bit | next_bit)
            message, near, pair = pl.pallas_call(
                functools.partial(join_two_kernel, level, cells, groups),
                out_shape=[held_array(*message.shape)] * 3,
                in_specs=[VMEM] * 6,
                out_specs=[VMEM] * 3,
                name=f"join{level}",
            )(*map(inside, (message, one, two, cross, decay, scale)))
            received += [near, pair]
            level += 2
    tables = (lane_transform(1.0), twiddles(radix))
    piece = held_array(parts * rows, inner, SUBS, LANES)
    pieces = pl.pallas_call(
        functools.partial(local_kernel, groups),
        out_shape=[piece] * groups,
        in_specs=[VMEM] * 5,
        out_specs=[VMEM] * groups,
        name="local",
    )(*map(inside, (local, scale, *tables, received[0] if after is None else after)))
    held = [lax.ppermute(x, "gy", d) for x, d in zip(pieces[1:], distances)]

    edge = pl.pallas_call(
        functools.partial(edge_kernel, level, cells, groups),
        out_shape=held_array(radix + 1, SUBS, LANES),
        in_specs=[VMEM] * 3,
        out_specs=VMEM,
        name="edge",
    )(*map(inside, (message, decay, scale)))
    other = swapped(edge, 1 << level, 1 << level)
    entering = pl.pallas_call(
        functools.partial(entering_kernel, groups, slabs, cells),
        out_shape=held_array(*message.shape),
        in_specs=[VMEM] * (levels + 4),
        out_specs=VMEM,
        name="entering",
    )(*map(inside, (message, *received, edge, other, decay, scale)))
    entered = [entering] + [lax.ppermute(entering, "gy", d) for d in distances]
    own = pl.pallas_call(
        functools.partial(own_kernel, groups),
        out_shape=piece,
        in_specs=[VMEM] * 6,
        out_specs=VMEM,
        name="own",
    )(*map(inside, (entering, decay, scale, *tables, pieces[0])))

    preconditioned, direction, total = pl.pallas_call(
        functools.partial(finish_kernel, groups),
        out_shape=[float_array(*residual.shape), float_array(*residual.shape), float_array(1, 1)],
        in_specs=[VMEM] * (4 * groups + 4) + [SMEM],
        out_specs=[ANY] * 3,
        scratch_shapes=[
            pltpu.VMEM(residual.shape, jnp.float32),
            pltpu.VMEM(residual.shape, jnp.float32),
            pltpu.VMEM((1, 1), jnp.float32),
            pltpu.SemaphoreType.DMA((2, cells)),
            pltpu.SemaphoreType.DMA,
        ],
        name="finish",
    )(*map(inside, (*entered, own, *held, *roots, *tables, weight, direction_prev)), rz_prev)
    return preconditioned, direction, jnp.reshape(total, (1,))


def solution(mesh):
    placed = (P("gz", None, None, "gy"), P("gz", None, None, "gy"), P("gz", "gy"), P(), P(), P())
    return jax.shard_map(
        on_device,
        mesh=mesh,
        in_specs=placed,
        out_specs=(P("gz", None, None, "gy"), P("gz", None, None, "gy"), P()),
        check_vma=False,
    )
```

```python
import functools

import jax
import jax.numpy as jnp
import numpy as np
from jax import lax
from jax.experimental import pallas as pl
from jax.experimental.pallas import tpu as pltpu
from jax.sharding import PartitionSpec as P

LANES = 128
SUBS = 8
HALF = 4
VMEM = pl.BlockSpec(memory_space=pltpu.VMEM)
SMEM = pl.BlockSpec(memory_space=pltpu.SMEM)
ANY = pl.BlockSpec(memory_space=pl.ANY)


def split_bf16(table):
    high = table.astype(jnp.bfloat16)
    low = (table - np.asarray(high, np.float64)).astype(jnp.bfloat16)
    return np.stack([np.asarray(high), np.asarray(low)])


def lane_transform(sign):
    ids = np.arange(LANES)
    angle = 2.0 * np.pi * (ids[:, None] * ids[None, :] % LANES) / LANES
    cosine, sine = np.cos(angle), sign * np.sin(angle)
    return split_bf16(np.block([[cosine, sine], [-sine, cosine]]))


def twiddles(radix):
    angle = 2.0 * np.pi * np.arange(radix)[:, None] * np.arange(LANES)[None, :] / (radix * LANES)
    return np.stack([np.cos(angle), np.sin(angle)]).astype(np.float32)


def y_eigen(radix):
    wave = np.arange(radix)[:, None] + radix * np.arange(LANES)[None, :]
    return (4.0 * np.sin(np.pi * wave / (radix * LANES)) ** 2).astype(np.float32)


def power(base, exponent):
    result = None
    while exponent:
        if exponent & 1:
            result = base if result is None else result * base
        exponent >>= 1
        if exponent:
            base = base * base
    return result


def small_dft(re, im, sign):
    count = len(re)
    if count == 1:
        return re, im
    even_re, even_im = small_dft(re[0::2], im[0::2], sign)
    odd_re, odd_im = small_dft(re[1::2], im[1::2], sign)
    out_re, out_im = [None] * count, [None] * count
    for i in range(count // 2):
        angle = 2.0 * np.pi * i / count
        c, s = float(np.cos(angle)), float(sign * np.sin(angle))
        if i == 0:
            a, b = odd_re[i], odd_im[i]
        elif 4 * i == count:
            a, b = (odd_im[i], -odd_re[i]) if sign < 0 else (-odd_im[i], odd_re[i])
        else:
            a = odd_re[i] * c - odd_im[i] * s
            b = odd_re[i] * s + odd_im[i] * c
        out_re[i], out_im[i] = even_re[i] + a, even_im[i] + b
        out_re[i + count // 2], out_im[i + count // 2] = even_re[i] - a, even_im[i] - b
    return out_re, out_im


def lane_product(re, im, table_ref):
    count, shape = len(re), re[0].shape
    rows = int(np.prod(shape[:-1]))
    flat = jnp.concatenate(
        [jnp.concatenate([a.reshape(rows, LANES), b.reshape(rows, LANES)], axis=1) for a, b in zip(re, im)],
        axis=0,
    )
    high = flat.astype(jnp.bfloat16)
    low = (flat - high.astype(jnp.float32)).astype(jnp.bfloat16)
    dot = functools.partial(jnp.dot, preferred_element_type=jnp.float32)
    out = dot(high, table_ref[0]) + (dot(low, table_ref[0]) + dot(high, table_ref[1]))
    out_re = [out[i * rows : (i + 1) * rows, :LANES].reshape(shape) for i in range(count)]
    out_im = [out[i * rows : (i + 1) * rows, LANES:].reshape(shape) for i in range(count)]
    return out_re, out_im


def sub_ids(shape):
    return lax.broadcasted_iota(jnp.int32, shape, len(shape) - 2)


def turn(value, shift):
    shift = shift % SUBS
    return value if shift == 0 else pltpu.roll(value, shift, value.ndim - 2)


def for_targets(pieces, me):
    peers = len(pieces)
    out = []
    for s in range(peers):
        chosen = pieces[0]
        for t in range(1, peers):
            chosen = jnp.where(lax.rem(me + s, peers) == t, pieces[t], chosen)
        out.append(chosen)
    return out


def by_source(held, me):
    peers = len(held)
    out = []
    for t in range(peers):
        chosen = held[0]
        for s in range(1, peers):
            chosen = jnp.where(lax.rem(me + (peers - t), peers) == s, held[s], chosen)
        out.append(chosen)
    return out


def cell_weight(labels, diffusivity_ref):
    weight = jnp.zeros(labels.shape, jnp.float32)
    for i in range(diffusivity_ref.shape[0]):
        value = lax.rsqrt(jnp.full(labels.shape, diffusivity_ref[i], jnp.float32))
        weight = jnp.where(labels == i, value, weight)
    return weight


def mode_roots(eigen_ref, y_eigen_ref, me, kept, length):
    radix = y_eigen_ref.shape[0]
    subs = sub_ids((SUBS, LANES))
    x_part = jnp.zeros((SUBS, LANES), jnp.float32)
    for i in range(kept):
        x_part = jnp.where(lax.rem(subs, kept) == i, eigen_ref[me * kept + i], x_part)
    half_shift = 0.5 * jnp.stack([x_part + y_eigen_ref[a : a + 1, :] for a in range(radix)])
    root = jnp.sqrt(half_shift * (half_shift + 2.0))
    return 1.0 / (1.0 + half_shift + root), (0.5 / length) / root


def group_powers(decay, cells, groups, kept):
    group = sub_ids((SUBS, LANES)) // kept
    ahead = jnp.ones_like(decay)
    behind = jnp.ones_like(decay)
    bit = 1
    while bit < groups:
        factor = power(decay, cells * bit)
        ahead = ahead * jnp.where((group & bit) != 0, factor, 1.0)
        behind = behind * jnp.where((group & bit) != 0, 1.0, factor)
        bit *= 2
    return ahead, behind


def pack_kernel(groups, residual_any, labels_any, diffusivity_any, weight_ref, *refs):
    out_refs, (residual_ref, labels_ref, diffusivity_ref, cell_sems, label_sem, value_sem) = refs[:groups], refs[groups:]
    values = pltpu.make_async_copy(diffusivity_any, diffusivity_ref, value_sem)
    labels = pltpu.make_async_copy(labels_any, labels_ref, label_sem)
    values.start()
    labels.start()
    arriving = [
        pltpu.make_async_copy(residual_any.at[z], residual_ref.at[z], cell_sems.at[z]) for z in range(residual_ref.shape[0])
    ]
    order = [zg * (len(arriving) // groups) + zp for zp in range(len(arriving) // groups) for zg in range(groups)]
    for z in order:
        arriving[z].start()
    values.wait()
    labels.wait()
    cells, _, waves, planes = residual_ref.shape
    kept, inner = waves // groups, cells // groups
    me = lax.axis_index("gy")
    group = sub_ids((SUBS, LANES)) // kept
    weight = cell_weight(labels_ref[...], diffusivity_ref)
    weight_ref[...] = weight
    for zp in range(inner):
        for zg in range(groups):
            arriving[zg * inner + zp].wait()
        for part in range(2):
            for a in range(planes // LANES):
                lanes = slice(a * LANES, (a + 1) * LANES)
                rows = [residual_ref[z, part, :, lanes] * weight[z : z + 1, lanes] for z in range(zp, cells, inner)]
                pieces = []
                for t in range(groups):
                    piece = turn(rows[0], -t * kept)
                    for zg in range(1, groups):
                        piece = jnp.where(group == zg, turn(rows[zg], (zg - t) * kept), piece)
                    pieces.append(piece)
                for ref, value in zip(out_refs, for_targets(pieces, me)):
                    ref[part, a, zp] = value


def roots_kernel(groups, y_eigen_ref, eigen_ref, *out_refs):
    length = y_eigen_ref.shape[0] * LANES
    for s in range(groups):
        device = lax.rem(lax.axis_index("gy") + groups - s, groups)
        decay, scale = mode_roots(eigen_ref, y_eigen_ref, device, SUBS // groups, length)
        out_refs[2 * s][...] = decay
        out_refs[2 * s + 1][...] = scale


def forward_kernel(groups, *refs):
    held = refs[:groups]
    lane_ref, twiddle_ref, decay_ref, scale_ref = refs[groups : groups + 4]
    message_ref, local_ref = refs[groups + 4 :]
    _, block_rows, inner, _, _ = held[0].shape
    radix = block_rows * groups
    kept = SUBS // groups
    me = lax.axis_index("gy")
    re, im = [], []
    blocks = [by_source([ref[part] for ref in held], me) for part in range(2)]
    for t in range(groups):
        for a in range(block_rows):
            re.append(blocks[0][t][a])
            im.append(blocks[1][t][a])
    re, im = small_dft(re, im, -1.0)
    turned_re, turned_im = [], []
    for a in range(radix):
        c, s = twiddle_ref[0, a : a + 1, :], twiddle_ref[1, a : a + 1, :]
        turned_re.append(re[a] * c + im[a] * s)
        turned_im.append(im[a] * c - re[a] * s)
    re, im = lane_product(turned_re, turned_im, lane_ref)
    decay, scale = decay_ref[...], scale_ref[...]
    group = sub_ids((SUBS, LANES)) // kept
    subs = sub_ids((SUBS, LANES))
    energy = jnp.zeros((SUBS, LANES), jnp.float32)
    for part, field in enumerate((re, im)):
        for a in range(radix):
            d, g = decay[a], scale[a]
            cell = [field[a][i] for i in range(inner)]
            ahead, behind = [cell[0]], [cell[-1]]
            for i in range(1, inner):
                ahead.append(cell[i] + d * ahead[-1])
                behind.append(cell[inner - 1 - i] + d * behind[-1])
            behind = behind[::-1]
            value = [ahead[i] + behind[i] - cell[i] for i in range(inner)]
            total = sum(cell[i] * value[i] for i in range(inner))
            last, first = ahead[-1], behind[0]
            from_low = jnp.zeros_like(last)
            from_high = jnp.zeros_like(first)
            low_weight, high_weight = jnp.ones_like(last), jnp.ones_like(first)
            bit = 1
            while bit < groups:
                upper = (group & bit) != 0
                step = bit * kept
                if 2 * step == SUBS:
                    other_last, other_first = turn(last, step), turn(first, step)
                else:
                    other_last = jnp.where(upper, turn(last, step), turn(last, -step))
                    other_first = jnp.where(upper, turn(first, step), turn(first, -step))
                span = power(d, inner * bit)
                joined = 2.0 * d * other_last * first
                total = total + jnp.where(upper & ((group & (bit - 1)) == 0), joined, 0.0)
                from_low = from_low + jnp.where(upper, low_weight * other_last, 0.0)
                from_high = from_high + jnp.where(upper, 0.0, high_weight * other_first)
                low_weight = low_weight * jnp.where(upper, span, 1.0)
                high_weight = high_weight * jnp.where(upper, 1.0, span)
                last = jnp.where(upper, last + span * other_last, other_last + span * last)
                first = jnp.where(upper, other_first + span * first, first + span * other_first)
                bit *= 2
            energy = energy + g * total
            message_ref[part * radix + a] = jnp.where(subs < HALF, last, first)
            for i in range(inner):
                spread = power(d, i + 1) * from_low + power(d, inner - i) * from_high
                local_ref[part, a, i] = value[i] + spread
    message_ref[2 * radix] = energy


def facing(level):
    low = sub_ids((SUBS, LANES)) < HALF
    right = lax.rem(lax.shift_right_logical(lax.axis_index("gz"), level), 2)
    return jnp.where(low, 1, 0) != right, right


def join(level, cells, groups, own, other, decay, scale):
    radix = decay.shape[0]
    kept = SUBS // groups
    outer, _ = facing(level)
    joined, couple = [], jnp.zeros((SUBS, LANES), jnp.float32)
    for i in range(2 * radix):
        d, g = decay[i % radix], scale[i % radix]
        span = power(d, cells << level)
        joined.append(jnp.where(outer, other[i] + span * own[i], own[i] + span * other[i]))
        couple = couple + (2.0 * g * d) * jnp.where(outer, own[i] * turn(other[i], HALF), 0.0)
    couple = couple + turn(couple, HALF)
    joined.append(own[-1] + other[-1] + jnp.where(sub_ids((SUBS, LANES)) < kept, couple, 0.0))
    return joined


def rows_of(ref):
    return [ref[i] for i in range(ref.shape[0])]


def join_kernel(level, cells, groups, own_ref, other_ref, decay_ref, scale_ref, out_ref):
    joined = join(level, cells, groups, rows_of(own_ref), rows_of(other_ref), decay_ref[...], scale_ref[...])
    for i, value in enumerate(joined):
        out_ref[i] = value


def join_two_kernel(level, cells, groups, own_ref, near_ref, far_ref, cross_ref, decay_ref, scale_ref, out_ref, pair_ref):
    decay, scale = decay_ref[...], scale_ref[...]
    own = join(level, cells, groups, rows_of(own_ref), rows_of(near_ref), decay, scale)
    other = join(level, cells, groups, rows_of(far_ref), rows_of(cross_ref), decay, scale)
    joined = join(level + 1, cells, groups, own, other, decay, scale)
    for i in range(len(joined)):
        out_ref[i] = joined[i]
        pair_ref[i] = other[i]


def edge_kernel(level, cells, groups, own_ref, decay_ref, scale_ref, out_ref):
    radix = decay_ref.shape[0]
    kept = SUBS // groups
    subs = sub_ids((SUBS, LANES))
    outer, _ = facing(level)
    walls = jnp.zeros((SUBS, LANES), jnp.float32)
    for a in range(radix):
        d = decay_ref[a]
        image = power(d, (cells << level) + 1)
        both = []
        for part in range(2):
            own = own_ref[part * radix + a]
            near = jnp.where(outer, 0.0, own)
            walls = walls + (scale_ref[a] * d * d) * (near * near)
            sent = own - image * turn(own, HALF)
            both.append(jnp.where(outer, sent, turn(sent, HALF)))
        out_ref[a] = jnp.where(subs < HALF, both[0], both[1])
    out_ref[radix] = own_ref[2 * radix] - jnp.where(lax.rem(subs, HALF) < kept, walls, 0.0)


def to_planes(re, im, lane_ref, twiddle_ref):
    re, im = lane_product(re, im, lane_ref)
    turned_re, turned_im = [], []
    for a in range(len(re)):
        c, s = twiddle_ref[0, a : a + 1, :], twiddle_ref[1, a : a + 1, :]
        turned_re.append(re[a] * c - im[a] * s)
        turned_im.append(im[a] * c + re[a] * s)
    return small_dft(turned_re, turned_im, 1.0)


def local_kernel(groups, local_ref, scale_ref, lane_ref, twiddle_ref, *out_refs):
    radix = scale_ref.shape[0]
    rows = radix // groups
    fields = [[scale_ref[a] * local_ref[part, a] for a in range(radix)] for part in range(2)]
    for part, field in enumerate(to_planes(*fields, lane_ref, twiddle_ref)):
        for a in range(rows):
            pieces = [field[t * rows + a] for t in range(groups)]
            for ref, value in zip(out_refs, for_targets(pieces, lax.axis_index("gy"))):
                ref[part * rows + a] = value


def entering_kernel(groups, slabs, cells, *refs):
    levels = slabs.bit_length() - 1
    own_ref, first_ref, received = refs[0], refs[1], refs[2 : levels + 1]
    edge_ref, other_ref, decay_ref, scale_ref, out_ref, mate_ref = refs[levels + 1 :]
    radix = decay_ref.shape[0]
    kept = SUBS // groups
    subs = sub_ids((SUBS, LANES))
    low = subs < HALF
    outers = [facing(level)[0] for level in range(levels)]
    right = facing(levels - 1)[1] == 1
    couple = jnp.zeros((SUBS, LANES), jnp.float32)
    for a in range(radix):
        d = decay_ref[a]
        spans = [power(d, cells)]
        for level in range(1, levels + 1):
            spans.append(spans[-1] * spans[-1])
        far = spans[levels] * d
        image = spans[levels - 1] * d
        rest = 1.0 / (1.0 - far * far)
        edge, other = edge_ref[a], other_ref[a]
        edge_turned, other_turned = turn(edge, HALF), turn(other, HALF)
        for part in range(2):
            i = part * radix + a
            sides = [
                (jnp.where(outers[0], 0.0, received[0][i]), jnp.where(outers[0], 1.0, spans[0])),
                (jnp.where(outers[0], first_ref[i], 0.0), jnp.where(outers[0], spans[0], 1.0)),
            ]
            mine = jnp.where(low, edge, edge_turned) if part == 0 else jnp.where(low, edge_turned, edge)
            theirs = jnp.where(low, other, other_turned) if part == 0 else jnp.where(low, other_turned, other)
            entering = rest * (theirs - far * mine)
            leaving = rest * (mine - far * theirs)
            here, there = mine * entering, theirs * leaving
            couple = couple + (scale_ref[a] * d) * (jnp.where(right, there, here) + jnp.where(right, here, there))
            wall = d * turn(own_ref[i], HALF) + image * entering
            for ref, (incoming, weight) in zip((out_ref, mate_ref), sides):
                for level in range(1, levels - 1):
                    incoming = incoming + jnp.where(outers[level], 0.0, weight * received[level][i])
                    weight = weight * jnp.where(outers[level], 1.0, spans[level])
                ref[i] = incoming + weight * jnp.where(outers[levels - 1], -wall, entering)
    energy = edge_ref[radix] + other_ref[radix] + jnp.where(subs < kept, couple, 0.0)
    out_ref[2 * radix] = energy
    mate_ref[2 * radix] = energy


def response(groups, inner, entering_ref, decay_ref, scale_ref, lane_ref, twiddle_ref):
    radix = decay_ref.shape[0]
    rows = radix // groups
    low = sub_ids((SUBS, LANES)) < HALF
    decay = decay_ref[...]
    ahead, behind = group_powers(decay, inner, groups, SUBS // groups)
    fields = ([], [])
    for part in range(2):
        for a in range(radix):
            d, incoming = decay[a], entering_ref[part * radix + a]
            turned = turn(incoming, HALF)
            from_low = scale_ref[a] * ahead[a] * jnp.where(low, incoming, turned)
            from_high = scale_ref[a] * behind[a] * jnp.where(low, turned, incoming)
            fields[part].append(
                jnp.stack([power(d, z + 1) * from_low + power(d, inner - z) * from_high for z in range(inner)])
            )
    planes = to_planes(*fields, lane_ref, twiddle_ref)
    me = lax.axis_index("gy")
    return [[for_targets([field[t * rows + a] for t in range(groups)], me)[0] for a in range(rows)] for field in planes]


def own_kernel(groups, entering_ref, decay_ref, scale_ref, lane_ref, twiddle_ref, local_ref, out_ref):
    rows, inner = local_ref.shape[0] // 2, local_ref.shape[1]
    field = response(groups, inner, entering_ref, decay_ref, scale_ref, lane_ref, twiddle_ref)
    for part in range(2):
        for a in range(rows):
            out_ref[part * rows + a] = field[part][a] + local_ref[part * rows + a]


def finish_kernel(groups, *refs):
    entering, parts = refs[:groups], refs[groups : 2 * groups]
    roots = refs[2 * groups : 4 * groups]
    lane_ref, twiddle_ref, weight_ref, previous_ref, rz_prev_ref = refs[4 * groups : 4 * groups + 5]
    out_ref, direction_ref, total_ref, out_buffer, direction_buffer, total_buffer, sems, total_sem = refs[4 * groups + 5 :]
    cells, _, waves, planes = out_buffer.shape
    kept, inner, rows = waves // groups, cells // groups, planes // LANES
    me = lax.axis_index("gy")
    block = sub_ids((SUBS, LANES)) // kept
    energies = by_source([ref[ref.shape[0] - 1] for ref in entering], me)
    total = jnp.sum(sum(energies[1:], energies[0]), axis=(0, 1), keepdims=True)
    total_buffer[...] = total
    copies = [pltpu.make_async_copy(total_buffer, total_ref, total_sem)]
    copies[0].start()
    ratio = total / rz_prev_ref[0]
    held = [[[parts[0][part * rows + a] for a in range(rows)] for part in range(2)]]
    for s in range(1, groups):
        field = response(groups, inner, entering[s], roots[2 * s], roots[2 * s + 1], lane_ref, twiddle_ref)
        held.append([[field[part][a] + parts[s][part * rows + a] for a in range(rows)] for part in range(2)])
    for zp in range(inner):
        for part in range(2):
            for a in range(rows):
                lanes = slice(a * LANES, (a + 1) * LANES)
                sources = by_source([fields[part][a][zp] for fields in held], me)
                for zg in range(groups):
                    z = zg * inner + zp
                    value = turn(sources[0], -zg * kept)
                    for t in range(1, groups):
                        value = jnp.where(block == t, turn(sources[t], (t - zg) * kept), value)
                    value = value * weight_ref[z : z + 1, lanes]
                    out_buffer[z, part, :, lanes] = value
                    direction_buffer[z, part, :, lanes] = value + ratio * previous_ref[z, part, :, lanes]
        for zg in range(groups):
            z = zg * inner + zp
            for i, (source, target) in enumerate(((out_buffer, out_ref), (direction_buffer, direction_ref))):
                copies.append(pltpu.make_async_copy(source.at[z], target.at[z], sems.at[i, z]))
                copies[-1].start()
    for copy in copies:
        copy.wait()


def float_array(*shape):
    return jax.ShapeDtypeStruct(shape, jnp.float32)


def held_array(*shape):
    return pltpu.VMEM(shape, jnp.float32)


def inside(value):
    return pltpu.with_memory_space_constraint(jnp.asarray(value), pltpu.VMEM)


def on_device(residual, direction_prev, phase_labels, phase_diffusivity, x_eigen, rz_prev):
    cells, parts, waves, planes = residual.shape
    groups, slabs = lax.axis_size("gy"), lax.axis_size("gz")
    levels = slabs.bit_length() - 1
    inner, rows = cells // groups, planes // LANES
    radix = rows * groups
    distances = [[(i, (i + s) % groups) for i in range(groups)] for s in range(1, groups)]

    weight, *pieces = pl.pallas_call(
        functools.partial(pack_kernel, groups),
        out_shape=[held_array(cells, planes)] + [held_array(parts, rows, inner, SUBS, LANES)] * groups,
        in_specs=[ANY] * 3,
        out_specs=[VMEM] * (groups + 1),
        scratch_shapes=[
            pltpu.VMEM(residual.shape, jnp.float32),
            pltpu.VMEM(phase_labels.shape, jnp.int32),
            pltpu.SMEM(phase_diffusivity.shape, jnp.float32),
            pltpu.SemaphoreType.DMA((cells,)),
            pltpu.SemaphoreType.DMA,
            pltpu.SemaphoreType.DMA,
        ],
        name="pack",
    )(residual, phase_labels, phase_diffusivity)
    held = [pieces[0]] + [lax.ppermute(x, "gy", d) for x, d in zip(pieces[1:], distances)]
    roots = pl.pallas_call(
        functools.partial(roots_kernel, groups),
        out_shape=[held_array(radix, SUBS, LANES)] * (2 * groups),
        in_specs=[VMEM, SMEM],
        out_specs=[VMEM] * (2 * groups),
        name="roots",
    )(inside(y_eigen(radix)), x_eigen)
    decay, scale = roots[:2]

    message, local = pl.pallas_call(
        functools.partial(forward_kernel, groups),
        out_shape=[
            held_array(parts * radix + 1, SUBS, LANES),
            held_array(parts, radix, inner, SUBS, LANES),
        ],
        in_specs=[VMEM] * (groups + 4),
        out_specs=[VMEM] * 2,
        name="forward",
    )(*map(inside, (*held, lane_transform(-1.0), twiddles(radix), decay, scale)))

    def swapped(value, bits):
        return lax.ppermute(value, "gz", [(i, i ^ bits) for i in range(slabs)])

    first, received, level = message, [], 0
    while level < levels - 1:
        bit, cross = 1 << level, min(level, 1)
        near = swapped(message, bit | cross)
        received.append(near)
        if level == 0 or level == levels - 2:
            message = pl.pallas_call(
                functools.partial(join_kernel, level, cells, groups),
                out_shape=held_array(*message.shape),
                in_specs=[VMEM] * 4,
                out_specs=VMEM,
                name=f"join{level}",
            )(*map(inside, (message, near, decay, scale)))
            level += 1
        else:
            message, pair = pl.pallas_call(
                functools.partial(join_two_kernel, level, cells, groups),
                out_shape=[held_array(*message.shape)] * 2,
                in_specs=[VMEM] * 6,
                out_specs=[VMEM] * 2,
                name=f"join{level}",
            )(*map(inside, (message, near, swapped(message, 2 * bit | 1), swapped(message, 3 * bit | 1), decay, scale)))
            received.append(pair)
            level += 2
    tables = (lane_transform(1.0), twiddles(radix))
    piece = held_array(parts * rows, inner, SUBS, LANES)
    pieces = pl.pallas_call(
        functools.partial(local_kernel, groups),
        out_shape=[piece] * groups,
        in_specs=[VMEM] * 4,
        out_specs=[VMEM] * groups,
        name="local",
    )(*map(inside, (local, scale, *tables)))
    held = [lax.ppermute(x, "gy", d) for x, d in zip(pieces[1:], distances)]

    edge = pl.pallas_call(
        functools.partial(edge_kernel, level, cells, groups),
        out_shape=held_array(radix + 1, SUBS, LANES),
        in_specs=[VMEM] * 3,
        out_specs=VMEM,
        name="edge",
    )(*map(inside, (message, decay, scale)))
    other = swapped(edge, 1 << level | 1)
    entering, mate = pl.pallas_call(
        functools.partial(entering_kernel, groups, slabs, cells),
        out_shape=[held_array(*message.shape)] * 2,
        in_specs=[VMEM] * (levels + 5),
        out_specs=[VMEM] * 2,
        name="entering",
    )(*map(inside, (message, first, *received, edge, other, decay, scale)))
    crossed = [[(i * slabs + z, j * slabs + (z ^ 1)) for i, j in d for z in range(slabs)] for d in distances]
    entered = [entering] + [lax.ppermute(mate, ("gy", "gz"), d) for d in crossed]
    own = pl.pallas_call(
        functools.partial(own_kernel, groups),
        out_shape=piece,
        in_specs=[VMEM] * 6,
        out_specs=VMEM,
        name="own",
    )(*map(inside, (entering, decay, scale, *tables, pieces[0])))

    preconditioned, direction, total = pl.pallas_call(
        functools.partial(finish_kernel, groups),
        out_shape=[float_array(*residual.shape), float_array(*residual.shape), float_array(1, 1)],
        in_specs=[VMEM] * (4 * groups + 4) + [SMEM],
        out_specs=[ANY] * 3,
        scratch_shapes=[
            pltpu.VMEM(residual.shape, jnp.float32),
            pltpu.VMEM(residual.shape, jnp.float32),
            pltpu.VMEM((1, 1), jnp.float32),
            pltpu.SemaphoreType.DMA((2, cells)),
            pltpu.SemaphoreType.DMA,
        ],
        name="finish",
    )(*map(inside, (*entered, own, *held, *roots, *tables, weight, direction_prev)), rz_prev)
    return preconditioned, direction, jnp.reshape(total, (1,))


def solution(mesh):
    placed = (P("gz", None, None, "gy"), P("gz", None, None, "gy"), P("gz", "gy"), P(), P(), P())
    return jax.shard_map(
        on_device,
        mesh=mesh,
        in_specs=placed,
        out_specs=(P("gz", None, None, "gy"), P("gz", None, None, "gy"), P()),
        check_vma=False,
    )
```

```python
import functools

import jax
import jax.numpy as jnp
import numpy as np
from jax import lax
from jax.experimental import pallas as pl
from jax.experimental.pallas import tpu as pltpu
from jax.sharding import PartitionSpec as P

LANES = 128
SUBS = 8
HALF = 4
VMEM = pl.BlockSpec(memory_space=pltpu.VMEM)
SMEM = pl.BlockSpec(memory_space=pltpu.SMEM)
ANY = pl.BlockSpec(memory_space=pl.ANY)


def split_bf16(table):
    high = table.astype(jnp.bfloat16)
    low = (table - np.asarray(high, np.float64)).astype(jnp.bfloat16)
    return np.stack([np.asarray(high), np.asarray(low)])


def lane_transform(sign):
    ids = np.arange(LANES)
    angle = 2.0 * np.pi * (ids[:, None] * ids[None, :] % LANES) / LANES
    cosine, sine = np.cos(angle), sign * np.sin(angle)
    return split_bf16(np.block([[cosine, sine], [-sine, cosine]]))


def twiddles(radix):
    angle = 2.0 * np.pi * np.arange(radix)[:, None] * np.arange(LANES)[None, :] / (radix * LANES)
    return np.stack([np.cos(angle), np.sin(angle)]).astype(np.float32)


def y_eigen(radix):
    wave = np.arange(radix)[:, None] + radix * np.arange(LANES)[None, :]
    return (4.0 * np.sin(np.pi * wave / (radix * LANES)) ** 2).astype(np.float32)


def power(base, exponent):
    result = None
    while exponent:
        if exponent & 1:
            result = base if result is None else result * base
        exponent >>= 1
        if exponent:
            base = base * base
    return result


def small_dft(re, im, sign):
    count = len(re)
    if count == 1:
        return re, im
    even_re, even_im = small_dft(re[0::2], im[0::2], sign)
    odd_re, odd_im = small_dft(re[1::2], im[1::2], sign)
    out_re, out_im = [None] * count, [None] * count
    for i in range(count // 2):
        angle = 2.0 * np.pi * i / count
        c, s = float(np.cos(angle)), float(sign * np.sin(angle))
        if i == 0:
            a, b = odd_re[i], odd_im[i]
        elif 4 * i == count:
            a, b = (odd_im[i], -odd_re[i]) if sign < 0 else (-odd_im[i], odd_re[i])
        else:
            a = odd_re[i] * c - odd_im[i] * s
            b = odd_re[i] * s + odd_im[i] * c
        out_re[i], out_im[i] = even_re[i] + a, even_im[i] + b
        out_re[i + count // 2], out_im[i + count // 2] = even_re[i] - a, even_im[i] - b
    return out_re, out_im


def lane_product(re, im, table_ref):
    count, shape = len(re), re[0].shape
    rows = int(np.prod(shape[:-1]))
    flat = jnp.concatenate(
        [jnp.concatenate([a.reshape(rows, LANES), b.reshape(rows, LANES)], axis=1) for a, b in zip(re, im)],
        axis=0,
    )
    high = flat.astype(jnp.bfloat16)
    low = (flat - high.astype(jnp.float32)).astype(jnp.bfloat16)
    dot = functools.partial(jnp.dot, preferred_element_type=jnp.float32)
    out = dot(high, table_ref[0]) + (dot(low, table_ref[0]) + dot(high, table_ref[1]))
    out_re = [out[i * rows : (i + 1) * rows, :LANES].reshape(shape) for i in range(count)]
    out_im = [out[i * rows : (i + 1) * rows, LANES:].reshape(shape) for i in range(count)]
    return out_re, out_im


def sub_ids(shape):
    return lax.broadcasted_iota(jnp.int32, shape, len(shape) - 2)


def turn(value, shift):
    shift = shift % SUBS
    return value if shift == 0 else pltpu.roll(value, shift, value.ndim - 2)


def for_targets(pieces, me):
    peers = len(pieces)
    out = []
    for s in range(peers):
        chosen = pieces[0]
        for t in range(1, peers):
            chosen = jnp.where(lax.rem(me + s, peers) == t, pieces[t], chosen)
        out.append(chosen)
    return out


def by_source(held, me):
    peers = len(held)
    out = []
    for t in range(peers):
        chosen = held[0]
        for s in range(1, peers):
            chosen = jnp.where(lax.rem(me + (peers - t), peers) == s, held[s], chosen)
        out.append(chosen)
    return out


def cell_weight(labels, diffusivity_ref):
    weight = jnp.zeros(labels.shape, jnp.float32)
    for i in range(diffusivity_ref.shape[0]):
        value = lax.rsqrt(jnp.full(labels.shape, diffusivity_ref[i], jnp.float32))
        weight = jnp.where(labels == i, value, weight)
    return weight


def mode_roots(eigen_ref, y_eigen_ref, me, kept, length):
    radix = y_eigen_ref.shape[0]
    subs = sub_ids((SUBS, LANES))
    x_part = jnp.zeros((SUBS, LANES), jnp.float32)
    for i in range(kept):
        x_part = jnp.where(lax.rem(subs, kept) == i, eigen_ref[me * kept + i], x_part)
    half_shift = 0.5 * jnp.stack([x_part + y_eigen_ref[a : a + 1, :] for a in range(radix)])
    root = jnp.sqrt(half_shift * (half_shift + 2.0))
    return 1.0 / (1.0 + half_shift + root), (0.5 / length) / root


def group_powers(decay, cells, groups, kept):
    group = sub_ids((SUBS, LANES)) // kept
    ahead = jnp.ones_like(decay)
    behind = jnp.ones_like(decay)
    bit = 1
    while bit < groups:
        factor = power(decay, cells * bit)
        ahead = ahead * jnp.where((group & bit) != 0, factor, 1.0)
        behind = behind * jnp.where((group & bit) != 0, 1.0, factor)
        bit *= 2
    return ahead, behind


def pack_kernel(groups, residual_any, labels_any, diffusivity_any, weight_ref, *refs):
    out_refs, (residual_ref, labels_ref, diffusivity_ref, cell_sems, label_sem, value_sem) = refs[:groups], refs[groups:]
    values = pltpu.make_async_copy(diffusivity_any, diffusivity_ref, value_sem)
    labels = pltpu.make_async_copy(labels_any, labels_ref, label_sem)
    values.start()
    labels.start()
    arriving = [
        pltpu.make_async_copy(residual_any.at[z], residual_ref.at[z], cell_sems.at[z]) for z in range(residual_ref.shape[0])
    ]
    order = [zg * (len(arriving) // groups) + zp for zp in range(len(arriving) // groups) for zg in range(groups)]
    for z in order:
        arriving[z].start()
    values.wait()
    labels.wait()
    cells, _, waves, planes = residual_ref.shape
    kept, inner = waves // groups, cells // groups
    me = lax.axis_index("gy")
    group = sub_ids((SUBS, LANES)) // kept
    weight = cell_weight(labels_ref[...], diffusivity_ref)
    weight_ref[...] = weight
    for zp in range(inner):
        for zg in range(groups):
            arriving[zg * inner + zp].wait()
        for part in range(2):
            for a in range(planes // LANES):
                lanes = slice(a * LANES, (a + 1) * LANES)
                rows = [residual_ref[z, part, :, lanes] * weight[z : z + 1, lanes] for z in range(zp, cells, inner)]
                pieces = []
                for t in range(groups):
                    piece = turn(rows[0], -t * kept)
                    for zg in range(1, groups):
                        piece = jnp.where(group == zg, turn(rows[zg], (zg - t) * kept), piece)
                    pieces.append(piece)
                for ref, value in zip(out_refs, for_targets(pieces, me)):
                    ref[part, a, zp] = value


def roots_kernel(groups, y_eigen_ref, eigen_ref, *out_refs):
    length = y_eigen_ref.shape[0] * LANES
    for s in range(groups):
        device = lax.rem(lax.axis_index("gy") + groups - s, groups)
        decay, scale = mode_roots(eigen_ref, y_eigen_ref, device, SUBS // groups, length)
        out_refs[2 * s][...] = decay
        out_refs[2 * s + 1][...] = scale


def forward_kernel(groups, *refs):
    held = refs[:groups]
    lane_ref, twiddle_ref, decay_ref, scale_ref = refs[groups : groups + 4]
    message_ref, local_ref = refs[groups + 4 :]
    _, block_rows, inner, _, _ = held[0].shape
    radix = block_rows * groups
    kept = SUBS // groups
    me = lax.axis_index("gy")
    re, im = [], []
    blocks = [by_source([ref[part] for ref in held], me) for part in range(2)]
    for t in range(groups):
        for a in range(block_rows):
            re.append(blocks[0][t][a])
            im.append(blocks[1][t][a])
    re, im = small_dft(re, im, -1.0)
    turned_re, turned_im = [], []
    for a in range(radix):
        c, s = twiddle_ref[0, a : a + 1, :], twiddle_ref[1, a : a + 1, :]
        turned_re.append(re[a] * c + im[a] * s)
        turned_im.append(im[a] * c - re[a] * s)
    re, im = lane_product(turned_re, turned_im, lane_ref)
    decay, scale = decay_ref[...], scale_ref[...]
    group = sub_ids((SUBS, LANES)) // kept
    subs = sub_ids((SUBS, LANES))
    energy = jnp.zeros((SUBS, LANES), jnp.float32)
    for part, field in enumerate((re, im)):
        for a in range(radix):
            d, g = decay[a], scale[a]
            cell = [field[a][i] for i in range(inner)]
            ahead, behind = [cell[0]], [cell[-1]]
            for i in range(1, inner):
                ahead.append(cell[i] + d * ahead[-1])
                behind.append(cell[inner - 1 - i] + d * behind[-1])
            behind = behind[::-1]
            value = [ahead[i] + behind[i] - cell[i] for i in range(inner)]
            total = sum(cell[i] * value[i] for i in range(inner))
            last, first = ahead[-1], behind[0]
            from_low = jnp.zeros_like(last)
            from_high = jnp.zeros_like(first)
            low_weight, high_weight = jnp.ones_like(last), jnp.ones_like(first)
            bit = 1
            while bit < groups:
                upper = (group & bit) != 0
                step = bit * kept
                if 2 * step == SUBS:
                    other_last, other_first = turn(last, step), turn(first, step)
                else:
                    other_last = jnp.where(upper, turn(last, step), turn(last, -step))
                    other_first = jnp.where(upper, turn(first, step), turn(first, -step))
                span = power(d, inner * bit)
                joined = 2.0 * d * other_last * first
                total = total + jnp.where(upper & ((group & (bit - 1)) == 0), joined, 0.0)
                from_low = from_low + jnp.where(upper, low_weight * other_last, 0.0)
                from_high = from_high + jnp.where(upper, 0.0, high_weight * other_first)
                low_weight = low_weight * jnp.where(upper, span, 1.0)
                high_weight = high_weight * jnp.where(upper, 1.0, span)
                last = jnp.where(upper, last + span * other_last, other_last + span * last)
                first = jnp.where(upper, other_first + span * first, first + span * other_first)
                bit *= 2
            energy = energy + g * total
            message_ref[part * radix + a] = jnp.where(subs < HALF, last, first)
            for i in range(inner):
                spread = power(d, i + 1) * from_low + power(d, inner - i) * from_high
                local_ref[part, a, i] = value[i] + spread
    message_ref[2 * radix] = energy


def facing(level):
    low = sub_ids((SUBS, LANES)) < HALF
    right = lax.rem(lax.shift_right_logical(lax.axis_index("gz"), level), 2)
    return jnp.where(low, 1, 0) != right, right


def join(level, cells, groups, own, other, decay, scale):
    radix = decay.shape[0]
    kept = SUBS // groups
    outer, _ = facing(level)
    joined, couple = [], jnp.zeros((SUBS, LANES), jnp.float32)
    for i in range(2 * radix):
        d, g = decay[i % radix], scale[i % radix]
        span = power(d, cells << level)
        joined.append(jnp.where(outer, other[i] + span * own[i], own[i] + span * other[i]))
        couple = couple + (2.0 * g * d) * jnp.where(outer, own[i] * turn(other[i], HALF), 0.0)
    couple = couple + turn(couple, HALF)
    joined.append(own[-1] + other[-1] + jnp.where(sub_ids((SUBS, LANES)) < kept, couple, 0.0))
    return joined


def rows_of(ref):
    return [ref[i] for i in range(ref.shape[0])]


def join_kernel(level, cells, groups, own_ref, other_ref, decay_ref, scale_ref, out_ref, *edge_refs):
    joined = join(level, cells, groups, rows_of(own_ref), rows_of(other_ref), decay_ref[...], scale_ref[...])
    for i, value in enumerate(joined):
        out_ref[i] = value
    for edge_ref in edge_refs:
        edge_of(level + 1, cells, groups, joined, decay_ref, scale_ref, edge_ref)


def join_two_kernel(
    level, cells, groups, own_ref, near_ref, far_ref, cross_ref, decay_ref, scale_ref, out_ref, pair_ref, *edge_refs
):
    decay, scale = decay_ref[...], scale_ref[...]
    own = join(level, cells, groups, rows_of(own_ref), rows_of(near_ref), decay, scale)
    other = join(level, cells, groups, rows_of(far_ref), rows_of(cross_ref), decay, scale)
    joined = join(level + 1, cells, groups, own, other, decay, scale)
    for i in range(len(joined)):
        out_ref[i] = joined[i]
        pair_ref[i] = other[i]
    for edge_ref in edge_refs:
        edge_of(level + 2, cells, groups, joined, decay_ref, scale_ref, edge_ref)


def edge_of(level, cells, groups, moments, decay_ref, scale_ref, out_ref):
    radix = decay_ref.shape[0]
    kept = SUBS // groups
    subs = sub_ids((SUBS, LANES))
    outer, _ = facing(level)
    walls = jnp.zeros((SUBS, LANES), jnp.float32)
    for a in range(radix):
        d = decay_ref[a]
        image = power(d, (cells << level) + 1)
        both = []
        for part in range(2):
            own = moments[part * radix + a]
            near = jnp.where(outer, 0.0, own)
            walls = walls + (scale_ref[a] * d * d) * (near * near)
            sent = own - image * turn(own, HALF)
            both.append(jnp.where(outer, sent, turn(sent, HALF)))
        out_ref[a] = jnp.where(subs < HALF, both[0], both[1])
    out_ref[radix] = moments[2 * radix] - jnp.where(lax.rem(subs, HALF) < kept, walls, 0.0)


def to_planes(re, im, lane_ref, twiddle_ref):
    re, im = lane_product(re, im, lane_ref)
    turned_re, turned_im = [], []
    for a in range(len(re)):
        c, s = twiddle_ref[0, a : a + 1, :], twiddle_ref[1, a : a + 1, :]
        turned_re.append(re[a] * c - im[a] * s)
        turned_im.append(im[a] * c + re[a] * s)
    return small_dft(turned_re, turned_im, 1.0)


def local_kernel(groups, local_ref, scale_ref, lane_ref, twiddle_ref, *out_refs):
    radix = scale_ref.shape[0]
    rows = radix // groups
    fields = [[scale_ref[a] * local_ref[part, a] for a in range(radix)] for part in range(2)]
    for part, field in enumerate(to_planes(*fields, lane_ref, twiddle_ref)):
        for a in range(rows):
            pieces = [field[t * rows + a] for t in range(groups)]
            for ref, value in zip(out_refs, for_targets(pieces, lax.axis_index("gy"))):
                ref[part * rows + a] = value


def both_parts(packed):
    low = sub_ids((SUBS, LANES)) < HALF
    turned = turn(packed, HALF)
    return jnp.where(low, packed, turned), jnp.where(low, turned, packed)


def near_side_kernel(slabs, cells, *refs):
    levels = slabs.bit_length() - 1
    own_ref, first_ref, received = refs[0], refs[1], refs[2 : levels + 1]
    edge_ref, decay_ref, scale_ref, out_ref, mate_ref, factor_ref = refs[levels + 1 :]
    radix = decay_ref.shape[0]
    outers = [facing(level)[0] for level in range(levels)]
    for a in range(radix):
        d = decay_ref[a]
        spans = [power(d, cells)]
        for level in range(1, levels + 1):
            spans.append(spans[-1] * spans[-1])
        far = spans[levels] * d
        rest = 1.0 / (1.0 - far * far)
        facing_factor = jnp.where(outers[levels - 1], -spans[levels - 1] * d, 1.0) * rest
        parts = both_parts(edge_ref[a])
        for part in range(2):
            i = part * radix + a
            wall = jnp.where(outers[levels - 1], d * turn(own_ref[i], HALF), 0.0) + facing_factor * (far * parts[part])
            sides = [
                (jnp.where(outers[0], 0.0, received[0][i]), jnp.where(outers[0], 1.0, spans[0])),
                (jnp.where(outers[0], first_ref[i], 0.0), jnp.where(outers[0], spans[0], 1.0)),
            ]
            for side, (ref, (incoming, weight)) in enumerate(zip((out_ref, mate_ref), sides)):
                for level in range(1, levels - 1):
                    incoming = incoming + jnp.where(outers[level], 0.0, weight * received[level][i])
                    weight = weight * jnp.where(outers[level], 1.0, spans[level])
                ref[i] = incoming - weight * wall
                factor_ref[side * radix + a] = weight * facing_factor
        factor_ref[2 * radix + a] = scale_ref[a] * d * rest
        factor_ref[3 * radix + a] = far
    for ref in (out_ref, mate_ref):
        ref[2 * radix] = edge_ref[radix]


def entering_kernel(groups, slabs, edge_ref, other_ref, near_ref, near_mate_ref, factor_ref, out_ref, mate_ref):
    radix = edge_ref.shape[0] - 1
    right = facing(slabs.bit_length() - 2)[1] == 1
    couple = jnp.zeros((SUBS, LANES), jnp.float32)
    for a in range(radix):
        for part, (mine, theirs) in enumerate(zip(both_parts(edge_ref[a]), both_parts(other_ref[a]))):
            i = part * radix + a
            out_ref[i] = near_ref[i] + factor_ref[a] * theirs
            mate_ref[i] = near_mate_ref[i] + factor_ref[radix + a] * theirs
            left_value, right_value = jnp.where(right, theirs, mine), jnp.where(right, mine, theirs)
            squares = left_value * left_value + right_value * right_value
            joined = 2.0 * (left_value * right_value) - factor_ref[3 * radix + a] * squares
            couple = couple + factor_ref[2 * radix + a] * joined
    energy = edge_ref[radix] + other_ref[radix] + jnp.where(sub_ids((SUBS, LANES)) < SUBS // groups, couple, 0.0)
    out_ref[2 * radix] = energy
    mate_ref[2 * radix] = energy


def response(groups, inner, entering_ref, decay_ref, scale_ref, lane_ref, twiddle_ref):
    radix = decay_ref.shape[0]
    rows = radix // groups
    low = sub_ids((SUBS, LANES)) < HALF
    decay = decay_ref[...]
    ahead, behind = group_powers(decay, inner, groups, SUBS // groups)
    fields = ([], [])
    for part in range(2):
        for a in range(radix):
            d, incoming = decay[a], entering_ref[part * radix + a]
            turned = turn(incoming, HALF)
            from_low = scale_ref[a] * ahead[a] * jnp.where(low, incoming, turned)
            from_high = scale_ref[a] * behind[a] * jnp.where(low, turned, incoming)
            fields[part].append(
                jnp.stack([power(d, z + 1) * from_low + power(d, inner - z) * from_high for z in range(inner)])
            )
    planes = to_planes(*fields, lane_ref, twiddle_ref)
    me = lax.axis_index("gy")
    return [[for_targets([field[t * rows + a] for t in range(groups)], me)[0] for a in range(rows)] for field in planes]


def own_kernel(groups, entering_ref, decay_ref, scale_ref, lane_ref, twiddle_ref, local_ref, out_ref):
    rows, inner = local_ref.shape[0] // 2, local_ref.shape[1]
    field = response(groups, inner, entering_ref, decay_ref, scale_ref, lane_ref, twiddle_ref)
    for part in range(2):
        for a in range(rows):
            out_ref[part * rows + a] = field[part][a] + local_ref[part * rows + a]


def finish_kernel(groups, *refs):
    entering, parts = refs[:groups], refs[groups : 2 * groups]
    roots = refs[2 * groups : 4 * groups]
    lane_ref, twiddle_ref, weight_ref, previous_ref, rz_prev_ref = refs[4 * groups : 4 * groups + 5]
    out_ref, direction_ref, total_ref, out_buffer, direction_buffer, total_buffer, sems, total_sem = refs[4 * groups + 5 :]
    cells, _, waves, planes = out_buffer.shape
    kept, inner, rows = waves // groups, cells // groups, planes // LANES
    me = lax.axis_index("gy")
    block = sub_ids((SUBS, LANES)) // kept
    energies = by_source([ref[ref.shape[0] - 1] for ref in entering], me)
    total = jnp.sum(sum(energies[1:], energies[0]), axis=(0, 1), keepdims=True)
    total_buffer[...] = total
    copies = [pltpu.make_async_copy(total_buffer, total_ref, total_sem)]
    copies[0].start()
    ratio = total / rz_prev_ref[0]
    held = [[[parts[0][part * rows + a] for a in range(rows)] for part in range(2)]]
    for s in range(1, groups):
        field = response(groups, inner, entering[s], roots[2 * s], roots[2 * s + 1], lane_ref, twiddle_ref)
        held.append([[field[part][a] + parts[s][part * rows + a] for a in range(rows)] for part in range(2)])
    for zp in range(inner):
        for part in range(2):
            for a in range(rows):
                lanes = slice(a * LANES, (a + 1) * LANES)
                sources = by_source([fields[part][a][zp] for fields in held], me)
                for zg in range(groups):
                    z = zg * inner + zp
                    value = turn(sources[0], -zg * kept)
                    for t in range(1, groups):
                        value = jnp.where(block == t, turn(sources[t], (t - zg) * kept), value)
                    value = value * weight_ref[z : z + 1, lanes]
                    out_buffer[z, part, :, lanes] = value
                    direction_buffer[z, part, :, lanes] = value + ratio * previous_ref[z, part, :, lanes]
        for zg in range(groups):
            z = zg * inner + zp
            for i, (source, target) in enumerate(((out_buffer, out_ref), (direction_buffer, direction_ref))):
                copies.append(pltpu.make_async_copy(source.at[z], target.at[z], sems.at[i, z]))
                copies[-1].start()
    for copy in copies:
        copy.wait()


def float_array(*shape):
    return jax.ShapeDtypeStruct(shape, jnp.float32)


def held_array(*shape):
    return pltpu.VMEM(shape, jnp.float32)


def inside(value):
    return pltpu.with_memory_space_constraint(jnp.asarray(value), pltpu.VMEM)


def on_device(residual, direction_prev, phase_labels, phase_diffusivity, x_eigen, rz_prev):
    cells, parts, waves, planes = residual.shape
    groups, slabs = lax.axis_size("gy"), lax.axis_size("gz")
    levels = slabs.bit_length() - 1
    inner, rows = cells // groups, planes // LANES
    radix = rows * groups
    distances = [[(i, (i + s) % groups) for i in range(groups)] for s in range(1, groups)]

    weight, *pieces = pl.pallas_call(
        functools.partial(pack_kernel, groups),
        out_shape=[held_array(cells, planes)] + [held_array(parts, rows, inner, SUBS, LANES)] * groups,
        in_specs=[ANY] * 3,
        out_specs=[VMEM] * (groups + 1),
        scratch_shapes=[
            pltpu.VMEM(residual.shape, jnp.float32),
            pltpu.VMEM(phase_labels.shape, jnp.int32),
            pltpu.SMEM(phase_diffusivity.shape, jnp.float32),
            pltpu.SemaphoreType.DMA((cells,)),
            pltpu.SemaphoreType.DMA,
            pltpu.SemaphoreType.DMA,
        ],
        name="pack",
    )(residual, phase_labels, phase_diffusivity)
    held = [pieces[0]] + [lax.ppermute(x, "gy", d) for x, d in zip(pieces[1:], distances)]
    roots = pl.pallas_call(
        functools.partial(roots_kernel, groups),
        out_shape=[held_array(radix, SUBS, LANES)] * (2 * groups),
        in_specs=[VMEM, SMEM],
        out_specs=[VMEM] * (2 * groups),
        name="roots",
    )(inside(y_eigen(radix)), x_eigen)
    decay, scale = roots[:2]

    message, local = pl.pallas_call(
        functools.partial(forward_kernel, groups),
        out_shape=[
            held_array(parts * radix + 1, SUBS, LANES),
            held_array(parts, radix, inner, SUBS, LANES),
        ],
        in_specs=[VMEM] * (groups + 4),
        out_specs=[VMEM] * 2,
        name="forward",
    )(*map(inside, (*held, lane_transform(-1.0), twiddles(radix), decay, scale)))

    def swapped(value, bits):
        return lax.ppermute(value, "gz", [(i, i ^ bits) for i in range(slabs)])

    first, received, level = message, [], 0
    edge_shape = held_array(radix + 1, SUBS, LANES)
    while level < levels - 1:
        bit, cross = 1 << level, min(level, 1)
        near = swapped(message, bit | cross)
        received.append(near)
        if level == 0 or level == levels - 2:
            last = [edge_shape] if level == levels - 2 else []
            message, *edge = pl.pallas_call(
                functools.partial(join_kernel, level, cells, groups),
                out_shape=[held_array(*message.shape)] + last,
                in_specs=[VMEM] * 4,
                out_specs=[VMEM] * (1 + len(last)),
                name=f"join{level}",
            )(*map(inside, (message, near, decay, scale)))
            level += 1
        else:
            last = [edge_shape] if level == levels - 3 else []
            message, pair, *edge = pl.pallas_call(
                functools.partial(join_two_kernel, level, cells, groups),
                out_shape=[held_array(*message.shape)] * 2 + last,
                in_specs=[VMEM] * 6,
                out_specs=[VMEM] * (2 + len(last)),
                name=f"join{level}",
            )(*map(inside, (message, near, swapped(message, 2 * bit | 1), swapped(message, 3 * bit | 1), decay, scale)))
            received.append(pair)
            level += 2
    tables = (lane_transform(1.0), twiddles(radix))
    piece = held_array(parts * rows, inner, SUBS, LANES)
    pieces = pl.pallas_call(
        functools.partial(local_kernel, groups),
        out_shape=[piece] * groups,
        in_specs=[VMEM] * 4,
        out_specs=[VMEM] * groups,
        name="local",
    )(*map(inside, (local, scale, *tables)))
    held = [lax.ppermute(x, "gy", d) for x, d in zip(pieces[1:], distances)]

    other = swapped(edge[0], 1 << level | 1)
    near_side = pl.pallas_call(
        functools.partial(near_side_kernel, slabs, cells),
        out_shape=[held_array(*message.shape)] * 2 + [held_array(4 * radix, SUBS, LANES)],
        in_specs=[VMEM] * (levels + 4),
        out_specs=[VMEM] * 3,
        name="near_side",
    )(*map(inside, (message, first, *received, edge[0], decay, scale)))
    entering, mate = pl.pallas_call(
        functools.partial(entering_kernel, groups, slabs),
        out_shape=[held_array(*message.shape)] * 2,
        in_specs=[VMEM] * 5,
        out_specs=[VMEM] * 2,
        name="entering",
    )(*map(inside, (edge[0], other, *near_side)))
    crossed = [[(i * slabs + z, j * slabs + (z ^ 1)) for i, j in d for z in range(slabs)] for d in distances]
    entered = [entering] + [lax.ppermute(mate, ("gy", "gz"), d) for d in crossed]
    own = pl.pallas_call(
        functools.partial(own_kernel, groups),
        out_shape=piece,
        in_specs=[VMEM] * 6,
        out_specs=VMEM,
        name="own",
    )(*map(inside, (entering, decay, scale, *tables, pieces[0])))

    preconditioned, direction, total = pl.pallas_call(
        functools.partial(finish_kernel, groups),
        out_shape=[float_array(*residual.shape), float_array(*residual.shape), float_array(1, 1)],
        in_specs=[VMEM] * (4 * groups + 4) + [SMEM],
        out_specs=[ANY] * 3,
        scratch_shapes=[
            pltpu.VMEM(residual.shape, jnp.float32),
            pltpu.VMEM(residual.shape, jnp.float32),
            pltpu.VMEM((1, 1), jnp.float32),
            pltpu.SemaphoreType.DMA((2, cells)),
            pltpu.SemaphoreType.DMA,
        ],
        name="finish",
    )(*map(inside, (*entered, own, *held, *roots, *tables, weight, direction_prev)), rz_prev)
    return preconditioned, direction, jnp.reshape(total, (1,))


def solution(mesh):
    placed = (P("gz", None, None, "gy"), P("gz", None, None, "gy"), P("gz", "gy"), P(), P(), P())
    return jax.shard_map(
        on_device,
        mesh=mesh,
        in_specs=placed,
        out_specs=(P("gz", None, None, "gy"), P("gz", None, None, "gy"), P()),
        check_vma=False,
    )
```

```python
import functools

import jax
import jax.numpy as jnp
import numpy as np
from jax import lax
from jax.experimental import pallas as pl
from jax.experimental.pallas import tpu as pltpu
from jax.sharding import PartitionSpec as P

LANES = 128
SUBS = 8
HALF = 4
VMEM = pl.BlockSpec(memory_space=pltpu.VMEM)
SMEM = pl.BlockSpec(memory_space=pltpu.SMEM)
ANY = pl.BlockSpec(memory_space=pl.ANY)


def split_bf16(table):
    high = table.astype(jnp.bfloat16)
    low = (table - np.asarray(high, np.float64)).astype(jnp.bfloat16)
    return np.stack([np.asarray(high), np.asarray(low)])


def lane_transform(sign):
    ids = np.arange(LANES)
    angle = 2.0 * np.pi * (ids[:, None] * ids[None, :] % LANES) / LANES
    cosine, sine = np.cos(angle), sign * np.sin(angle)
    return split_bf16(np.block([[cosine, sine], [-sine, cosine]]))


def twiddles(radix):
    angle = 2.0 * np.pi * np.arange(radix)[:, None] * np.arange(LANES)[None, :] / (radix * LANES)
    return np.stack([np.cos(angle), np.sin(angle)]).astype(np.float32)


def y_eigen(radix):
    wave = np.arange(radix)[:, None] + radix * np.arange(LANES)[None, :]
    return (4.0 * np.sin(np.pi * wave / (radix * LANES)) ** 2).astype(np.float32)


def power(base, exponent):
    result = None
    while exponent:
        if exponent & 1:
            result = base if result is None else result * base
        exponent >>= 1
        if exponent:
            base = base * base
    return result


def small_dft(re, im, sign):
    count = len(re)
    if count == 1:
        return re, im
    even_re, even_im = small_dft(re[0::2], im[0::2], sign)
    odd_re, odd_im = small_dft(re[1::2], im[1::2], sign)
    out_re, out_im = [None] * count, [None] * count
    for i in range(count // 2):
        angle = 2.0 * np.pi * i / count
        c, s = float(np.cos(angle)), float(sign * np.sin(angle))
        if i == 0:
            a, b = odd_re[i], odd_im[i]
        elif 4 * i == count:
            a, b = (odd_im[i], -odd_re[i]) if sign < 0 else (-odd_im[i], odd_re[i])
        else:
            a = odd_re[i] * c - odd_im[i] * s
            b = odd_re[i] * s + odd_im[i] * c
        out_re[i], out_im[i] = even_re[i] + a, even_im[i] + b
        out_re[i + count // 2], out_im[i + count // 2] = even_re[i] - a, even_im[i] - b
    return out_re, out_im


def lane_product(re, im, table_ref):
    count, shape = len(re), re[0].shape
    rows = int(np.prod(shape[:-1]))
    flat = jnp.concatenate(
        [jnp.concatenate([a.reshape(rows, LANES), b.reshape(rows, LANES)], axis=1) for a, b in zip(re, im)],
        axis=0,
    )
    high = flat.astype(jnp.bfloat16)
    low = (flat - high.astype(jnp.float32)).astype(jnp.bfloat16)
    dot = functools.partial(jnp.dot, preferred_element_type=jnp.float32)
    out = dot(high, table_ref[0]) + (dot(low, table_ref[0]) + dot(high, table_ref[1]))
    out_re = [out[i * rows : (i + 1) * rows, :LANES].reshape(shape) for i in range(count)]
    out_im = [out[i * rows : (i + 1) * rows, LANES:].reshape(shape) for i in range(count)]
    return out_re, out_im


def sub_ids(shape):
    return lax.broadcasted_iota(jnp.int32, shape, len(shape) - 2)


def turn(value, shift):
    shift = shift % SUBS
    return value if shift == 0 else pltpu.roll(value, shift, value.ndim - 2)


def for_targets(pieces, me):
    peers = len(pieces)
    out = []
    for s in range(peers):
        chosen = pieces[0]
        for t in range(1, peers):
            chosen = jnp.where(lax.rem(me + s, peers) == t, pieces[t], chosen)
        out.append(chosen)
    return out


def by_source(held, me):
    peers = len(held)
    out = []
    for t in range(peers):
        chosen = held[0]
        for s in range(1, peers):
            chosen = jnp.where(lax.rem(me + (peers - t), peers) == s, held[s], chosen)
        out.append(chosen)
    return out


def cell_weight(labels, diffusivity_ref):
    weight = jnp.zeros(labels.shape, jnp.float32)
    for i in range(diffusivity_ref.shape[0]):
        value = lax.rsqrt(jnp.full(labels.shape, diffusivity_ref[i], jnp.float32))
        weight = jnp.where(labels == i, value, weight)
    return weight


def mode_roots(eigen_ref, y_eigen_ref, me, kept, length):
    radix = y_eigen_ref.shape[0]
    subs = sub_ids((SUBS, LANES))
    x_part = jnp.zeros((SUBS, LANES), jnp.float32)
    for i in range(kept):
        x_part = jnp.where(lax.rem(subs, kept) == i, eigen_ref[me * kept + i], x_part)
    half_shift = 0.5 * jnp.stack([x_part + y_eigen_ref[a : a + 1, :] for a in range(radix)])
    root = jnp.sqrt(half_shift * (half_shift + 2.0))
    return 1.0 / (1.0 + half_shift + root), (0.5 / length) / root


def group_powers(decay, cells, groups, kept):
    group = sub_ids((SUBS, LANES)) // kept
    ahead = jnp.ones_like(decay)
    behind = jnp.ones_like(decay)
    bit = 1
    while bit < groups:
        factor = power(decay, cells * bit)
        ahead = ahead * jnp.where((group & bit) != 0, factor, 1.0)
        behind = behind * jnp.where((group & bit) != 0, 1.0, factor)
        bit *= 2
    return ahead, behind


def pack_kernel(groups, residual_any, labels_any, diffusivity_any, weight_ref, *refs):
    out_refs, (residual_ref, labels_ref, diffusivity_ref, cell_sems, label_sem, value_sem) = refs[:groups], refs[groups:]
    values = pltpu.make_async_copy(diffusivity_any, diffusivity_ref, value_sem)
    labels = pltpu.make_async_copy(labels_any, labels_ref, label_sem)
    values.start()
    labels.start()
    arriving = [
        pltpu.make_async_copy(residual_any.at[z], residual_ref.at[z], cell_sems.at[z]) for z in range(residual_ref.shape[0])
    ]
    order = [zg * (len(arriving) // groups) + zp for zp in range(len(arriving) // groups) for zg in range(groups)]
    for z in order:
        arriving[z].start()
    values.wait()
    labels.wait()
    cells, _, waves, planes = residual_ref.shape
    kept, inner = waves // groups, cells // groups
    me = lax.axis_index("gy")
    group = sub_ids((SUBS, LANES)) // kept
    weight = cell_weight(labels_ref[...], diffusivity_ref)
    weight_ref[...] = weight
    for zp in range(inner):
        for zg in range(groups):
            arriving[zg * inner + zp].wait()
        for part in range(2):
            for a in range(planes // LANES):
                lanes = slice(a * LANES, (a + 1) * LANES)
                rows = [residual_ref[z, part, :, lanes] * weight[z : z + 1, lanes] for z in range(zp, cells, inner)]
                pieces = []
                for t in range(groups):
                    piece = turn(rows[0], -t * kept)
                    for zg in range(1, groups):
                        piece = jnp.where(group == zg, turn(rows[zg], (zg - t) * kept), piece)
                    pieces.append(piece)
                for ref, value in zip(out_refs, for_targets(pieces, me)):
                    ref[part, a, zp] = value


def roots_kernel(groups, y_eigen_ref, eigen_ref, *out_refs):
    length = y_eigen_ref.shape[0] * LANES
    for s in range(groups):
        device = lax.rem(lax.axis_index("gy") + groups - s, groups)
        decay, scale = mode_roots(eigen_ref, y_eigen_ref, device, SUBS // groups, length)
        out_refs[2 * s][...] = decay
        out_refs[2 * s + 1][...] = scale


def slab_scan(cell, d, groups):
    inner, kept = len(cell), SUBS // groups
    group = sub_ids((SUBS, LANES)) // kept
    ahead, behind = [cell[0]], [cell[-1]]
    for i in range(1, inner):
        ahead.append(cell[i] + d * ahead[-1])
        behind.append(cell[inner - 1 - i] + d * behind[-1])
    behind = behind[::-1]
    value = [ahead[i] + behind[i] - cell[i] for i in range(inner)]
    total = sum(cell[i] * value[i] for i in range(inner))
    last, first = ahead[-1], behind[0]
    from_low = jnp.zeros_like(last)
    from_high = jnp.zeros_like(first)
    low_weight, high_weight = jnp.ones_like(last), jnp.ones_like(first)
    bit = 1
    while bit < groups:
        upper = (group & bit) != 0
        step = bit * kept
        if 2 * step == SUBS:
            other_last, other_first = turn(last, step), turn(first, step)
        else:
            other_last = jnp.where(upper, turn(last, step), turn(last, -step))
            other_first = jnp.where(upper, turn(first, step), turn(first, -step))
        span = power(d, inner * bit)
        joined = 2.0 * d * other_last * first
        total = total + jnp.where(upper & ((group & (bit - 1)) == 0), joined, 0.0)
        from_low = from_low + jnp.where(upper, low_weight * other_last, 0.0)
        from_high = from_high + jnp.where(upper, 0.0, high_weight * other_first)
        low_weight = low_weight * jnp.where(upper, span, 1.0)
        high_weight = high_weight * jnp.where(upper, 1.0, span)
        last = jnp.where(upper, last + span * other_last, other_last + span * last)
        first = jnp.where(upper, other_first + span * first, first + span * other_first)
        bit *= 2
    return last, first, total, value, from_low, from_high


def forward_kernel(groups, *refs):
    held = refs[:groups]
    lane_ref, twiddle_ref, decay_ref, scale_ref = refs[groups : groups + 4]
    message_ref, local_ref = refs[groups + 4 :]
    _, block_rows, inner, _, _ = held[0].shape
    radix = block_rows * groups
    kept = SUBS // groups
    me = lax.axis_index("gy")
    re, im = [], []
    blocks = [by_source([ref[part] for ref in held], me) for part in range(2)]
    for t in range(groups):
        for a in range(block_rows):
            re.append(blocks[0][t][a])
            im.append(blocks[1][t][a])
    re, im = small_dft(re, im, -1.0)
    turned_re, turned_im = [], []
    for a in range(radix):
        c, s = twiddle_ref[0, a : a + 1, :], twiddle_ref[1, a : a + 1, :]
        turned_re.append(re[a] * c + im[a] * s)
        turned_im.append(im[a] * c - re[a] * s)
    re, im = lane_product(turned_re, turned_im, lane_ref)
    decay, scale = decay_ref[...], scale_ref[...]
    group = sub_ids((SUBS, LANES)) // kept
    subs = sub_ids((SUBS, LANES))
    energy = jnp.zeros((SUBS, LANES), jnp.float32)
    for part, field in enumerate((re, im)):
        for a in range(radix):
            d, g = decay[a], scale[a]
            cell = [field[a][i] for i in range(inner)]
            last, first, total, _, _, _ = slab_scan(cell, d, groups)
            energy = energy + g * total
            message_ref[part * radix + a] = jnp.where(subs < HALF, last, first)
            local_ref[part, a] = field[a]
    message_ref[2 * radix] = energy


def facing(level):
    low = sub_ids((SUBS, LANES)) < HALF
    right = lax.rem(lax.shift_right_logical(lax.axis_index("gz"), level), 2)
    return jnp.where(low, 1, 0) != right, right


def join(level, cells, groups, own, other, decay, scale):
    radix = decay.shape[0]
    kept = SUBS // groups
    outer, _ = facing(level)
    joined, couple = [], jnp.zeros((SUBS, LANES), jnp.float32)
    for i in range(2 * radix):
        d, g = decay[i % radix], scale[i % radix]
        span = power(d, cells << level)
        joined.append(jnp.where(outer, other[i] + span * own[i], own[i] + span * other[i]))
        couple = couple + (2.0 * g * d) * jnp.where(outer, own[i] * turn(other[i], HALF), 0.0)
    couple = couple + turn(couple, HALF)
    joined.append(own[-1] + other[-1] + jnp.where(sub_ids((SUBS, LANES)) < kept, couple, 0.0))
    return joined


def rows_of(ref):
    return [ref[i] for i in range(ref.shape[0])]


def join_kernel(level, cells, groups, own_ref, other_ref, decay_ref, scale_ref, out_ref, *edge_refs):
    joined = join(level, cells, groups, rows_of(own_ref), rows_of(other_ref), decay_ref[...], scale_ref[...])
    for i, value in enumerate(joined):
        out_ref[i] = value
    for edge_ref in edge_refs:
        edge_of(level + 1, cells, groups, joined, decay_ref, scale_ref, edge_ref)


def join_two_kernel(
    level, cells, groups, own_ref, near_ref, far_ref, cross_ref, decay_ref, scale_ref, out_ref, pair_ref, *edge_refs
):
    decay, scale = decay_ref[...], scale_ref[...]
    own = join(level, cells, groups, rows_of(own_ref), rows_of(near_ref), decay, scale)
    other = join(level, cells, groups, rows_of(far_ref), rows_of(cross_ref), decay, scale)
    joined = join(level + 1, cells, groups, own, other, decay, scale)
    for i in range(len(joined)):
        out_ref[i] = joined[i]
        pair_ref[i] = other[i]
    for edge_ref in edge_refs:
        edge_of(level + 2, cells, groups, joined, decay_ref, scale_ref, edge_ref)


def edge_of(level, cells, groups, moments, decay_ref, scale_ref, out_ref):
    radix = decay_ref.shape[0]
    kept = SUBS // groups
    subs = sub_ids((SUBS, LANES))
    outer, _ = facing(level)
    walls = jnp.zeros((SUBS, LANES), jnp.float32)
    for a in range(radix):
        d = decay_ref[a]
        image = power(d, (cells << level) + 1)
        both = []
        for part in range(2):
            own = moments[part * radix + a]
            near = jnp.where(outer, 0.0, own)
            walls = walls + (scale_ref[a] * d * d) * (near * near)
            sent = own - image * turn(own, HALF)
            both.append(jnp.where(outer, sent, turn(sent, HALF)))
        out_ref[a] = jnp.where(subs < HALF, both[0], both[1])
    out_ref[radix] = moments[2 * radix] - jnp.where(lax.rem(subs, HALF) < kept, walls, 0.0)


def to_planes(re, im, lane_ref, twiddle_ref):
    re, im = lane_product(re, im, lane_ref)
    turned_re, turned_im = [], []
    for a in range(len(re)):
        c, s = twiddle_ref[0, a : a + 1, :], twiddle_ref[1, a : a + 1, :]
        turned_re.append(re[a] * c - im[a] * s)
        turned_im.append(im[a] * c + re[a] * s)
    return small_dft(turned_re, turned_im, 1.0)


def local_kernel(groups, local_ref, decay_ref, scale_ref, lane_ref, twiddle_ref, *out_refs):
    radix = scale_ref.shape[0]
    rows = radix // groups
    inner = local_ref.shape[2]
    fields = ([], [])
    for part in range(2):
        for a in range(radix):
            d = decay_ref[a]
            _, _, _, value, from_low, from_high = slab_scan([local_ref[part, a, i] for i in range(inner)], d, groups)
            whole = [value[i] + power(d, i + 1) * from_low + power(d, inner - i) * from_high for i in range(inner)]
            fields[part].append(scale_ref[a] * jnp.stack(whole))
    for part, field in enumerate(to_planes(*fields, lane_ref, twiddle_ref)):
        for a in range(rows):
            pieces = [field[t * rows + a] for t in range(groups)]
            for ref, value in zip(out_refs, for_targets(pieces, lax.axis_index("gy"))):
                ref[part * rows + a] = value


def both_parts(packed):
    low = sub_ids((SUBS, LANES)) < HALF
    turned = turn(packed, HALF)
    return jnp.where(low, packed, turned), jnp.where(low, turned, packed)


def near_side_kernel(slabs, cells, *refs):
    levels = slabs.bit_length() - 1
    own_ref, first_ref, received = refs[0], refs[1], refs[2 : levels + 1]
    edge_ref, decay_ref, scale_ref, out_ref, mate_ref, factor_ref = refs[levels + 1 :]
    radix = decay_ref.shape[0]
    outers = [facing(level)[0] for level in range(levels)]
    for a in range(radix):
        d = decay_ref[a]
        spans = [power(d, cells)]
        for level in range(1, levels + 1):
            spans.append(spans[-1] * spans[-1])
        far = spans[levels] * d
        rest = 1.0 / (1.0 - far * far)
        facing_factor = jnp.where(outers[levels - 1], -spans[levels - 1] * d, 1.0) * rest
        parts = both_parts(edge_ref[a])
        for part in range(2):
            i = part * radix + a
            wall = jnp.where(outers[levels - 1], d * turn(own_ref[i], HALF), 0.0) + facing_factor * (far * parts[part])
            sides = [
                (jnp.where(outers[0], 0.0, received[0][i]), jnp.where(outers[0], 1.0, spans[0])),
                (jnp.where(outers[0], first_ref[i], 0.0), jnp.where(outers[0], spans[0], 1.0)),
            ]
            for side, (ref, (incoming, weight)) in enumerate(zip((out_ref, mate_ref), sides)):
                for level in range(1, levels - 1):
                    incoming = incoming + jnp.where(outers[level], 0.0, weight * received[level][i])
                    weight = weight * jnp.where(outers[level], 1.0, spans[level])
                ref[i] = incoming - weight * wall
                factor_ref[side * radix + a] = weight * facing_factor
        factor_ref[2 * radix + a] = scale_ref[a] * d * rest
        factor_ref[3 * radix + a] = far
    for ref in (out_ref, mate_ref):
        ref[2 * radix] = edge_ref[radix]


def entering_kernel(groups, slabs, edge_ref, other_ref, near_ref, near_mate_ref, factor_ref, out_ref, mate_ref):
    radix = edge_ref.shape[0] - 1
    right = facing(slabs.bit_length() - 2)[1] == 1
    couple = jnp.zeros((SUBS, LANES), jnp.float32)
    for a in range(radix):
        for part, (mine, theirs) in enumerate(zip(both_parts(edge_ref[a]), both_parts(other_ref[a]))):
            i = part * radix + a
            out_ref[i] = near_ref[i] + factor_ref[a] * theirs
            mate_ref[i] = near_mate_ref[i] + factor_ref[radix + a] * theirs
            left_value, right_value = jnp.where(right, theirs, mine), jnp.where(right, mine, theirs)
            squares = left_value * left_value + right_value * right_value
            joined = 2.0 * (left_value * right_value) - factor_ref[3 * radix + a] * squares
            couple = couple + factor_ref[2 * radix + a] * joined
    energy = edge_ref[radix] + other_ref[radix] + jnp.where(sub_ids((SUBS, LANES)) < SUBS // groups, couple, 0.0)
    out_ref[2 * radix] = energy
    mate_ref[2 * radix] = energy


def response(groups, inner, entering_ref, decay_ref, scale_ref, lane_ref, twiddle_ref):
    radix = decay_ref.shape[0]
    rows = radix // groups
    low = sub_ids((SUBS, LANES)) < HALF
    decay = decay_ref[...]
    ahead, behind = group_powers(decay, inner, groups, SUBS // groups)
    fields = ([], [])
    for part in range(2):
        for a in range(radix):
            d, incoming = decay[a], entering_ref[part * radix + a]
            turned = turn(incoming, HALF)
            from_low = scale_ref[a] * ahead[a] * jnp.where(low, incoming, turned)
            from_high = scale_ref[a] * behind[a] * jnp.where(low, turned, incoming)
            fields[part].append(
                jnp.stack([power(d, z + 1) * from_low + power(d, inner - z) * from_high for z in range(inner)])
            )
    planes = to_planes(*fields, lane_ref, twiddle_ref)
    me = lax.axis_index("gy")
    return [[for_targets([field[t * rows + a] for t in range(groups)], me)[0] for a in range(rows)] for field in planes]


def own_kernel(groups, entering_ref, decay_ref, scale_ref, lane_ref, twiddle_ref, local_ref, out_ref):
    rows, inner = local_ref.shape[0] // 2, local_ref.shape[1]
    field = response(groups, inner, entering_ref, decay_ref, scale_ref, lane_ref, twiddle_ref)
    for part in range(2):
        for a in range(rows):
            out_ref[part * rows + a] = field[part][a] + local_ref[part * rows + a]


def finish_kernel(groups, *refs):
    entering, parts = refs[:groups], refs[groups : 2 * groups]
    roots = refs[2 * groups : 4 * groups]
    lane_ref, twiddle_ref, weight_ref, previous_ref, rz_prev_ref = refs[4 * groups : 4 * groups + 5]
    out_ref, direction_ref, total_ref, out_buffer, direction_buffer, total_buffer, sems, total_sem = refs[4 * groups + 5 :]
    cells, _, waves, planes = out_buffer.shape
    kept, inner, rows = waves // groups, cells // groups, planes // LANES
    me = lax.axis_index("gy")
    block = sub_ids((SUBS, LANES)) // kept
    energies = by_source([ref[ref.shape[0] - 1] for ref in entering], me)
    total = jnp.sum(sum(energies[1:], energies[0]), axis=(0, 1), keepdims=True)
    total_buffer[...] = total
    copies = [pltpu.make_async_copy(total_buffer, total_ref, total_sem)]
    copies[0].start()
    ratio = total / rz_prev_ref[0]
    held = [[[parts[0][part * rows + a] for a in range(rows)] for part in range(2)]]
    for s in range(1, groups):
        field = response(groups, inner, entering[s], roots[2 * s], roots[2 * s + 1], lane_ref, twiddle_ref)
        held.append([[field[part][a] + parts[s][part * rows + a] for a in range(rows)] for part in range(2)])
    for zp in range(inner):
        for part in range(2):
            for a in range(rows):
                lanes = slice(a * LANES, (a + 1) * LANES)
                sources = by_source([fields[part][a][zp] for fields in held], me)
                for zg in range(groups):
                    z = zg * inner + zp
                    value = turn(sources[0], -zg * kept)
                    for t in range(1, groups):
                        value = jnp.where(block == t, turn(sources[t], (t - zg) * kept), value)
                    value = value * weight_ref[z : z + 1, lanes]
                    out_buffer[z, part, :, lanes] = value
                    direction_buffer[z, part, :, lanes] = value + ratio * previous_ref[z, part, :, lanes]
        for zg in range(groups):
            z = zg * inner + zp
            for i, (source, target) in enumerate(((out_buffer, out_ref), (direction_buffer, direction_ref))):
                copies.append(pltpu.make_async_copy(source.at[z], target.at[z], sems.at[i, z]))
                copies[-1].start()
    for copy in copies:
        copy.wait()


def float_array(*shape):
    return jax.ShapeDtypeStruct(shape, jnp.float32)


def held_array(*shape):
    return pltpu.VMEM(shape, jnp.float32)


def inside(value):
    return pltpu.with_memory_space_constraint(jnp.asarray(value), pltpu.VMEM)


def on_device(residual, direction_prev, phase_labels, phase_diffusivity, x_eigen, rz_prev):
    cells, parts, waves, planes = residual.shape
    groups, slabs = lax.axis_size("gy"), lax.axis_size("gz")
    levels = slabs.bit_length() - 1
    inner, rows = cells // groups, planes // LANES
    radix = rows * groups
    distances = [[(i, (i + s) % groups) for i in range(groups)] for s in range(1, groups)]

    weight, *pieces = pl.pallas_call(
        functools.partial(pack_kernel, groups),
        out_shape=[held_array(cells, planes)] + [held_array(parts, rows, inner, SUBS, LANES)] * groups,
        in_specs=[ANY] * 3,
        out_specs=[VMEM] * (groups + 1),
        scratch_shapes=[
            pltpu.VMEM(residual.shape, jnp.float32),
            pltpu.VMEM(phase_labels.shape, jnp.int32),
            pltpu.SMEM(phase_diffusivity.shape, jnp.float32),
            pltpu.SemaphoreType.DMA((cells,)),
            pltpu.SemaphoreType.DMA,
            pltpu.SemaphoreType.DMA,
        ],
        name="pack",
    )(residual, phase_labels, phase_diffusivity)
    held = [pieces[0]] + [lax.ppermute(x, "gy", d) for x, d in zip(pieces[1:], distances)]
    roots = pl.pallas_call(
        functools.partial(roots_kernel, groups),
        out_shape=[held_array(radix, SUBS, LANES)] * (2 * groups),
        in_specs=[VMEM, SMEM],
        out_specs=[VMEM] * (2 * groups),
        name="roots",
    )(inside(y_eigen(radix)), x_eigen)
    decay, scale = roots[:2]

    message, local = pl.pallas_call(
        functools.partial(forward_kernel, groups),
        out_shape=[
            held_array(parts * radix + 1, SUBS, LANES),
            held_array(parts, radix, inner, SUBS, LANES),
        ],
        in_specs=[VMEM] * (groups + 4),
        out_specs=[VMEM] * 2,
        name="forward",
    )(*map(inside, (*held, lane_transform(-1.0), twiddles(radix), decay, scale)))

    def swapped(value, bits):
        return lax.ppermute(value, "gz", [(i, i ^ bits) for i in range(slabs)])

    first, received, level = message, [], 0
    edge_shape = held_array(radix + 1, SUBS, LANES)
    while level < levels - 1:
        bit, cross = 1 << level, min(level, 1)
        near = swapped(message, bit | cross)
        received.append(near)
        if level == 0 or level == levels - 2:
            last = [edge_shape] if level == levels - 2 else []
            message, *edge = pl.pallas_call(
                functools.partial(join_kernel, level, cells, groups),
                out_shape=[held_array(*message.shape)] + last,
                in_specs=[VMEM] * 4,
                out_specs=[VMEM] * (1 + len(last)),
                name=f"join{level}",
            )(*map(inside, (message, near, decay, scale)))
            level += 1
        else:
            last = [edge_shape] if level == levels - 3 else []
            message, pair, *edge = pl.pallas_call(
                functools.partial(join_two_kernel, level, cells, groups),
                out_shape=[held_array(*message.shape)] * 2 + last,
                in_specs=[VMEM] * 6,
                out_specs=[VMEM] * (2 + len(last)),
                name=f"join{level}",
            )(*map(inside, (message, near, swapped(message, 2 * bit | 1), swapped(message, 3 * bit | 1), decay, scale)))
            received.append(pair)
            level += 2
    tables = (lane_transform(1.0), twiddles(radix))
    piece = held_array(parts * rows, inner, SUBS, LANES)
    pieces = pl.pallas_call(
        functools.partial(local_kernel, groups),
        out_shape=[piece] * groups,
        in_specs=[VMEM] * 5,
        out_specs=[VMEM] * groups,
        name="local",
    )(*map(inside, (local, decay, scale, *tables)))
    held = [lax.ppermute(x, "gy", d) for x, d in zip(pieces[1:], distances)]

    other = swapped(edge[0], 1 << level | 1)
    near_side = pl.pallas_call(
        functools.partial(near_side_kernel, slabs, cells),
        out_shape=[held_array(*message.shape)] * 2 + [held_array(4 * radix, SUBS, LANES)],
        in_specs=[VMEM] * (levels + 4),
        out_specs=[VMEM] * 3,
        name="near_side",
    )(*map(inside, (message, first, *received, edge[0], decay, scale)))
    entering, mate = pl.pallas_call(
        functools.partial(entering_kernel, groups, slabs),
        out_shape=[held_array(*message.shape)] * 2,
        in_specs=[VMEM] * 5,
        out_specs=[VMEM] * 2,
        name="entering",
    )(*map(inside, (edge[0], other, *near_side)))
    crossed = [[(i * slabs + z, j * slabs + (z ^ 1)) for i, j in d for z in range(slabs)] for d in distances]
    entered = [entering] + [lax.ppermute(mate, ("gy", "gz"), d) for d in crossed]
    own = pl.pallas_call(
        functools.partial(own_kernel, groups),
        out_shape=piece,
        in_specs=[VMEM] * 6,
        out_specs=VMEM,
        name="own",
    )(*map(inside, (entering, decay, scale, *tables, pieces[0])))

    preconditioned, direction, total = pl.pallas_call(
        functools.partial(finish_kernel, groups),
        out_shape=[float_array(*residual.shape), float_array(*residual.shape), float_array(1, 1)],
        in_specs=[VMEM] * (4 * groups + 4) + [SMEM],
        out_specs=[ANY] * 3,
        scratch_shapes=[
            pltpu.VMEM(residual.shape, jnp.float32),
            pltpu.VMEM(residual.shape, jnp.float32),
            pltpu.VMEM((1, 1), jnp.float32),
            pltpu.SemaphoreType.DMA((2, cells)),
            pltpu.SemaphoreType.DMA,
        ],
        name="finish",
    )(*map(inside, (*entered, own, *held, *roots, *tables, weight, direction_prev)), rz_prev)
    return preconditioned, direction, jnp.reshape(total, (1,))


def solution(mesh):
    placed = (P("gz", None, None, "gy"), P("gz", None, None, "gy"), P("gz", "gy"), P(), P(), P())
    return jax.shard_map(
        on_device,
        mesh=mesh,
        in_specs=placed,
        out_specs=(P("gz", None, None, "gy"), P("gz", None, None, "gy"), P()),
        check_vma=False,
    )
```

```python
import functools

import jax
import jax.numpy as jnp
import numpy as np
from jax import lax
from jax.experimental import pallas as pl
from jax.experimental.pallas import tpu as pltpu
from jax.sharding import PartitionSpec as P

LANES = 128
SUBS = 8
HALF = 4
VMEM = pl.BlockSpec(memory_space=pltpu.VMEM)
SMEM = pl.BlockSpec(memory_space=pltpu.SMEM)
ANY = pl.BlockSpec(memory_space=pl.ANY)


def split_bf16(table):
    high = table.astype(jnp.bfloat16)
    low = (table - np.asarray(high, np.float64)).astype(jnp.bfloat16)
    return np.stack([np.asarray(high), np.asarray(low)])


def lane_transform(sign):
    ids = np.arange(LANES)
    angle = 2.0 * np.pi * (ids[:, None] * ids[None, :] % LANES) / LANES
    cosine, sine = np.cos(angle), sign * np.sin(angle)
    return split_bf16(np.block([[cosine, sine], [-sine, cosine]]))


def twiddles(radix):
    angle = 2.0 * np.pi * np.arange(radix)[:, None] * np.arange(LANES)[None, :] / (radix * LANES)
    return np.stack([np.cos(angle), np.sin(angle)]).astype(np.float32)


def y_eigen(radix):
    wave = np.arange(radix)[:, None] + radix * np.arange(LANES)[None, :]
    return (4.0 * np.sin(np.pi * wave / (radix * LANES)) ** 2).astype(np.float32)


def power(base, exponent):
    result = None
    while exponent:
        if exponent & 1:
            result = base if result is None else result * base
        exponent >>= 1
        if exponent:
            base = base * base
    return result


def small_dft(re, im, sign):
    count = len(re)
    if count == 1:
        return re, im
    even_re, even_im = small_dft(re[0::2], im[0::2], sign)
    odd_re, odd_im = small_dft(re[1::2], im[1::2], sign)
    out_re, out_im = [None] * count, [None] * count
    for i in range(count // 2):
        angle = 2.0 * np.pi * i / count
        c, s = float(np.cos(angle)), float(sign * np.sin(angle))
        if i == 0:
            a, b = odd_re[i], odd_im[i]
        elif 4 * i == count:
            a, b = (odd_im[i], -odd_re[i]) if sign < 0 else (-odd_im[i], odd_re[i])
        else:
            a = odd_re[i] * c - odd_im[i] * s
            b = odd_re[i] * s + odd_im[i] * c
        out_re[i], out_im[i] = even_re[i] + a, even_im[i] + b
        out_re[i + count // 2], out_im[i + count // 2] = even_re[i] - a, even_im[i] - b
    return out_re, out_im


def lane_product(re, im, table_ref):
    count, shape = len(re), re[0].shape
    rows = int(np.prod(shape[:-1]))
    flat = jnp.concatenate(
        [jnp.concatenate([a.reshape(rows, LANES), b.reshape(rows, LANES)], axis=1) for a, b in zip(re, im)],
        axis=0,
    )
    high = flat.astype(jnp.bfloat16)
    low = (flat - high.astype(jnp.float32)).astype(jnp.bfloat16)
    dot = functools.partial(jnp.dot, preferred_element_type=jnp.float32)
    out = dot(high, table_ref[0]) + (dot(low, table_ref[0]) + dot(high, table_ref[1]))
    out_re = [out[i * rows : (i + 1) * rows, :LANES].reshape(shape) for i in range(count)]
    out_im = [out[i * rows : (i + 1) * rows, LANES:].reshape(shape) for i in range(count)]
    return out_re, out_im


def sub_ids(shape):
    return lax.broadcasted_iota(jnp.int32, shape, len(shape) - 2)


def turn(value, shift):
    shift = shift % SUBS
    return value if shift == 0 else pltpu.roll(value, shift, value.ndim - 2)


def for_targets(pieces, me):
    peers = len(pieces)
    out = []
    for s in range(peers):
        chosen = pieces[0]
        for t in range(1, peers):
            chosen = jnp.where(lax.rem(me + s, peers) == t, pieces[t], chosen)
        out.append(chosen)
    return out


def by_source(held, me):
    peers = len(held)
    out = []
    for t in range(peers):
        chosen = held[0]
        for s in range(1, peers):
            chosen = jnp.where(lax.rem(me + (peers - t), peers) == s, held[s], chosen)
        out.append(chosen)
    return out


def cell_weight(labels, diffusivity_ref):
    weight = jnp.zeros(labels.shape, jnp.float32)
    for i in range(diffusivity_ref.shape[0]):
        value = lax.rsqrt(jnp.full(labels.shape, diffusivity_ref[i], jnp.float32))
        weight = jnp.where(labels == i, value, weight)
    return weight


def mode_roots(eigen_ref, y_eigen_ref, me, kept, length):
    radix = y_eigen_ref.shape[0]
    subs = sub_ids((SUBS, LANES))
    x_part = jnp.zeros((SUBS, LANES), jnp.float32)
    for i in range(kept):
        x_part = jnp.where(lax.rem(subs, kept) == i, eigen_ref[me * kept + i], x_part)
    half_shift = 0.5 * jnp.stack([x_part + y_eigen_ref[a : a + 1, :] for a in range(radix)])
    root = jnp.sqrt(half_shift * (half_shift + 2.0))
    return 1.0 / (1.0 + half_shift + root), (0.5 / length) / root


def group_powers(decay, cells, groups, kept):
    group = sub_ids((SUBS, LANES)) // kept
    ahead = jnp.ones_like(decay)
    behind = jnp.ones_like(decay)
    bit = 1
    while bit < groups:
        factor = power(decay, cells * bit)
        ahead = ahead * jnp.where((group & bit) != 0, factor, 1.0)
        behind = behind * jnp.where((group & bit) != 0, 1.0, factor)
        bit *= 2
    return ahead, behind


def pack_kernel(groups, residual_any, labels_any, diffusivity_any, weight_ref, *refs):
    out_refs, (residual_ref, labels_ref, diffusivity_ref, cell_sems, label_sem, value_sem) = refs[:groups], refs[groups:]
    values = pltpu.make_async_copy(diffusivity_any, diffusivity_ref, value_sem)
    labels = pltpu.make_async_copy(labels_any, labels_ref, label_sem)
    values.start()
    labels.start()
    arriving = [
        pltpu.make_async_copy(residual_any.at[z], residual_ref.at[z], cell_sems.at[z]) for z in range(residual_ref.shape[0])
    ]
    order = [zg * (len(arriving) // groups) + zp for zp in range(len(arriving) // groups) for zg in range(groups)]
    for z in order:
        arriving[z].start()
    values.wait()
    labels.wait()
    cells, _, waves, planes = residual_ref.shape
    kept, inner = waves // groups, cells // groups
    me = lax.axis_index("gy")
    group = sub_ids((SUBS, LANES)) // kept
    weight = cell_weight(labels_ref[...], diffusivity_ref)
    weight_ref[...] = weight
    for zp in range(inner):
        for zg in range(groups):
            arriving[zg * inner + zp].wait()
        for part in range(2):
            for a in range(planes // LANES):
                lanes = slice(a * LANES, (a + 1) * LANES)
                rows = [residual_ref[z, part, :, lanes] * weight[z : z + 1, lanes] for z in range(zp, cells, inner)]
                pieces = []
                for t in range(groups):
                    piece = turn(rows[0], -t * kept)
                    for zg in range(1, groups):
                        piece = jnp.where(group == zg, turn(rows[zg], (zg - t) * kept), piece)
                    pieces.append(piece)
                for ref, value in zip(out_refs, for_targets(pieces, me)):
                    ref[part, a, zp] = value


def roots_kernel(groups, y_eigen_ref, eigen_ref, *out_refs):
    length = y_eigen_ref.shape[0] * LANES
    for s in range(groups):
        device = lax.rem(lax.axis_index("gy") + groups - s, groups)
        decay, scale = mode_roots(eigen_ref, y_eigen_ref, device, SUBS // groups, length)
        out_refs[2 * s][...] = decay
        out_refs[2 * s + 1][...] = scale


def slab_scan(cell, d, groups):
    inner, kept = len(cell), SUBS // groups
    group = sub_ids((SUBS, LANES)) // kept
    ahead, behind = [cell[0]], [cell[-1]]
    for i in range(1, inner):
        ahead.append(cell[i] + d * ahead[-1])
        behind.append(cell[inner - 1 - i] + d * behind[-1])
    behind = behind[::-1]
    value = [ahead[i] + behind[i] - cell[i] for i in range(inner)]
    total = sum(cell[i] * value[i] for i in range(inner))
    last, first = ahead[-1], behind[0]
    from_low = jnp.zeros_like(last)
    from_high = jnp.zeros_like(first)
    low_weight, high_weight = jnp.ones_like(last), jnp.ones_like(first)
    bit = 1
    while bit < groups:
        upper = (group & bit) != 0
        step = bit * kept
        if 2 * step == SUBS:
            other_last, other_first = turn(last, step), turn(first, step)
        else:
            other_last = jnp.where(upper, turn(last, step), turn(last, -step))
            other_first = jnp.where(upper, turn(first, step), turn(first, -step))
        span = power(d, inner * bit)
        joined = 2.0 * d * other_last * first
        total = total + jnp.where(upper & ((group & (bit - 1)) == 0), joined, 0.0)
        from_low = from_low + jnp.where(upper, low_weight * other_last, 0.0)
        from_high = from_high + jnp.where(upper, 0.0, high_weight * other_first)
        low_weight = low_weight * jnp.where(upper, span, 1.0)
        high_weight = high_weight * jnp.where(upper, 1.0, span)
        last = jnp.where(upper, last + span * other_last, other_last + span * last)
        first = jnp.where(upper, other_first + span * first, first + span * other_first)
        bit *= 2
    return last, first, total, value, from_low, from_high


def forward_kernel(groups, *refs):
    held = refs[:groups]
    lane_ref, twiddle_ref, decay_ref, scale_ref = refs[groups : groups + 4]
    message_ref, local_ref = refs[groups + 4 :]
    _, block_rows, inner, _, _ = held[0].shape
    radix = block_rows * groups
    kept = SUBS // groups
    me = lax.axis_index("gy")
    re, im = [], []
    blocks = [by_source([ref[part] for ref in held], me) for part in range(2)]
    for t in range(groups):
        for a in range(block_rows):
            re.append(blocks[0][t][a])
            im.append(blocks[1][t][a])
    re, im = small_dft(re, im, -1.0)
    turned_re, turned_im = [], []
    for a in range(radix):
        c, s = twiddle_ref[0, a : a + 1, :], twiddle_ref[1, a : a + 1, :]
        turned_re.append(re[a] * c + im[a] * s)
        turned_im.append(im[a] * c - re[a] * s)
    re, im = lane_product(turned_re, turned_im, lane_ref)
    decay, scale = decay_ref[...], scale_ref[...]
    group = sub_ids((SUBS, LANES)) // kept
    subs = sub_ids((SUBS, LANES))
    energy = jnp.zeros((SUBS, LANES), jnp.float32)
    for part, field in enumerate((re, im)):
        for a in range(radix):
            d, g = decay[a], scale[a]
            cell = [field[a][i] for i in range(inner)]
            last, first, total, _, _, _ = slab_scan(cell, d, groups)
            energy = energy + g * total
            message_ref[part * radix + a] = jnp.where(subs < HALF, last, first)
            local_ref[part, a] = field[a]
    message_ref[2 * radix] = energy


def facing(level):
    low = sub_ids((SUBS, LANES)) < HALF
    right = lax.rem(lax.shift_right_logical(lax.axis_index("gz"), level), 2)
    return jnp.where(low, 1, 0) != right, right


def join(level, cells, groups, own, other, decay, scale):
    radix = decay.shape[0]
    kept = SUBS // groups
    outer, _ = facing(level)
    joined, couple = [], jnp.zeros((SUBS, LANES), jnp.float32)
    for i in range(2 * radix):
        d, g = decay[i % radix], scale[i % radix]
        span = power(d, cells << level)
        joined.append(jnp.where(outer, other[i] + span * own[i], own[i] + span * other[i]))
        couple = couple + (2.0 * g * d) * jnp.where(outer, own[i] * turn(other[i], HALF), 0.0)
    couple = couple + turn(couple, HALF)
    joined.append(own[-1] + other[-1] + jnp.where(sub_ids((SUBS, LANES)) < kept, couple, 0.0))
    return joined


def rows_of(ref):
    return [ref[i] for i in range(ref.shape[0])]


def join_kernel(level, cells, groups, own_ref, other_ref, decay_ref, scale_ref, out_ref, *edge_refs):
    joined = join(level, cells, groups, rows_of(own_ref), rows_of(other_ref), decay_ref[...], scale_ref[...])
    for i, value in enumerate(joined):
        out_ref[i] = value
    for edge_ref in edge_refs:
        edge_of(level + 1, cells, groups, joined, decay_ref, scale_ref, edge_ref)


def join_two_kernel(
    level, cells, groups, own_ref, near_ref, far_ref, cross_ref, decay_ref, scale_ref, out_ref, pair_ref, *edge_refs
):
    decay, scale = decay_ref[...], scale_ref[...]
    own = join(level, cells, groups, rows_of(own_ref), rows_of(near_ref), decay, scale)
    other = join(level, cells, groups, rows_of(far_ref), rows_of(cross_ref), decay, scale)
    joined = join(level + 1, cells, groups, own, other, decay, scale)
    for i in range(len(joined)):
        out_ref[i] = joined[i]
        pair_ref[i] = other[i]
    for edge_ref in edge_refs:
        edge_of(level + 2, cells, groups, joined, decay_ref, scale_ref, edge_ref)


def edge_of(level, cells, groups, moments, decay_ref, scale_ref, out_ref):
    radix = decay_ref.shape[0]
    kept = SUBS // groups
    subs = sub_ids((SUBS, LANES))
    outer, _ = facing(level)
    walls = jnp.zeros((SUBS, LANES), jnp.float32)
    for a in range(radix):
        d = decay_ref[a]
        image = power(d, (cells << level) + 1)
        both = []
        for part in range(2):
            own = moments[part * radix + a]
            near = jnp.where(outer, 0.0, own)
            walls = walls + (scale_ref[a] * d * d) * (near * near)
            sent = own - image * turn(own, HALF)
            both.append(jnp.where(outer, sent, turn(sent, HALF)))
        out_ref[a] = jnp.where(subs < HALF, both[0], both[1])
    out_ref[radix] = moments[2 * radix] - jnp.where(lax.rem(subs, HALF) < kept, walls, 0.0)


def to_planes(re, im, twiddle_ref):
    turned_re, turned_im = [], []
    for a in range(len(re)):
        c, s = twiddle_ref[0, a : a + 1, :], twiddle_ref[1, a : a + 1, :]
        turned_re.append(re[a] * c - im[a] * s)
        turned_im.append(im[a] * c + re[a] * s)
    return small_dft(turned_re, turned_im, 1.0)


def local_kernel(groups, local_ref, decay_ref, scale_ref, lane_ref, twiddle_ref, *out_refs):
    radix = scale_ref.shape[0]
    rows = radix // groups
    inner = local_ref.shape[2]
    fields = ([], [])
    for part in range(2):
        for a in range(radix):
            d = decay_ref[a]
            _, _, _, value, from_low, from_high = slab_scan([local_ref[part, a, i] for i in range(inner)], d, groups)
            whole = [value[i] + power(d, i + 1) * from_low + power(d, inner - i) * from_high for i in range(inner)]
            fields[part].append(scale_ref[a] * jnp.stack(whole))
    for part, field in enumerate(to_planes(*lane_product(*fields, lane_ref), twiddle_ref)):
        for a in range(rows):
            pieces = [field[t * rows + a] for t in range(groups)]
            for ref, value in zip(out_refs, for_targets(pieces, lax.axis_index("gy"))):
                ref[part * rows + a] = value


def both_parts(packed):
    low = sub_ids((SUBS, LANES)) < HALF
    turned = turn(packed, HALF)
    return jnp.where(low, packed, turned), jnp.where(low, turned, packed)


def near_side_kernel(slabs, cells, *refs):
    levels = slabs.bit_length() - 1
    own_ref, first_ref, received = refs[0], refs[1], refs[2 : levels + 1]
    edge_ref, decay_ref, scale_ref, out_ref, mate_ref, factor_ref = refs[levels + 1 :]
    radix = decay_ref.shape[0]
    outers = [facing(level)[0] for level in range(levels)]
    for a in range(radix):
        d = decay_ref[a]
        spans = [power(d, cells)]
        for level in range(1, levels + 1):
            spans.append(spans[-1] * spans[-1])
        far = spans[levels] * d
        rest = 1.0 / (1.0 - far * far)
        facing_factor = jnp.where(outers[levels - 1], -spans[levels - 1] * d, 1.0) * rest
        parts = both_parts(edge_ref[a])
        for part in range(2):
            i = part * radix + a
            wall = jnp.where(outers[levels - 1], d * turn(own_ref[i], HALF), 0.0) + facing_factor * (far * parts[part])
            sides = [
                (jnp.where(outers[0], 0.0, received[0][i]), jnp.where(outers[0], 1.0, spans[0])),
                (jnp.where(outers[0], first_ref[i], 0.0), jnp.where(outers[0], spans[0], 1.0)),
            ]
            for side, (ref, (incoming, weight)) in enumerate(zip((out_ref, mate_ref), sides)):
                for level in range(1, levels - 1):
                    incoming = incoming + jnp.where(outers[level], 0.0, weight * received[level][i])
                    weight = weight * jnp.where(outers[level], 1.0, spans[level])
                ref[i] = incoming - weight * wall
                factor_ref[side * radix + a] = weight * facing_factor
        factor_ref[2 * radix + a] = scale_ref[a] * d * rest
        factor_ref[3 * radix + a] = far
    for ref in (out_ref, mate_ref):
        ref[2 * radix] = edge_ref[radix]


def entering_kernel(groups, slabs, edge_ref, other_ref, near_ref, near_mate_ref, factor_ref, out_ref, mate_ref):
    radix = edge_ref.shape[0] - 1
    right = facing(slabs.bit_length() - 2)[1] == 1
    couple = jnp.zeros((SUBS, LANES), jnp.float32)
    for a in range(radix):
        for part, (mine, theirs) in enumerate(zip(both_parts(edge_ref[a]), both_parts(other_ref[a]))):
            i = part * radix + a
            out_ref[i] = near_ref[i] + factor_ref[a] * theirs
            mate_ref[i] = near_mate_ref[i] + factor_ref[radix + a] * theirs
            left_value, right_value = jnp.where(right, theirs, mine), jnp.where(right, mine, theirs)
            squares = left_value * left_value + right_value * right_value
            joined = 2.0 * (left_value * right_value) - factor_ref[3 * radix + a] * squares
            couple = couple + factor_ref[2 * radix + a] * joined
    energy = edge_ref[radix] + other_ref[radix] + jnp.where(sub_ids((SUBS, LANES)) < SUBS // groups, couple, 0.0)
    out_ref[2 * radix] = energy
    mate_ref[2 * radix] = energy


def response(groups, inner, entering_ref, decay_ref, scale_ref, lane_ref):
    radix = decay_ref.shape[0]
    low = sub_ids((SUBS, LANES)) < HALF
    decay = decay_ref[...]
    ahead, behind = group_powers(decay, inner, groups, SUBS // groups)
    fields = ([], [])
    for part in range(2):
        for a in range(radix):
            d, incoming = decay[a], entering_ref[part * radix + a]
            turned = turn(incoming, HALF)
            from_low = scale_ref[a] * ahead[a] * jnp.where(low, incoming, turned)
            from_high = scale_ref[a] * behind[a] * jnp.where(low, turned, incoming)
            fields[part].append(
                jnp.stack([power(d, z + 1) * from_low + power(d, inner - z) * from_high for z in range(inner)])
            )
    return lane_product(*fields, lane_ref)


def own_planes(groups, re, im, twiddle_ref):
    rows = len(re) // groups
    me = lax.axis_index("gy")
    planes = to_planes(re, im, twiddle_ref)
    return [[for_targets([field[t * rows + a] for t in range(groups)], me)[0] for a in range(rows)] for field in planes]


def own_kernel(groups, entering_ref, decay_ref, scale_ref, lane_ref, twiddle_ref, local_ref, out_ref):
    rows, inner = local_ref.shape[0] // 2, local_ref.shape[1]
    field = own_planes(groups, *response(groups, inner, entering_ref, decay_ref, scale_ref, lane_ref), twiddle_ref)
    for part in range(2):
        for a in range(rows):
            out_ref[part * rows + a] = field[part][a] + local_ref[part * rows + a]


def finish_kernel(groups, *refs):
    entering, parts = refs[:groups], refs[groups : 2 * groups]
    roots = refs[2 * groups : 4 * groups]
    lane_ref, twiddle_ref, weight_ref, previous_ref, rz_prev_ref = refs[4 * groups : 4 * groups + 5]
    out_ref, direction_ref, total_ref, out_buffer, direction_buffer, total_buffer, sems, total_sem = refs[4 * groups + 5 :]
    cells, _, waves, planes = out_buffer.shape
    kept, inner, rows = waves // groups, cells // groups, planes // LANES
    me = lax.axis_index("gy")
    block = sub_ids((SUBS, LANES)) // kept
    energies = by_source([ref[ref.shape[0] - 1] for ref in entering], me)
    total = jnp.sum(sum(energies[1:], energies[0]), axis=(0, 1), keepdims=True)
    total_buffer[...] = total
    copies = [pltpu.make_async_copy(total_buffer, total_ref, total_sem)]
    copies[0].start()
    ratio = total / rz_prev_ref[0]
    responses = [
        response(groups, inner, entering[s], roots[2 * s], roots[2 * s + 1], lane_ref) for s in range(1, groups)
    ]
    for zp in range(inner):
        held = [[[parts[0][part * rows + a, zp] for a in range(rows)] for part in range(2)]]
        for s, (re, im) in enumerate(responses, 1):
            field = own_planes(groups, [v[zp] for v in re], [v[zp] for v in im], twiddle_ref)
            held.append([[field[part][a] + parts[s][part * rows + a, zp] for a in range(rows)] for part in range(2)])
        for part in range(2):
            for a in range(rows):
                lanes = slice(a * LANES, (a + 1) * LANES)
                sources = by_source([fields[part][a] for fields in held], me)
                for zg in range(groups):
                    z = zg * inner + zp
                    value = turn(sources[0], -zg * kept)
                    for t in range(1, groups):
                        value = jnp.where(block == t, turn(sources[t], (t - zg) * kept), value)
                    value = value * weight_ref[z : z + 1, lanes]
                    out_buffer[z, part, :, lanes] = value
                    direction_buffer[z, part, :, lanes] = value + ratio * previous_ref[z, part, :, lanes]
        for zg in range(groups):
            z = zg * inner + zp
            for i, (source, target) in enumerate(((out_buffer, out_ref), (direction_buffer, direction_ref))):
                copies.append(pltpu.make_async_copy(source.at[z], target.at[z], sems.at[i, z]))
                copies[-1].start()
    for copy in copies:
        copy.wait()


def float_array(*shape):
    return jax.ShapeDtypeStruct(shape, jnp.float32)


def held_array(*shape):
    return pltpu.VMEM(shape, jnp.float32)


def inside(value):
    return pltpu.with_memory_space_constraint(jnp.asarray(value), pltpu.VMEM)


def on_device(residual, direction_prev, phase_labels, phase_diffusivity, x_eigen, rz_prev):
    cells, parts, waves, planes = residual.shape
    groups, slabs = lax.axis_size("gy"), lax.axis_size("gz")
    levels = slabs.bit_length() - 1
    inner, rows = cells // groups, planes // LANES
    radix = rows * groups
    distances = [[(i, (i + s) % groups) for i in range(groups)] for s in range(1, groups)]

    weight, *pieces = pl.pallas_call(
        functools.partial(pack_kernel, groups),
        out_shape=[held_array(cells, planes)] + [held_array(parts, rows, inner, SUBS, LANES)] * groups,
        in_specs=[ANY] * 3,
        out_specs=[VMEM] * (groups + 1),
        scratch_shapes=[
            pltpu.VMEM(residual.shape, jnp.float32),
            pltpu.VMEM(phase_labels.shape, jnp.int32),
            pltpu.SMEM(phase_diffusivity.shape, jnp.float32),
            pltpu.SemaphoreType.DMA((cells,)),
            pltpu.SemaphoreType.DMA,
            pltpu.SemaphoreType.DMA,
        ],
        name="pack",
    )(residual, phase_labels, phase_diffusivity)
    held = [pieces[0]] + [lax.ppermute(x, "gy", d) for x, d in zip(pieces[1:], distances)]
    roots = pl.pallas_call(
        functools.partial(roots_kernel, groups),
        out_shape=[held_array(radix, SUBS, LANES)] * (2 * groups),
        in_specs=[VMEM, SMEM],
        out_specs=[VMEM] * (2 * groups),
        name="roots",
    )(inside(y_eigen(radix)), x_eigen)
    decay, scale = roots[:2]

    message, local = pl.pallas_call(
        functools.partial(forward_kernel, groups),
        out_shape=[
            held_array(parts * radix + 1, SUBS, LANES),
            held_array(parts, radix, inner, SUBS, LANES),
        ],
        in_specs=[VMEM] * (groups + 4),
        out_specs=[VMEM] * 2,
        name="forward",
    )(*map(inside, (*held, lane_transform(-1.0), twiddles(radix), decay, scale)))

    def swapped(value, bits):
        return lax.ppermute(value, "gz", [(i, i ^ bits) for i in range(slabs)])

    first, received, level = message, [], 0
    edge_shape = held_array(radix + 1, SUBS, LANES)
    while level < levels - 1:
        bit, cross = 1 << level, min(level, 1)
        near = swapped(message, bit | cross)
        received.append(near)
        if level == 0 or level == levels - 2:
            last = [edge_shape] if level == levels - 2 else []
            message, *edge = pl.pallas_call(
                functools.partial(join_kernel, level, cells, groups),
                out_shape=[held_array(*message.shape)] + last,
                in_specs=[VMEM] * 4,
                out_specs=[VMEM] * (1 + len(last)),
                name=f"join{level}",
            )(*map(inside, (message, near, decay, scale)))
            level += 1
        else:
            last = [edge_shape] if level == levels - 3 else []
            message, pair, *edge = pl.pallas_call(
                functools.partial(join_two_kernel, level, cells, groups),
                out_shape=[held_array(*message.shape)] * 2 + last,
                in_specs=[VMEM] * 6,
                out_specs=[VMEM] * (2 + len(last)),
                name=f"join{level}",
            )(*map(inside, (message, near, swapped(message, 2 * bit | 1), swapped(message, 3 * bit | 1), decay, scale)))
            received.append(pair)
            level += 2
    tables = (lane_transform(1.0), twiddles(radix))
    piece = held_array(parts * rows, inner, SUBS, LANES)
    pieces = pl.pallas_call(
        functools.partial(local_kernel, groups),
        out_shape=[piece] * groups,
        in_specs=[VMEM] * 5,
        out_specs=[VMEM] * groups,
        name="local",
    )(*map(inside, (local, decay, scale, *tables)))
    held = [lax.ppermute(x, "gy", d) for x, d in zip(pieces[1:], distances)]

    other = swapped(edge[0], 1 << level | 1)
    near_side = pl.pallas_call(
        functools.partial(near_side_kernel, slabs, cells),
        out_shape=[held_array(*message.shape)] * 2 + [held_array(4 * radix, SUBS, LANES)],
        in_specs=[VMEM] * (levels + 4),
        out_specs=[VMEM] * 3,
        name="near_side",
    )(*map(inside, (message, first, *received, edge[0], decay, scale)))
    entering, mate = pl.pallas_call(
        functools.partial(entering_kernel, groups, slabs),
        out_shape=[held_array(*message.shape)] * 2,
        in_specs=[VMEM] * 5,
        out_specs=[VMEM] * 2,
        name="entering",
    )(*map(inside, (edge[0], other, *near_side)))
    crossed = [[(i * slabs + z, j * slabs + (z ^ 1)) for i, j in d for z in range(slabs)] for d in distances]
    entered = [entering] + [lax.ppermute(mate, ("gy", "gz"), d) for d in crossed]
    own = pl.pallas_call(
        functools.partial(own_kernel, groups),
        out_shape=piece,
        in_specs=[VMEM] * 6,
        out_specs=VMEM,
        name="own",
    )(*map(inside, (entering, decay, scale, *tables, pieces[0])))

    preconditioned, direction, total = pl.pallas_call(
        functools.partial(finish_kernel, groups),
        out_shape=[float_array(*residual.shape), float_array(*residual.shape), float_array(1, 1)],
        in_specs=[VMEM] * (4 * groups + 4) + [SMEM],
        out_specs=[ANY] * 3,
        scratch_shapes=[
            pltpu.VMEM(residual.shape, jnp.float32),
            pltpu.VMEM(residual.shape, jnp.float32),
            pltpu.VMEM((1, 1), jnp.float32),
            pltpu.SemaphoreType.DMA((2, cells)),
            pltpu.SemaphoreType.DMA,
        ],
        name="finish",
    )(*map(inside, (*entered, own, *held, *roots, *tables, weight, direction_prev)), rz_prev)
    return preconditioned, direction, jnp.reshape(total, (1,))


def solution(mesh):
    placed = (P("gz", None, None, "gy"), P("gz", None, None, "gy"), P("gz", "gy"), P(), P(), P())
    return jax.shard_map(
        on_device,
        mesh=mesh,
        in_specs=placed,
        out_specs=(P("gz", None, None, "gy"), P("gz", None, None, "gy"), P()),
        check_vma=False,
    )
```
